512 devices in a mesh: dp: 64 (over x_hi, z, core), mp: 8 (over y, x_lo).
Axes of the slice: x: 4 (x_hi: 2, x_lo: 2; x = x_hi * 2 + x_lo), y: 4, z: 16, core: 2. Of those that a mesh axis runs over, the one named last changes fastest.
Arguments:
- patches: bfloat16 [32768, 1152], P('dp', 'mp'), may hold values from -6 to 6
- patch_shard: int32 [32768, 1], P('dp'), may hold values from 0 to 63; in each aligned block of 512 rows (0 to 511, 512 to 1023, ...) at most 10 rows name the same one
- patch_image: int32 [64, 512], P('dp'), may hold values from 0 to 15, as said below
- caption_of: int32 [1024], P('dp'), may hold values from 0 to 1023, as said below
- text_embed: bfloat16 [1024, 1152], P('dp', 'mp'), may hold values from -8 to 8
- ln_gain: bfloat16 [1152], P('mp'), may hold values from 0.099609375 to 1.8984375
- fc1_weight: bfloat16 [1152, 4304], P(None, 'mp'), may hold values from -0.1875 to 0.1875
- fc1_bias: bfloat16 [4304], P('mp'), may hold values from -3 to 3
- fc2_weight: bfloat16 [4304, 1152], P('mp'), may hold values from -0.09375 to 0.09375
- fc2_bias: bfloat16 [1152], P('mp'), may hold values from -3 to 3
Outputs:
- packed: bfloat16 [64, 640, 1152], P('dp', None, 'mp')
- image_grad: float32 [1024, 1152], P('dp', 'mp')
- text_grad: float32 [1024, 1152], P('dp', 'mp')
The draws below stay inside these ranges and needn't reach their ends.
Inputs may be any that keep to these rules, and one draw needn't show every extreme that they name: `patch_shard`: within the 512 rows of one dp shard at most 10 rows name the same encoder shard, and in some dp shard one encoder shard is named by exactly 10 rows. `patch_image`: in each dp shard the ids never fall and every image 0 to 15 has one or more patches; no image has more than 64 patches and some image has exactly 64. `caption_of`: each text is paired with exactly one image.
All inputs are finite; a program needn't handle non-finite values.
Results may differ from the reference program's by a relative error of at most 0.017.
Values may be sent and summed in bfloat16 or wider, within the bound.
A program may use at most 128 MiB of HBM per device.

```python
import math
import jax
import jax.numpy as jnp
import numpy as np
from jax import lax

D = 1152
FF = 4304
PATCH_DEV = 512
MAXP = 64
IMG_DEV = 16
SHARDS = 64
CAP = 10
SLOTS = 640
PATCHES = 32768
IMAGES = 1024


def segment_ids(key):
    key = jax.random.fold_in(key, 101)
    half = MAXP // 2
    first, second = jax.random.split(key)
    lifts = jax.random.randint(first, (SHARDS, IMG_DEV), 1, half, dtype=jnp.int32)
    chosen = jax.random.randint(second, (SHARDS, 1), 0, IMG_DEV, dtype=jnp.int32)
    columns = jnp.arange(IMG_DEV, dtype=jnp.int32)[None, :]
    lifts = jnp.where(columns == chosen, half, jnp.where(columns == (chosen + 1) % IMG_DEV, 0, lifts))
    lengths = half + lifts - jnp.roll(lifts, -1, axis=1)
    ends = jnp.cumsum(lengths, axis=1)
    positions = jnp.arange(PATCH_DEV, dtype=jnp.int32)
    return jnp.sum((ends[:, :, None] <= positions[None, None, :]).astype(jnp.int32), axis=1).astype(jnp.int32)


def image_directions(key, spread):
    key = jax.random.fold_in(key, 102)
    first, second = jax.random.split(key)
    scales = jnp.exp(jax.random.uniform(first, (IMAGES, 1), jnp.float32, -spread, spread))
    return jax.random.normal(second, (IMAGES, D), jnp.float32) * scales


def pairing(key):
    return jax.random.permutation(jax.random.fold_in(key, 103), IMAGES).astype(jnp.int32)


def draw_patch_image(key, part):
    return segment_ids(key)


def draw_caption_of(key, part):
    return pairing(key)


def draw_patches(key, part):
    owners = segment_ids(key) + IMG_DEV * jnp.arange(SHARDS, dtype=jnp.int32)[:, None]
    directions = image_directions(key, 0.0)
    key = jax.random.fold_in(key, 1)
    noise = jax.random.normal(key, (PATCHES, D), jnp.float32)
    rows = directions[owners.reshape(-1)] + noise
    return jnp.clip(rows, -6.0, 6.0).astype(jnp.bfloat16)


def draw_text_embed(key, part):
    partner = pairing(key)
    directions = image_directions(key, 0.0)
    key = jax.random.fold_in(key, 2)
    first, second = jax.random.split(key)
    noise = jax.random.normal(second, (IMAGES, D), jnp.float32)
    aligned = jnp.zeros((IMAGES, D), jnp.float32).at[partner].set(directions)
    strength = jax.random.uniform(first, (IMAGES, 1), jnp.float32, 0.1, 1.2)
    return jnp.clip(strength * aligned + noise, -8.0, 8.0).astype(jnp.bfloat16)


def block_scale(key, extent, cuts, least, largest):
    factor_of = 1.0
    for axis_at, shards_of in cuts:
        draws = jax.random.uniform(jax.random.fold_in(jax.random.fold_in(key, 6), axis_at), (shards_of,), jnp.float32, least / len(cuts), largest / len(cuts))
        factor_of = factor_of * jnp.repeat(jnp.exp(draws), extent[axis_at] // shards_of).reshape((-1,) + (1,) * (len(extent) - 1 - axis_at))
    return factor_of


def deal_out(rng, own, number, rows, count, top, reach, slope):
    sequence = jax.random.permutation(rng, count)
    crowded, usual = shares(count, rows * top, reach, slope, True), shares(count, rows * top, reach, slope, False)
    places = jnp.arange(count)

    def named(sizes, turn):
        used = int((sizes > 0).sum())
        fixed = max(1, used // 4)
        shifted = fixed + (places - fixed + turn * (used - fixed)) % max(1, count - fixed)
        return jnp.zeros((count,), jnp.int32).at[sequence[jnp.where(places < fixed, places, shifted)]].set(jnp.asarray(sizes, jnp.int32))

    sizes = jnp.where(number % 4 == 0, named(crowded, number // 4), named(usual, number - number // 4 - 1))
    mixed = jax.random.permutation(jax.random.fold_in(own, 3), count)
    donor, sink = mixed[0:count // 2 * 2:2], mixed[1:count // 2 * 2:2]
    room = jnp.minimum(sizes[donor] - 1, reach - sizes[sink]) // 2
    room = jnp.where((donor == sequence[0]) | (sink == sequence[0]) | (sizes[sink] == 0), 0, jnp.maximum(room, 0))
    shifted = jax.random.randint(jax.random.fold_in(own, 4), (count // 2,), 0, 1 << 20) % (room + 1)
    sizes = sizes.at[donor].add(-shifted).at[sink].add(shifted)
    labels = jnp.searchsorted(jnp.cumsum(sizes), jnp.arange(rows * top), side="right").astype(jnp.int32)
    table = labels.reshape(top, rows).T
    table = table[jax.random.permutation(jax.random.fold_in(own, 1), rows)]
    turn = jax.random.randint(jax.random.fold_in(own, 2), (rows, 1), 0, top)
    return jnp.take_along_axis(table, (jnp.arange(top)[None, :] + turn) % top, axis=1)


def shares(amount, total, most, skew, full):
    weights = [(1 << 20) // math.isqrt(rank ** skew) + 1 for rank in range(1, amount + 1)]
    largest = most if full else min(most, max(-(-total // amount), total * weights[0] // sum(weights)))
    least = 1 if total - largest >= amount - 1 else 0
    holding, surplus = [largest] + [least] * (amount - 1), total - largest - least * (amount - 1)
    while surplus > 0:
        candidates = [i for i in range(1, amount) if holding[i] < largest] or [i for i in range(1, amount) if holding[i] < most]
        pool, budget = sum([weights[i] for i in candidates]), surplus
        for i in candidates:
            extra = min(most - holding[i], max(1, budget * weights[i] // pool), surplus)
            holding[i] = holding[i] + extra
            surplus = surplus - extra
    return np.array(holding)


def bell_draw(own_key, extent, scale, limit, shards=(), kind=jnp.bfloat16):
    loudness = block_scale(own_key, extent, shards, -0.22, 0.18) if shards else 1.0
    array = jax.random.normal(own_key, extent, jnp.float32) * scale * loudness
    return jnp.minimum(jnp.maximum(array, -limit), limit).astype(kind)


def setup_inputs(seed: int = 0) -> dict:
    arg_keys = jax.random.split(jax.random.key(seed), 11)
    patches = draw_patches(jax.random.fold_in(arg_keys[10], 71), 0)
    patch_shard_keys = jax.random.split(jax.random.fold_in(arg_keys[1], 1), PATCHES // PATCH_DEV)
    patch_shard_turns = jax.random.permutation(jax.random.fold_in(arg_keys[1], 3), PATCHES // PATCH_DEV)
    patch_shard = jax.vmap(lambda own, number: deal_out(jax.random.fold_in(arg_keys[1], 2), own, number, PATCH_DEV, SHARDS, 1, CAP, 2))(patch_shard_keys, patch_shard_turns).reshape((PATCHES, 1))
    patch_image = draw_patch_image(jax.random.fold_in(arg_keys[10], 71), 0)
    caption_of = draw_caption_of(jax.random.fold_in(arg_keys[10], 71), 0)
    text_embed = draw_text_embed(jax.random.fold_in(arg_keys[10], 71), 0)
    ln_gain = jnp.clip(1.0 + 0.18 * jax.random.normal(arg_keys[5], (D,), jnp.float32), 0.099609375, 1.8984375).astype(jnp.bfloat16)
    fc1_weight = bell_draw(arg_keys[6], (D, FF), D ** -0.5, 0.1875, ((1, 8),))
    fc1_bias = bell_draw(arg_keys[7], (FF,), 0.5, 3.0, ((0, 8),))
    fc2_weight = bell_draw(arg_keys[8], (FF, D), FF ** -0.5, 0.09375, ((0, 8),))
    fc2_bias = bell_draw(arg_keys[9], (D,), 0.5, 3.0, ((0, 8),))
    return {"patches": patches, "patch_shard": patch_shard, "patch_image": patch_image, "caption_of": caption_of, "text_embed": text_embed, "ln_gain": ln_gain, "fc1_weight": fc1_weight, "fc1_bias": fc1_bias, "fc2_weight": fc2_weight, "fc2_bias": fc2_bias}


LOGIT_SCALE = 10.0
LOGIT_BIAS = -2.0

def layer_norm(row_block, row_gain):
    widened = row_block.astype(jnp.float32)
    centre = widened - lax.optimization_barrier(jnp.mean(widened, axis=-1, keepdims=True))
    spread = lax.optimization_barrier(jnp.mean(centre * centre, axis=-1, keepdims=True))
    return (centre * lax.rsqrt(spread + 1e-06) * row_gain.astype(jnp.float32)).astype(jnp.bfloat16)

def encode(row_block, ln_gain, fc1_weight, fc1_bias, fc2_weight, fc2_bias):
    normed = layer_norm(row_block, ln_gain)
    hidden = jax.nn.gelu(jnp.dot(normed, fc1_weight, preferred_element_type=jnp.float32) + fc1_bias.astype(jnp.float32), approximate=True).astype(jnp.bfloat16)
    mixed_sum = jnp.dot(hidden, fc2_weight, preferred_element_type=jnp.float32)
    return (row_block.astype(jnp.float32) + mixed_sum + fc2_bias.astype(jnp.float32)).astype(jnp.bfloat16)

def unit_rows(widened):
    return (widened * lax.rsqrt(lax.optimization_barrier(jnp.sum(widened * widened, axis=-1, keepdims=True)) + 1e-06)).astype(jnp.bfloat16)

def slot_ranks(targets):
    shard_ids = jnp.arange(SHARDS, dtype=jnp.int32)
    member = (targets[:, None] == shard_ids[None, :]).astype(jnp.int32)
    before = jnp.cumsum(member, axis=0) - member
    return lax.optimization_barrier(jnp.sum(before * member, axis=1)).astype(jnp.int32)

def reference(patches, patch_shard, patch_image, caption_of, text_embed, ln_gain, fc1_weight, fc1_bias, fc2_weight, fc2_bias):
    params = (ln_gain, fc1_weight, fc1_bias, fc2_weight, fc2_bias)
    shard_rows = patches.reshape(SHARDS, PATCH_DEV, D)

    def one_shard(pieces):
        return encode(pieces, *params)
    encoded = lax.map(one_shard, shard_rows)
    empty_row = encode(jnp.zeros((1, D), jnp.bfloat16), *params)[0]
    targets = patch_shard.reshape(SHARDS, PATCH_DEV).astype(jnp.int32)
    slot_rank = jax.vmap(slot_ranks)(targets)
    source = jnp.arange(SHARDS, dtype=jnp.int32)[:, None]
    slot_index = (targets * SLOTS + source * CAP + slot_rank).reshape(-1)
    packed = jnp.broadcast_to(empty_row, (SHARDS * SLOTS, D)).at[slot_index].set(encoded.reshape(-1, D)).reshape(SHARDS, SLOTS, D)
    image_ids = jnp.arange(IMG_DEV, dtype=jnp.int32)

    def pool_shard(items):
        pieces, owners = items
        member = owners[None, :] == image_ids[:, None]
        row_sums = jnp.dot(member.astype(jnp.bfloat16), pieces, preferred_element_type=jnp.float32)
        counts = lax.optimization_barrier(jnp.sum(member.astype(jnp.float32), axis=1, keepdims=True))
        return row_sums / counts
    pooled = lax.map(pool_shard, (encoded, patch_image)).reshape(IMAGES, D)
    image_unit = unit_rows(pooled)
    text_unit = unit_rows(text_embed.astype(jnp.float32))
    logits = LOGIT_SCALE * jnp.dot(image_unit, text_unit.T, preferred_element_type=jnp.float32) + LOGIT_BIAS
    paired = (caption_of[:, None] == jnp.arange(IMAGES, dtype=jnp.int32)[None, :]).astype(jnp.float32)
    pair_coef = (jax.nn.sigmoid(logits) - paired).astype(jnp.bfloat16)
    image_grad = LOGIT_SCALE * jnp.dot(pair_coef, text_unit, preferred_element_type=jnp.float32)
    text_grad = LOGIT_SCALE * jnp.dot(pair_coef.T, image_unit, preferred_element_type=jnp.float32)
    return (packed, image_grad, text_grad)
```

```python
import functools

import jax
import jax.numpy as jnp
from jax import lax
from jax.experimental import pallas as pl
from jax.experimental.pallas import tpu as pltpu
from jax.sharding import PartitionSpec as P

LOGIT_SCALE = 10.0
LOGIT_BIAS = -2.0
F32 = jnp.float32
BF16 = jnp.bfloat16
I32 = jnp.int32
MESH = pl.DeviceIdType.MESH

DP, MP = 64, 8
GROUP = 8
ROWS, PART, FULL = 512, 144, 1152
FF, FFP = 538, 640
IMG, CAP = 16, 10
SLOTS = DP * CAP
CH = 2
L = ROWS // CH
SIDE = GROUP * IMG
XROWS = PART + 16


def nn(a, b):
    return jnp.dot(a, b, preferred_element_type=F32)


def nt(a, b):
    return lax.dot_general(a, b, (((1,), (1,)), ((), ())), preferred_element_type=F32)


def tn(a, b):
    return lax.dot_general(a, b, (((0,), (0,)), ((), ())), preferred_element_type=F32)


def iota(shape, axis):
    return lax.broadcasted_iota(I32, shape, axis)


def gelu(h):
    return 0.5 * h * (1.0 + jnp.tanh(0.7978845608028654 * (h + 0.044715 * (h * h * h))))


def wide(column_block):
    return jnp.concatenate([column_block] * (L // 128), axis=1)


def kernel(
    x_hbm, text_hbm, target_hbm, owner_hbm, caption_hbm, gain_hbm, b1_hbm, b2_hbm, w1_hbm, w2_hbm,
    packed_ref, image_grad_ref, text_grad_ref,
    x_ref, text_ref, target_ref, owner_ref, caption_ref, gain_ref, b1_ref, b2_ref, w1, w2,
    small_ref, w2t, xall, gain_b, b1_b, b2_b, hid, part_out, part_in,
    pool_out, pool_in, tbuf, ibuf, pair_out, pair_in, coef_in, grad_out, grad_in,
    pick, empty_pick, sel, rows_out, slot_out, slot_in,
    load_sem, x_send, x_recv, t_send, t_recv, p_send, p_recv,
    pool_send, pool_recv, i_send, i_recv, pair_send, pair_recv, coef_send, coef_recv,
    grad_send, grad_recv, slot_send, slot_recv,
):
    s = lax.axis_index("dp")
    m = lax.axis_index("mp")
    a = s // GROUP
    b = lax.rem(s, GROUP)
    neighbour = lax.rem(s + 1, DP)

    ring, side = m // 2, lax.rem(m, 2)
    ahead = lax.rem(ring + 1, 4) * 2 + side
    behind = lax.rem(ring + 3, 4) * 2 + side
    far = lax.rem(ring + 2, 4) * 2 + side
    across = ring * 2 + 1 - side
    ahead_across = lax.rem(ring + 1, 4) * 2 + 1 - side
    behind_across = lax.rem(ring + 3, 4) * 2 + 1 - side
    far_across = lax.rem(ring + 2, 4) * 2 + 1 - side

    loads = [
        pltpu.make_async_copy(src, dst, load_sem.at[n])
        for n, (src, dst) in enumerate(
            (
                (x_hbm, x_ref), (gain_hbm, gain_ref), (text_hbm, text_ref), (caption_hbm, caption_ref),
                (target_hbm, target_ref), (owner_hbm, owner_ref), (b1_hbm, b1_ref), (b2_hbm, b2_ref),
                (w1_hbm, w1), (w2_hbm, w2),
            )
        )
    ]
    for load in loads:
        load.start()

    barrier = pltpu.get_barrier_semaphore()

    def greet_mp(i, c):
        pl.semaphore_signal(barrier, inc=1, device_id=(s, lax.rem(m + i, MP)), device_id_type=MESH)
        return c

    def greet_dp(i, c):
        pl.semaphore_signal(barrier, inc=1, device_id=(lax.rem(s + i, DP), m), device_id_type=MESH)
        return c

    lax.fori_loop(1, MP, greet_mp, 0)
    lax.fori_loop(1, DP, greet_dp, 0)

    def to_member(member, src, dst, send, recv):
        return pltpu.make_async_remote_copy(
            src_ref=src, dst_ref=dst, send_sem=send, recv_sem=recv,
            device_id=(s, member), device_id_type=MESH,
        )

    def to_mp(i, src, dst, send, recv):
        return to_member(lax.rem(m + i, MP), src, dst, send, recv)

    def to_dp(peer, src, dst, send, recv):
        return pltpu.make_async_remote_copy(
            src_ref=src, dst_ref=dst, send_sem=send, recv_sem=recv,
            device_id=(peer, m), device_id_type=MESH,
        )

    small_ref[...] = jnp.zeros_like(small_ref)
    loads[0].wait()
    loads[1].wait()
    small_ref[1:2, 0:PART] = gain_ref[...].astype(F32).reshape(1, PART)
    for c in range(CH):
        xall[c, m, 0:PART] = x_ref[:, c * L : (c + 1) * L]
    xall[0, m, PART:XROWS] = jnp.broadcast_to(small_ref[1:2, 0:L], (XROWS - PART, L)).astype(BF16)

    pl.semaphore_wait(barrier, DP + MP - 2)

    def block(c, member):
        return xall.at[c, member, pl.ds(0, XROWS if c == 0 else PART)]

    def hand_on(c, owner, member, kind):
        to_member(member, block(c, owner), block(c, owner), x_send.at[c], x_recv.at[c, kind]).start()

    def expect(c, kind):
        to_member(across, block(c, m), block(c, m), x_send.at[c], x_recv.at[c, kind]).wait_recv()

    for c in range(CH):
        hand_on(c, m, across, 2)
        hand_on(c, m, ahead, 0)
        hand_on(c, m, behind, 1)

    for load in loads[2:8]:
        load.wait()
    small_ref[0:1, 0:FF] = b1_ref[...].astype(F32).reshape(1, FF)
    small_ref[2:3, 0:PART] = b2_ref[...].astype(F32).reshape(1, PART)
    diagonal = iota((IMG, IMG), 0) == iota((IMG, IMG), 1)
    caption_row = caption_ref[...]
    caption_high = jnp.right_shift(caption_row, 5)
    caption_low = jnp.bitwise_and(caption_row, 31)

    def as_column(row):
        return jnp.sum(jnp.where(diagonal, row.astype(F32), 0.0), axis=1, keepdims=True)

    text_own_f = jnp.concatenate([text_ref[...].astype(F32), jnp.zeros((IMG, 256 - PART), F32)], axis=1)
    tbuf[a] = text_own_f.astype(BF16)

    def send_text(i, k):
        peer = lax.rem(a + i, GROUP) * GROUP + b
        to_dp(peer, tbuf.at[a], tbuf.at[a], t_send.at[0], t_recv.at[0]).start()
        return k


    for c in range(CH):
        expect(c, 2)
        hand_on(c, across, ahead, 3)
        hand_on(c, across, behind, 4)
        if c == 0:
            expect(c, 0)
            hand_on(c, behind, ahead, 5)
        else:
            expect(c, 1)
            hand_on(c, ahead, behind, 5)

    lax.fori_loop(1, GROUP, send_text, 0)

    targets = target_ref[...]
    named = iota((DP, ROWS), 0) == targets
    named_b = jnp.where(named, 1.0, 0.0).astype(BF16)
    earlier = jnp.where(iota((ROWS, ROWS), 0) < iota((ROWS, ROWS), 1), 1.0, 0.0).astype(BF16)
    before = nn(named_b, earlier)
    rank = jnp.sum(jnp.where(named, before, 0.0), axis=0, keepdims=True).astype(I32)
    code = targets * 16 + rank

    first_row = jnp.where(iota((16, 128), 0) == 0, 1.0, 0.0).astype(BF16)
    b1_row = jnp.broadcast_to(small_ref[0:1, :], (16, FFP))
    b1_b[...] = tn(b1_row.astype(BF16), first_row)
    b2_row = jnp.broadcast_to(small_ref[2:3, 0:256], (16, 256)).astype(BF16)
    b2_b[...] = tn(b2_row, first_row)[0:PART]
    hid[...] = jnp.zeros_like(hid)
    for c in range(CH):
        expect(c, 5)
        hand_on(c, far, across, 6)

    def build_pick(b, k):
        row = iota((128, 1), 0) + b * 128
        slot = jnp.bitwise_and(row, 15)
        base = row - slot
        is_head = slot < CAP
        is_tail = jnp.logical_and(slot >= CAP, slot < CAP + CAP // 2)
        even = base + 2 * (slot - CAP)
        lines = pl.ds(pl.multiple_of(b * 128, 128), 128)
        lane = iota((128, 128), 1)
        main = jnp.where(jnp.where(is_head, row, jnp.where(is_tail, even, -1)) == code, 1.0, 0.0)
        odd = jnp.where(jnp.where(is_tail, even + 1, -1) == code, 1.0, 0.0)
        pick[0, lines, :] = main.astype(BF16)
        pick[1, lines, :] = odd.astype(BF16)
        lack = 1.0 - jnp.sum(main, axis=1, keepdims=True)
        lack_odd = 1.0 - jnp.sum(odd, axis=1, keepdims=True)
        lacks = jnp.where(
            lane == 0,
            jnp.where(is_head, lack, 0.0),
            jnp.where(lane == 1, jnp.where(is_tail, lack, 0.0), jnp.where(lane == 2, jnp.where(is_tail, lack_odd, 0.0), 0.0)),
        )
        empty_pick[lines, :] = lacks.astype(BF16)
        column = iota((128, SLOTS), 1)
        first = jnp.right_shift(row, 4) * CAP
        even_at = first + 2 * (slot - CAP)
        main_at = jnp.where(is_head, first + slot, jnp.where(is_tail, even_at, -1))
        odd_at = jnp.where(is_tail, even_at + 1, -1)
        sel[0, lines, :] = jnp.where(main_at == column, 1.0, 0.0).astype(BF16)
        sel[1, lines, :] = jnp.where(odd_at == column, 1.0, 0.0).astype(BF16)
        return k

    lax.fori_loop(0, DP * 16 // 128, build_pick, 0)

    loads[8].wait()
    loads[9].wait()
    w2t[:, 0:512] = jnp.transpose(w2[0:512, :])
    tail_rows = jnp.concatenate([w2[512:FF, :].astype(F32), jnp.zeros((FFP - FF, FULL), F32)], axis=0)
    w2t[:, 512:FFP] = jnp.transpose(tail_rows).astype(BF16)

    def share(c, member):
        lines = pl.ds(pl.multiple_of(member * PART, 16), PART)
        return nn(w2t[lines, :], hid[:, c * L : (c + 1) * L])

    def pass_on(c, value, member, kind):
        part_out[c, kind] = value.astype(BF16)
        to_member(member, part_out.at[c, kind], part_in.at[c, kind], p_send.at[c], p_recv.at[c, kind]).start()

    def arrived_sum(c, kind):
        to_member(across, part_in.at[c, kind], part_in.at[c, kind], p_send.at[c], p_recv.at[c, kind]).wait_recv()
        return part_in[c, kind].astype(F32)

    def first_sums(c):
        pass_on(c, share(c, far_across), across, 0)
        pass_on(c, share(c, ahead_across), ahead, 1)
        pass_on(c, share(c, behind_across), behind, 2)
        if c == 0:
            pass_on(c, share(c, behind), behind, 5)
        else:
            pass_on(c, share(c, ahead), ahead, 4)

    def second_sums(c):
        pass_on(c, share(c, far) + arrived_sum(c, 0), ahead if c == 0 else behind, 3)
        pass_on(c, share(c, across) + arrived_sum(c, 1) + arrived_sum(c, 2), across, 6)

    def third_sums(c):
        if c == 0:
            pass_on(c, share(c, ahead) + arrived_sum(c, 3), ahead, 4)
        else:
            pass_on(c, share(c, behind) + arrived_sum(c, 3), behind, 5)

    for c in range(CH):
        for kind in (1 if c == 0 else 0, 3, 4, 6):
            expect(c, kind)
        if c == 0:
            for k in range(MP):
                gain_b[k * PART : (k + 1) * PART, :] = tn(xall[0, k, PART:XROWS], first_row)[0:PART]

        rows = xall[c, :, 0:PART].reshape(FULL, L).astype(F32)
        centre = rows - jnp.sum(rows, axis=0, keepdims=True) * (1.0 / FULL)
        spread = jnp.sum(centre * centre, axis=0, keepdims=True) * (1.0 / FULL)
        normed = (centre * lax.rsqrt(spread + 1e-06) * wide(gain_b[...])).astype(BF16)
        pre = nn(w1[...], normed) + wide(b1_b[0:FF, :])
        hid[0:FF, c * L : (c + 1) * L] = gelu(pre).astype(BF16)

        if c < CH - 1:
            first_sums(c)

    first_sums(CH - 1)
    member_f = jnp.where(iota((IMG, ROWS), 0) == owner_ref[...], 1.0, 0.0)
    member = member_f.astype(BF16)
    sums = nt(member, hid[...])
    high = sums.astype(BF16)
    low = (sums - high.astype(F32)).astype(BF16)
    lone = gelu(b1_row).astype(BF16)
    mixed = jnp.concatenate([high, low, lone], axis=0)

    def pool_block(i, k):
        there = lax.rem(m + i, MP)
        lines = pl.ds(pl.multiple_of(there * PART, 16), PART)
        got = nt(mixed, w2t[lines, :])
        pool_out[there, 0:16, 0:PART] = got[0:16] + got[16:32]
        pool_out[there, 16:24, 0:PART] = got[32:40]
        return k

    pool_out[...] = jnp.zeros_like(pool_out)
    lax.fori_loop(0, MP, pool_block, 0)

    def send_pool(i, k):
        there = lax.rem(m + i, MP)
        to_mp(i, pool_out.at[there], pool_in.at[m], pool_send.at[0], pool_recv.at[0]).start()
        return k

    lax.fori_loop(1, MP, send_pool, 0)
    pool_in[m] = pool_out[m]

    for c in range(CH):
        second_sums(c)

    some = pool_in.at[pl.ds(0, MP - 1)]
    to_mp(1, some, some, pool_send.at[0], pool_recv.at[0]).wait_recv()
    pooled = pool_in[0]
    for k in range(1, MP):
        pooled = pooled + pool_in[k]
    b2_wide = jnp.where(iota((1, 256), 1) < PART, small_ref[2:3, 0:256], 0.0)
    counts = jnp.sum(member_f, axis=1, keepdims=True)
    own_sum = nt(member, x_ref[...])
    own_sum = jnp.concatenate([own_sum, jnp.zeros((IMG, 256 - PART), F32)], axis=1)
    image_own = (pooled[0:16] + own_sum) / counts + b2_wide
    empty = (pooled[16:17] + b2_wide).astype(BF16)
    lane = iota((IMG, 256), 1)
    image_note = jnp.where(lane == PART, as_column(caption_high), jnp.where(lane == PART + 1, as_column(caption_low), image_own))
    ibuf[b] = image_note.astype(BF16)

    def send_image(i, k):
        peer = a * GROUP + lax.rem(b + i, GROUP)
        to_dp(peer, ibuf.at[b], ibuf.at[b], i_send.at[0], i_recv.at[0]).start()
        return k

    lax.fori_loop(1, GROUP, send_image, 0)

    for c in range(CH):
        third_sums(c)

    some = tbuf.at[pl.ds(0, GROUP - 1)]
    to_dp(neighbour, some, some, t_send.at[0], t_recv.at[0]).wait_recv()
    some = ibuf.at[pl.ds(0, GROUP - 1)]
    to_dp(neighbour, some, some, i_send.at[0], i_recv.at[0]).wait_recv()
    dots = nt(ibuf[...].reshape(SIDE, 256), tbuf[...].reshape(SIDE, 256))
    feature = iota((1, 256), 1) < PART
    image_f = jnp.where(feature, ibuf[...].reshape(SIDE, 256).astype(F32), 0.0)
    image_sq = jnp.sum(image_f * image_f, axis=1, keepdims=True)
    image_sq = jnp.where(iota((SIDE, SIDE), 1) == 0, image_sq, 0.0)
    text_f = tbuf[...].reshape(SIDE, 256).astype(F32)
    text_f = text_f * text_f
    top = text_f.astype(BF16)
    rest = (text_f - top.astype(F32)).astype(BF16)
    ones = jnp.ones((16, 256), BF16)
    text_sq = (nt(ones, top) + nt(ones, rest))[0:8]
    for k in range(MP):
        pair_out[k, 0:16] = dots[k * IMG : (k + 1) * IMG]
        pair_out[k, 16:32] = image_sq[k * IMG : (k + 1) * IMG]
        pair_out[k, 32:40] = text_sq

    def send_pair(i, k):
        there = lax.rem(m + i, MP)
        to_mp(i, pair_out.at[there], pair_in.at[m], pair_send.at[0], pair_recv.at[0]).start()
        return k

    lax.fori_loop(1, MP, send_pair, 0)
    pair_in[m] = pair_out[m]


    encoded = []
    for c in range(CH):
        total = share(c, m) + arrived_sum(c, 4) + arrived_sum(c, 5) + arrived_sum(c, 6)
        own = x_ref[:, c * L : (c + 1) * L].astype(F32)
        encoded.append(own + total + wide(b2_b[...]))
    encoded = jnp.concatenate(encoded, axis=1)
    by_row = jnp.transpose(jnp.concatenate([encoded, jnp.zeros((256 - PART, ROWS), F32)], axis=0))
    rows_out[:, 0:256] = by_row.astype(BF16)
    rows_out[:, 256:384] = pltpu.roll(by_row[:, 128:256], 16, 1).astype(BF16)
    empty_f = jnp.broadcast_to(empty.astype(F32), (128, 256))
    line = iota((128, 128), 0)
    empty_tail = empty_f[:, 128:256]
    empties = jnp.where(
        line == 0,
        empty_f[:, 0:128],
        jnp.where(line == 1, empty_tail, jnp.where(line == 2, pltpu.roll(empty_tail, 16, 1), 0.0)),
    ).astype(BF16)
    head_row = jnp.bitwise_and(iota((256, 1), 0), 15) < CAP

    def fill(i, k):
        b = lax.rem(s // 16 + 1 + i, DP // 16)
        lines = pl.ds(pl.multiple_of(b * 256, 256), 256)
        main = nn(pick[0, lines, :], rows_out[:, 0:256])
        odd = nn(pick[1, lines, :], rows_out[:, 256:384])
        got = jnp.where(head_row, main[:, 0:128], main[:, 128:256] + odd) + nn(empty_pick[lines, :], empties)
        slot_out[pl.ds(b * 16, 16)] = got.astype(BF16).reshape(16, 16, 128)

        def send_slots(j, k):
            peer = b * 16 + j

            @pl.when(peer != s)
            def _():
                to_dp(peer, slot_out.at[peer], slot_in.at[s], slot_send.at[0], slot_recv.at[0]).start()

            return k

        lax.fori_loop(0, 16, send_slots, 0)
        return k

    lax.fori_loop(0, DP // 16, fill, 0)
    slot_in[s] = slot_out[s]

    some = pair_in.at[pl.ds(0, MP - 1)]
    to_mp(1, some, some, pair_send.at[0], pair_recv.at[0]).wait_recv()
    total = pair_in[0]
    for k in range(1, MP):
        total = total + pair_in[k]
    image_scale = lax.rsqrt(total[16:32, 0:1] + 1e-06)
    text_scale = lax.rsqrt(total[32:33] + 1e-06)
    place = iota((1, SIDE), 1)
    text_name = (jnp.right_shift(place, 4) * (GROUP * IMG) + b * IMG + jnp.bitwise_and(place, 15)).astype(F32)
    noted = ibuf[m].astype(F32)
    caption = noted[:, PART : PART + 1] * 32.0 + noted[:, PART + 1 : PART + 2]
    logits = LOGIT_SCALE * (total[0:16] * image_scale * text_scale) + LOGIT_BIAS
    coef = 1.0 / (1.0 + jnp.exp(-logits)) - jnp.where(caption == text_name, 1.0, 0.0)
    coef_in[m] = jnp.concatenate([coef * text_scale, coef * image_scale], axis=0).astype(BF16)

    def send_coef(i, k):
        to_mp(i, coef_in.at[m], coef_in.at[m], coef_send.at[0], coef_recv.at[0]).start()
        return k

    lax.fori_loop(1, MP, send_coef, 0)
    some = coef_in.at[pl.ds(0, MP - 1)]
    to_mp(1, some, some, coef_send.at[0], coef_recv.at[0]).wait_recv()

    for_images = jnp.concatenate([coef_in[k, 0:16] for k in range(MP)], axis=0)
    for_texts = jnp.concatenate([coef_in[k, 16:32] for k in range(MP)], axis=0)
    part = LOGIT_SCALE * nn(for_images, tbuf[...].reshape(SIDE, 256))
    grad_out[0] = part.astype(BF16).reshape(GROUP, IMG, 256)
    part = LOGIT_SCALE * tn(for_texts, ibuf[...].reshape(SIDE, 256))
    grad_out[1] = part.astype(BF16).reshape(GROUP, IMG, 256)

    def send_grad(i, k):
        there = lax.rem(b + i, GROUP)
        to_dp(a * GROUP + there, grad_out.at[0, there], grad_in.at[0, b], grad_send.at[0], grad_recv.at[0]).start()
        there = lax.rem(a + i, GROUP)
        to_dp(there * GROUP + b, grad_out.at[1, there], grad_in.at[1, a], grad_send.at[1], grad_recv.at[1]).start()
        return k

    lax.fori_loop(1, GROUP, send_grad, 0)
    grad_in[0, b] = grad_out[0, b]
    grad_in[1, a] = grad_out[1, a]

    some = slot_in.at[pl.ds(0, DP - 1)]
    to_dp(neighbour, some, some, slot_send.at[0], slot_recv.at[0]).wait_recv()
    arrived = jnp.transpose(slot_in[...].reshape(DP * 16, 128))
    head_lane = jnp.bitwise_and(iota((1, DP * 16), 1), 15) < CAP
    nothing = jnp.zeros((16, DP * 16), BF16)
    main = jnp.concatenate([jnp.where(head_lane, arrived, 0), jnp.where(head_lane, nothing, arrived[0:16])], axis=0)
    odd = jnp.where(head_lane, nothing, arrived[16:32])
    placed = nn(main, sel[0])
    packed_ref[0:128, :] = placed[0:128].astype(BF16)
    packed_ref[128:PART, :] = (placed[128:PART] + nn(odd, sel[1])).astype(BF16)

    for n, result in enumerate((image_grad_ref, text_grad_ref)):
        some = grad_in.at[n, pl.ds(0, GROUP - 1)]
        to_dp(neighbour, some, some, grad_send.at[n], grad_recv.at[n]).wait_recv()
        sums = grad_in[n, 0].astype(F32)
        for k in range(1, GROUP):
            sums = sums + grad_in[n, k].astype(F32)
        result[...] = sums[:, 0:PART]

    for c in range(CH):
        some = xall.at[c, pl.ds(0, MP - 1), pl.ds(0, XROWS if c == 0 else PART)]
        to_mp(1, some, some, x_send.at[c], x_recv.at[c, 0]).wait_send()
        some = part_out.at[c, pl.ds(0, MP - 1)]
        to_mp(1, some, some, p_send.at[c], p_recv.at[c, 0]).wait_send()
    some = pool_out.at[pl.ds(0, MP - 1)]
    to_mp(1, some, some, pool_send.at[0], pool_recv.at[0]).wait_send()
    some = pair_out.at[pl.ds(0, MP - 1)]
    to_mp(1, some, some, pair_send.at[0], pair_recv.at[0]).wait_send()
    some = coef_in.at[pl.ds(0, MP - 1)]
    to_mp(1, some, some, coef_send.at[0], coef_recv.at[0]).wait_send()
    for buf, send, recv in (
        (tbuf, t_send.at[0], t_recv.at[0]),
        (ibuf, i_send.at[0], i_recv.at[0]),
        (grad_out.at[0], grad_send.at[0], grad_recv.at[0]),
        (grad_out.at[1], grad_send.at[1], grad_recv.at[1]),
    ):
        some = buf.at[pl.ds(0, GROUP - 1)]
        to_dp(neighbour, some, some, send, recv).wait_send()
    some = slot_out.at[pl.ds(0, DP - 1)]
    to_dp(neighbour, some, some, slot_send.at[0], slot_recv.at[0]).wait_send()


def hand_over(packed_in, image_in, text_in, packed_out, image_out, text_out):
    packed_out[...] = packed_in[...]
    image_out[...] = image_in[...]
    text_out[...] = text_in[...]


def shards(patches, patch_shard, patch_image, caption_of, text_embed, ln_gain, fc1_weight, fc1_bias, fc2_weight, fc2_bias):
    vmem = pl.BlockSpec(memory_space=pltpu.VMEM)
    hbm = pl.BlockSpec(memory_space=pltpu.HBM)
    dma = pltpu.SemaphoreType.DMA
    shapes = (
        jax.ShapeDtypeStruct((PART, SLOTS), BF16),
        jax.ShapeDtypeStruct((IMG, PART), F32),
        jax.ShapeDtypeStruct((IMG, PART), F32),
    )
    results = pl.pallas_call(
        kernel,
        out_shape=shapes,
        in_specs=[hbm] * 10,
        out_specs=(vmem, vmem, vmem),
        scratch_shapes=[
            pltpu.VMEM((PART, ROWS), BF16),
            pltpu.VMEM((IMG, PART), BF16),
            pltpu.VMEM((1, ROWS), I32),
            pltpu.VMEM((1, ROWS), I32),
            pltpu.VMEM((1, IMG), I32),
            pltpu.VMEM((PART,), BF16),
            pltpu.VMEM((FF,), BF16),
            pltpu.VMEM((PART,), BF16),
            pltpu.VMEM((FF, FULL), BF16),
            pltpu.VMEM((FF, FULL), BF16),
            pltpu.VMEM((8, FFP), F32),
            pltpu.VMEM((FULL, FFP), BF16),
            pltpu.VMEM((CH, MP, XROWS, L), BF16),
            pltpu.VMEM((FULL, 128), F32),
            pltpu.VMEM((FFP, 128), F32),
            pltpu.VMEM((PART, 128), F32),
            pltpu.VMEM((FFP, ROWS), BF16),
            pltpu.VMEM((CH, 7, PART, L), BF16),
            pltpu.VMEM((CH, 7, PART, L), BF16),
            pltpu.VMEM((MP, 24, 256), F32),
            pltpu.VMEM((MP, 24, 256), F32),
            pltpu.VMEM((GROUP, IMG, 256), BF16),
            pltpu.VMEM((GROUP, IMG, 256), BF16),
            pltpu.VMEM((MP, 40, SIDE), F32),
            pltpu.VMEM((MP, 40, SIDE), F32),
            pltpu.VMEM((MP, 32, SIDE), BF16),
            pltpu.VMEM((2, GROUP, IMG, 256), BF16),
            pltpu.VMEM((2, GROUP, IMG, 256), BF16),
            pltpu.VMEM((2, DP * 16, ROWS), BF16),
            pltpu.VMEM((DP * 16, 128), BF16),
            pltpu.VMEM((2, DP * 16, SLOTS), BF16),
            pltpu.VMEM((ROWS, 384), BF16),
            pltpu.VMEM((DP, 16, 128), BF16),
            pltpu.VMEM((DP, 16, 128), BF16),
            dma((10,)),
            dma((CH,)), dma((CH, 7)),
            dma((1,)), dma((1,)),
            dma((CH,)), dma((CH, 7)),
            dma((1,)), dma((1,)),
            dma((1,)), dma((1,)),
            dma((1,)), dma((1,)),
            dma((1,)), dma((1,)),
            dma((2,)), dma((2,)),
            dma((1,)), dma((1,)),
        ],
        compiler_params=pltpu.CompilerParams(
            collective_id=0, has_side_effects=True, vmem_limit_bytes=60 * 1024 * 1024
        ),
    )(
        patches.T, text_embed, patch_shard.reshape(1, ROWS), patch_image, caption_of.reshape(1, IMG),
        ln_gain, fc1_bias, fc2_bias, fc1_weight.T, fc2_weight,
    )
    packed, image_grad, text_grad = pl.pallas_call(
        hand_over,
        out_shape=shapes,
        in_specs=[vmem] * 3,
        out_specs=(vmem,) * 3,
        compiler_params=pltpu.CompilerParams(vmem_limit_bytes=60 * 1024 * 1024),
    )(*results)
    return packed.T[None], image_grad, text_grad


def solution(mesh):
    return jax.shard_map(
        shards,
        mesh=mesh,
        in_specs=(
            P("dp", "mp"),
            P("dp", None),
            P("dp", None),
            P("dp"),
            P("dp", "mp"),
            P("mp"),
            P(None, "mp"),
            P("mp"),
            P("mp", None),
            P("mp"),
        ),
        out_specs=(P("dp", None, "mp"), P("dp", "mp"), P("dp", "mp")),
        check_vma=False,
    )
```

```python
import functools

import jax
import jax.numpy as jnp
from jax import lax
from jax.experimental import pallas as pl
from jax.experimental.pallas import tpu as pltpu
from jax.sharding import PartitionSpec as P

LOGIT_SCALE = 10.0
LOGIT_BIAS = -2.0
F32 = jnp.float32
BF16 = jnp.bfloat16
I32 = jnp.int32
MESH = pl.DeviceIdType.MESH

DP, MP = 64, 8
GROUP = 8
ROWS, PART, FULL = 512, 144, 1152
FF, FFP = 538, 640
IMG, CAP = 16, 10
SLOTS = DP * CAP
CH = 2
L = ROWS // CH
SIDE = GROUP * IMG
XROWS = PART + 16


def nn(a, b):
    return jnp.dot(a, b, preferred_element_type=F32)


def nt(a, b):
    return lax.dot_general(a, b, (((1,), (1,)), ((), ())), preferred_element_type=F32)


def tn(a, b):
    return lax.dot_general(a, b, (((0,), (0,)), ((), ())), preferred_element_type=F32)


def iota(shape, axis):
    return lax.broadcasted_iota(I32, shape, axis)


def gelu(h):
    return 0.5 * h * (1.0 + jnp.tanh(0.7978845608028654 * (h + 0.044715 * (h * h * h))))


def wide(column_block):
    return jnp.concatenate([column_block] * (L // 128), axis=1)


def kernel(
    x_hbm, text_hbm, target_hbm, owner_hbm, caption_hbm, gain_hbm, b1_hbm, b2_hbm, w1_hbm, w2_hbm,
    packed_ref, image_grad_ref, text_grad_ref,
    x_ref, text_ref, target_ref, owner_ref, caption_ref, gain_ref, b1_ref, b2_ref, w1, w2,
    small_ref, w2t, xall, gain_b, b1_b, b2_b, hid, part_out, part_in,
    pool_out, pool_in, tbuf, ibuf, pair_out, pair_in, coef_in, grad_out, grad_in,
    pick, empty_pick, sel, rows_out, slot_out, slot_in,
    load_sem, x_send, x_recv, t_send, t_recv, p_send, p_recv,
    pool_send, pool_recv, i_send, i_recv, pair_send, pair_recv, coef_send, coef_recv,
    grad_send, grad_recv, slot_send, slot_recv,
):
    s = lax.axis_index("dp")
    m = lax.axis_index("mp")
    a = s // GROUP
    b = lax.rem(s, GROUP)
    neighbour = lax.rem(s + 1, DP)

    ring, side = m // 2, lax.rem(m, 2)
    ahead = lax.rem(ring + 1, 4) * 2 + side
    behind = lax.rem(ring + 3, 4) * 2 + side
    far = lax.rem(ring + 2, 4) * 2 + side
    across = ring * 2 + 1 - side
    ahead_across = lax.rem(ring + 1, 4) * 2 + 1 - side
    behind_across = lax.rem(ring + 3, 4) * 2 + 1 - side
    far_across = lax.rem(ring + 2, 4) * 2 + 1 - side

    loads = [
        pltpu.make_async_copy(src, dst, load_sem.at[n])
        for n, (src, dst) in enumerate(
            (
                (x_hbm, x_ref), (gain_hbm, gain_ref), (text_hbm, text_ref), (caption_hbm, caption_ref),
                (target_hbm, target_ref), (owner_hbm, owner_ref), (b1_hbm, b1_ref), (b2_hbm, b2_ref),
                (w1_hbm, w1), (w2_hbm, w2),
            )
        )
    ]
    for load in loads:
        load.start()

    barrier = pltpu.get_barrier_semaphore()

    def greet_mp(i, c):
        pl.semaphore_signal(barrier, inc=1, device_id=(s, lax.rem(m + i, MP)), device_id_type=MESH)
        return c

    def greet_dp(i, c):
        images = a * GROUP + lax.rem(b + i, GROUP)
        texts = lax.rem(a + i, GROUP) * GROUP + b
        pl.semaphore_signal(barrier, inc=1, device_id=(images, m), device_id_type=MESH)
        pl.semaphore_signal(barrier, inc=1, device_id=(texts, m), device_id_type=MESH)
        return c

    lax.fori_loop(1, MP, greet_mp, 0, unroll=True)
    lax.fori_loop(1, GROUP, greet_dp, 0, unroll=True)

    def to_member(member, src, dst, send, recv):
        return pltpu.make_async_remote_copy(
            src_ref=src, dst_ref=dst, send_sem=send, recv_sem=recv,
            device_id=(s, member), device_id_type=MESH,
        )

    def to_mp(i, src, dst, send, recv):
        return to_member(lax.rem(m + i, MP), src, dst, send, recv)

    def to_dp(peer, src, dst, send, recv):
        return pltpu.make_async_remote_copy(
            src_ref=src, dst_ref=dst, send_sem=send, recv_sem=recv,
            device_id=(peer, m), device_id_type=MESH,
        )

    small_ref[...] = jnp.zeros_like(small_ref)
    loads[0].wait()
    loads[1].wait()
    small_ref[1:2, 0:PART] = gain_ref[...].astype(F32).reshape(1, PART)
    for c in range(CH):
        xall[c, m, 0:PART] = x_ref[:, c * L : (c + 1) * L]
    xall[0, m, PART:XROWS] = jnp.broadcast_to(small_ref[1:2, 0:L], (XROWS - PART, L)).astype(BF16)

    pl.semaphore_wait(barrier, MP - 1 + 2 * (GROUP - 1))

    def block(c, member):
        return xall.at[c, member, pl.ds(0, XROWS if c == 0 else PART)]

    def hand_on(c, owner, member, kind):
        to_member(member, block(c, owner), block(c, owner), x_send.at[c], x_recv.at[c, kind]).start()

    def expect(c, kind):
        to_member(across, block(c, m), block(c, m), x_send.at[c], x_recv.at[c, kind]).wait_recv()

    for c in range(CH):
        hand_on(c, m, across, 2)
        hand_on(c, m, ahead, 0)
        hand_on(c, m, behind, 1)

    for load in loads[2:8]:
        load.wait()
    small_ref[0:1, 0:FF] = b1_ref[...].astype(F32).reshape(1, FF)
    small_ref[2:3, 0:PART] = b2_ref[...].astype(F32).reshape(1, PART)
    diagonal = iota((IMG, IMG), 0) == iota((IMG, IMG), 1)
    caption_row = caption_ref[...]
    caption_high = jnp.right_shift(caption_row, 5)
    caption_low = jnp.bitwise_and(caption_row, 31)

    def as_column(row):
        return jnp.sum(jnp.where(diagonal, row.astype(F32), 0.0), axis=1, keepdims=True)

    text_own_f = jnp.concatenate([text_ref[...].astype(F32), jnp.zeros((IMG, 256 - PART), F32)], axis=1)
    tbuf[a] = text_own_f.astype(BF16)

    def send_text(i, k):
        peer = lax.rem(a + i, GROUP) * GROUP + b
        to_dp(peer, tbuf.at[a], tbuf.at[a], t_send.at[0], t_recv.at[0]).start()
        return k


    for c in range(CH):
        if c == 0:
            expect(c, 0)
            hand_on(c, behind, ahead, 5)
        else:
            expect(c, 1)
            hand_on(c, ahead, behind, 5)
        expect(c, 2)
        hand_on(c, across, ahead, 3)
        hand_on(c, across, behind, 4)

    lax.fori_loop(1, GROUP, send_text, 0, unroll=True)

    targets = target_ref[...]
    named = iota((DP, ROWS), 0) == targets
    named_b = jnp.where(named, 1.0, 0.0).astype(BF16)
    earlier = jnp.where(iota((ROWS, ROWS), 0) < iota((ROWS, ROWS), 1), 1.0, 0.0).astype(BF16)
    before = nn(named_b, earlier)
    rank = jnp.sum(jnp.where(named, before, 0.0), axis=0, keepdims=True).astype(I32)
    code = targets * 16 + rank

    first_row = jnp.where(iota((16, 128), 0) == 0, 1.0, 0.0).astype(BF16)
    b1_row = jnp.broadcast_to(small_ref[0:1, :], (16, FFP))
    b1_b[...] = tn(b1_row.astype(BF16), first_row)
    b2_row = jnp.broadcast_to(small_ref[2:3, 0:256], (16, 256)).astype(BF16)
    b2_b[...] = tn(b2_row, first_row)[0:PART]
    hid[...] = jnp.zeros_like(hid)
    for c in range(CH):
        expect(c, 5)
        hand_on(c, far, across, 6)

    def build_pick(b, k):
        row = iota((128, 1), 0) + b * 128
        slot = jnp.bitwise_and(row, 15)
        base = row - slot
        is_head = slot < CAP
        is_tail = jnp.logical_and(slot >= CAP, slot < CAP + CAP // 2)
        even = base + 2 * (slot - CAP)
        lines = pl.ds(pl.multiple_of(b * 128, 128), 128)
        lane = iota((128, 128), 1)
        main = jnp.where(jnp.where(is_head, row, jnp.where(is_tail, even, -1)) == code, 1.0, 0.0)
        odd = jnp.where(jnp.where(is_tail, even + 1, -1) == code, 1.0, 0.0)
        pick[0, lines, :] = main.astype(BF16)
        pick[1, lines, :] = odd.astype(BF16)
        lack = 1.0 - jnp.sum(main, axis=1, keepdims=True)
        lack_odd = 1.0 - jnp.sum(odd, axis=1, keepdims=True)
        lacks = jnp.where(
            lane == 0,
            jnp.where(is_head, lack, 0.0),
            jnp.where(lane == 1, jnp.where(is_tail, lack, 0.0), jnp.where(lane == 2, jnp.where(is_tail, lack_odd, 0.0), 0.0)),
        )
        empty_pick[lines, :] = lacks.astype(BF16)
        column = iota((128, SLOTS), 1)
        first = jnp.right_shift(row, 4) * CAP
        even_at = first + 2 * (slot - CAP)
        main_at = jnp.where(is_head, first + slot, jnp.where(is_tail, even_at, -1))
        odd_at = jnp.where(is_tail, even_at + 1, -1)
        sel[0, lines, :] = jnp.where(main_at == column, 1.0, 0.0).astype(BF16)
        sel[1, lines, :] = jnp.where(odd_at == column, 1.0, 0.0).astype(BF16)
        return k

    lax.fori_loop(0, DP * 16 // 128, build_pick, 0)

    loads[8].wait()
    loads[9].wait()
    w2t[:, 0:512] = jnp.transpose(w2[0:512, :])
    tail_rows = jnp.concatenate([w2[512:FF, :].astype(F32), jnp.zeros((FFP - FF, FULL), F32)], axis=0)
    w2t[:, 512:FFP] = jnp.transpose(tail_rows).astype(BF16)

    def share(c, member):
        lines = pl.ds(pl.multiple_of(member * PART, 16), PART)
        return nn(w2t[lines, :], hid[:, c * L : (c + 1) * L])

    def pass_on(c, value, member, kind):
        part_out[c, kind] = value.astype(BF16)
        to_member(member, part_out.at[c, kind], part_in.at[c, kind], p_send.at[c], p_recv.at[c, kind]).start()

    def arrived_sum(c, kind):
        to_member(across, part_in.at[c, kind], part_in.at[c, kind], p_send.at[c], p_recv.at[c, kind]).wait_recv()
        return part_in[c, kind].astype(F32)

    def first_sums(c):
        pass_on(c, share(c, far_across), across, 0)
        pass_on(c, share(c, ahead_across), ahead, 1)
        pass_on(c, share(c, behind_across), behind, 2)
        if c == 0:
            pass_on(c, share(c, behind), behind, 5)
        else:
            pass_on(c, share(c, ahead), ahead, 4)

    def second_sums(c):
        pass_on(c, share(c, far) + arrived_sum(c, 0), ahead if c == 0 else behind, 3)
        pass_on(c, share(c, across) + arrived_sum(c, 1) + arrived_sum(c, 2), across, 6)

    def third_sums(c):
        if c == 0:
            pass_on(c, share(c, ahead) + arrived_sum(c, 3), ahead, 4)
        else:
            pass_on(c, share(c, behind) + arrived_sum(c, 3), behind, 5)

    for c in range(CH):
        for kind in (1 if c == 0 else 0, 3, 4, 6):
            expect(c, kind)
        if c == 0:
            for k in range(MP):
                gain_b[k * PART : (k + 1) * PART, :] = tn(xall[0, k, PART:XROWS], first_row)[0:PART]

        rows = xall[c, :, 0:PART].reshape(FULL, L).astype(F32)
        centre = rows - jnp.sum(rows, axis=0, keepdims=True) * (1.0 / FULL)
        spread = jnp.sum(centre * centre, axis=0, keepdims=True) * (1.0 / FULL)
        normed = (centre * lax.rsqrt(spread + 1e-06) * wide(gain_b[...])).astype(BF16)
        pre = nn(w1[...], normed) + wide(b1_b[0:FF, :])
        hid[0:FF, c * L : (c + 1) * L] = gelu(pre).astype(BF16)

        if c < CH - 1:
            first_sums(c)

    first_sums(CH - 1)
    member_f = jnp.where(iota((IMG, ROWS), 0) == owner_ref[...], 1.0, 0.0)
    member = member_f.astype(BF16)
    sums = nt(member, hid[...])
    high = sums.astype(BF16)
    low = (sums - high.astype(F32)).astype(BF16)
    lone = gelu(b1_row).astype(BF16)
    mixed = jnp.concatenate([high, low, lone], axis=0)

    def pool_block(i, k):
        there = lax.rem(m + i, MP)
        lines = pl.ds(pl.multiple_of(there * PART, 16), PART)
        got = nt(mixed, w2t[lines, :])
        pool_out[there, 0:16, 0:PART] = got[0:16] + got[16:32]
        pool_out[there, 16:24, 0:PART] = got[32:40]
        return k

    pool_out[...] = jnp.zeros_like(pool_out)
    lax.fori_loop(0, MP, pool_block, 0)

    def send_pool(i, k):
        there = lax.rem(m + i, MP)
        to_mp(i, pool_out.at[there], pool_in.at[m], pool_send.at[0], pool_recv.at[0]).start()
        return k

    lax.fori_loop(1, MP, send_pool, 0, unroll=True)
    pool_in[m] = pool_out[m]

    for c in range(CH):
        second_sums(c)

    some = pool_in.at[pl.ds(0, MP - 1)]
    to_mp(1, some, some, pool_send.at[0], pool_recv.at[0]).wait_recv()
    pooled = pool_in[0]
    for k in range(1, MP):
        pooled = pooled + pool_in[k]
    b2_wide = jnp.where(iota((1, 256), 1) < PART, small_ref[2:3, 0:256], 0.0)
    counts = jnp.sum(member_f, axis=1, keepdims=True)
    own_sum = nt(member, x_ref[...])
    own_sum = jnp.concatenate([own_sum, jnp.zeros((IMG, 256 - PART), F32)], axis=1)
    image_own = (pooled[0:16] + own_sum) / counts + b2_wide
    empty = (pooled[16:17] + b2_wide).astype(BF16)
    lane = iota((IMG, 256), 1)
    image_note = jnp.where(lane == PART, as_column(caption_high), jnp.where(lane == PART + 1, as_column(caption_low), image_own))
    ibuf[b] = image_note.astype(BF16)

    some = tbuf.at[pl.ds(0, GROUP - 1)]
    to_dp(neighbour, some, some, t_send.at[0], t_recv.at[0]).wait_recv()

    def send_image(i, k):
        peer = a * GROUP + lax.rem(b + i, GROUP)
        to_dp(peer, ibuf.at[b], ibuf.at[b], i_send.at[0], i_recv.at[0]).start()
        return k

    lax.fori_loop(1, GROUP, send_image, 0, unroll=True)

    for c in range(CH):
        third_sums(c)

    some = ibuf.at[pl.ds(0, GROUP - 1)]
    to_dp(neighbour, some, some, i_send.at[0], i_recv.at[0]).wait_recv()
    dots = nt(ibuf[...].reshape(SIDE, 256), tbuf[...].reshape(SIDE, 256))
    feature = iota((1, 256), 1) < PART
    image_f = jnp.where(feature, ibuf[...].reshape(SIDE, 256).astype(F32), 0.0)
    image_sq = jnp.sum(image_f * image_f, axis=1, keepdims=True)
    image_sq = jnp.where(iota((SIDE, SIDE), 1) == 0, image_sq, 0.0)
    text_f = tbuf[...].reshape(SIDE, 256).astype(F32)
    text_f = text_f * text_f
    top = text_f.astype(BF16)
    rest = (text_f - top.astype(F32)).astype(BF16)
    ones = jnp.ones((16, 256), BF16)
    text_sq = (nt(ones, top) + nt(ones, rest))[0:8]
    for k in range(MP):
        pair_out[k, 0:16] = dots[k * IMG : (k + 1) * IMG]
        pair_out[k, 16:32] = image_sq[k * IMG : (k + 1) * IMG]
        pair_out[k, 32:40] = text_sq

    def send_pair(i, k):
        there = lax.rem(m + i, MP)
        to_mp(i, pair_out.at[there], pair_in.at[m], pair_send.at[0], pair_recv.at[0]).start()
        return k

    lax.fori_loop(1, MP, send_pair, 0, unroll=True)
    pair_in[m] = pair_out[m]


    encoded = []
    for c in range(CH):
        total = share(c, m) + arrived_sum(c, 4) + arrived_sum(c, 5) + arrived_sum(c, 6)
        own = x_ref[:, c * L : (c + 1) * L].astype(F32)
        encoded.append(own + total + wide(b2_b[...]))
    encoded = jnp.concatenate(encoded, axis=1)
    by_row = jnp.transpose(jnp.concatenate([encoded, jnp.zeros((256 - PART, ROWS), F32)], axis=0))
    rows_out[:, 0:256] = by_row.astype(BF16)
    rows_out[:, 256:384] = pltpu.roll(by_row[:, 128:256], 16, 1).astype(BF16)
    empty_f = jnp.broadcast_to(empty.astype(F32), (128, 256))
    line = iota((128, 128), 0)
    empty_tail = empty_f[:, 128:256]
    empties = jnp.where(
        line == 0,
        empty_f[:, 0:128],
        jnp.where(line == 1, empty_tail, jnp.where(line == 2, pltpu.roll(empty_tail, 16, 1), 0.0)),
    ).astype(BF16)
    head_row = jnp.bitwise_and(iota((256, 1), 0), 15) < CAP

    def fill(block):
        lines = pl.ds(pl.multiple_of(block * 256, 256), 256)
        main = nn(pick[0, lines, :], rows_out[:, 0:256])
        odd = nn(pick[1, lines, :], rows_out[:, 256:384])
        got = jnp.where(head_row, main[:, 0:128], main[:, 128:256] + odd) + nn(empty_pick[lines, :], empties)
        slot_out[pl.ds(block * 16, 16)] = got.astype(BF16).reshape(16, 16, 128)

    def send_slot(peer):
        to_dp(peer, slot_out.at[peer], slot_in.at[s], slot_send.at[0], slot_recv.at[0]).start()

    def fill_other(i, k):
        block = lax.rem(s // 16 + i, DP // 16)
        fill(block)
        for j in range(16):
            send_slot(block * 16 + j)
        return k

    lax.fori_loop(1, DP // 16, fill_other, 0)
    fill(s // 16)
    for j in range(1, 16):
        send_slot(s // 16 * 16 + lax.rem(s + j, 16))
    slot_in[s] = slot_out[s]

    some = pair_in.at[pl.ds(0, MP - 1)]
    to_mp(1, some, some, pair_send.at[0], pair_recv.at[0]).wait_recv()
    total = pair_in[0]
    for k in range(1, MP):
        total = total + pair_in[k]
    image_scale = lax.rsqrt(total[16:32, 0:1] + 1e-06)
    text_scale = lax.rsqrt(total[32:33] + 1e-06)
    place = iota((1, SIDE), 1)
    text_name = (jnp.right_shift(place, 4) * (GROUP * IMG) + b * IMG + jnp.bitwise_and(place, 15)).astype(F32)
    noted = ibuf[m].astype(F32)
    caption = noted[:, PART : PART + 1] * 32.0 + noted[:, PART + 1 : PART + 2]
    logits = LOGIT_SCALE * (total[0:16] * image_scale * text_scale) + LOGIT_BIAS
    coef = 1.0 / (1.0 + jnp.exp(-logits)) - jnp.where(caption == text_name, 1.0, 0.0)
    coef_in[m] = jnp.concatenate([coef * text_scale, coef * image_scale], axis=0).astype(BF16)

    def send_coef(i, k):
        to_mp(i, coef_in.at[m], coef_in.at[m], coef_send.at[0], coef_recv.at[0]).start()
        return k

    lax.fori_loop(1, MP, send_coef, 0, unroll=True)
    some = coef_in.at[pl.ds(0, MP - 1)]
    to_mp(1, some, some, coef_send.at[0], coef_recv.at[0]).wait_recv()

    for_images = jnp.concatenate([coef_in[k, 0:16] for k in range(MP)], axis=0)
    for_texts = jnp.concatenate([coef_in[k, 16:32] for k in range(MP)], axis=0)
    part = LOGIT_SCALE * nn(for_images, tbuf[...].reshape(SIDE, 256))
    grad_out[0] = part.astype(BF16).reshape(GROUP, IMG, 256)
    part = LOGIT_SCALE * tn(for_texts, ibuf[...].reshape(SIDE, 256))
    grad_out[1] = part.astype(BF16).reshape(GROUP, IMG, 256)

    def send_grad(i, k):
        there = lax.rem(b + i, GROUP)
        to_dp(a * GROUP + there, grad_out.at[0, there], grad_in.at[0, b], grad_send.at[0], grad_recv.at[0]).start()
        there = lax.rem(a + i, GROUP)
        to_dp(there * GROUP + b, grad_out.at[1, there], grad_in.at[1, a], grad_send.at[1], grad_recv.at[1]).start()
        return k

    lax.fori_loop(1, GROUP, send_grad, 0, unroll=True)
    grad_in[0, b] = grad_out[0, b]
    grad_in[1, a] = grad_out[1, a]

    some = slot_in.at[pl.ds(0, DP - 1)]
    to_dp(neighbour, some, some, slot_send.at[0], slot_recv.at[0]).wait_recv()
    arrived = jnp.transpose(slot_in[...].reshape(DP * 16, 128))
    head_lane = jnp.bitwise_and(iota((1, DP * 16), 1), 15) < CAP
    nothing = jnp.zeros((16, DP * 16), BF16)
    main = jnp.concatenate([jnp.where(head_lane, arrived, 0), jnp.where(head_lane, nothing, arrived[0:16])], axis=0)
    odd = jnp.where(head_lane, nothing, arrived[16:32])
    placed = nn(main, sel[0])
    packed_ref[0:128, :] = placed[0:128].astype(BF16)
    packed_ref[128:PART, :] = (placed[128:PART] + nn(odd, sel[1])).astype(BF16)

    for n, result in enumerate((image_grad_ref, text_grad_ref)):
        some = grad_in.at[n, pl.ds(0, GROUP - 1)]
        to_dp(neighbour, some, some, grad_send.at[n], grad_recv.at[n]).wait_recv()
        sums = grad_in[n, 0].astype(F32)
        for k in range(1, GROUP):
            sums = sums + grad_in[n, k].astype(F32)
        result[...] = sums[:, 0:PART]

    for c in range(CH):
        some = xall.at[c, pl.ds(0, MP - 1), pl.ds(0, XROWS if c == 0 else PART)]
        to_mp(1, some, some, x_send.at[c], x_recv.at[c, 0]).wait_send()
        some = part_out.at[c, pl.ds(0, MP - 1)]
        to_mp(1, some, some, p_send.at[c], p_recv.at[c, 0]).wait_send()
    some = pool_out.at[pl.ds(0, MP - 1)]
    to_mp(1, some, some, pool_send.at[0], pool_recv.at[0]).wait_send()
    some = pair_out.at[pl.ds(0, MP - 1)]
    to_mp(1, some, some, pair_send.at[0], pair_recv.at[0]).wait_send()
    some = coef_in.at[pl.ds(0, MP - 1)]
    to_mp(1, some, some, coef_send.at[0], coef_recv.at[0]).wait_send()
    for buf, send, recv in (
        (tbuf, t_send.at[0], t_recv.at[0]),
        (ibuf, i_send.at[0], i_recv.at[0]),
        (grad_out.at[0], grad_send.at[0], grad_recv.at[0]),
        (grad_out.at[1], grad_send.at[1], grad_recv.at[1]),
    ):
        some = buf.at[pl.ds(0, GROUP - 1)]
        to_dp(neighbour, some, some, send, recv).wait_send()
    some = slot_out.at[pl.ds(0, DP - 1)]
    to_dp(neighbour, some, some, slot_send.at[0], slot_recv.at[0]).wait_send()


def hand_over(packed_in, image_in, text_in, packed_out, image_out, text_out):
    packed_out[...] = packed_in[...]
    image_out[...] = image_in[...]
    text_out[...] = text_in[...]


def shards(patches, patch_shard, patch_image, caption_of, text_embed, ln_gain, fc1_weight, fc1_bias, fc2_weight, fc2_bias):
    vmem = pl.BlockSpec(memory_space=pltpu.VMEM)
    hbm = pl.BlockSpec(memory_space=pltpu.HBM)
    dma = pltpu.SemaphoreType.DMA
    shapes = (
        jax.ShapeDtypeStruct((PART, SLOTS), BF16),
        jax.ShapeDtypeStruct((IMG, PART), F32),
        jax.ShapeDtypeStruct((IMG, PART), F32),
    )
    results = pl.pallas_call(
        kernel,
        out_shape=shapes,
        in_specs=[hbm] * 10,
        out_specs=(vmem, vmem, vmem),
        scratch_shapes=[
            pltpu.VMEM((PART, ROWS), BF16),
            pltpu.VMEM((IMG, PART), BF16),
            pltpu.VMEM((1, ROWS), I32),
            pltpu.VMEM((1, ROWS), I32),
            pltpu.VMEM((1, IMG), I32),
            pltpu.VMEM((PART,), BF16),
            pltpu.VMEM((FF,), BF16),
            pltpu.VMEM((PART,), BF16),
            pltpu.VMEM((FF, FULL), BF16),
            pltpu.VMEM((FF, FULL), BF16),
            pltpu.VMEM((8, FFP), F32),
            pltpu.VMEM((FULL, FFP), BF16),
            pltpu.VMEM((CH, MP, XROWS, L), BF16),
            pltpu.VMEM((FULL, 128), F32),
            pltpu.VMEM((FFP, 128), F32),
            pltpu.VMEM((PART, 128), F32),
            pltpu.VMEM((FFP, ROWS), BF16),
            pltpu.VMEM((CH, 7, PART, L), BF16),
            pltpu.VMEM((CH, 7, PART, L), BF16),
            pltpu.VMEM((MP, 24, 256), F32),
            pltpu.VMEM((MP, 24, 256), F32),
            pltpu.VMEM((GROUP, IMG, 256), BF16),
            pltpu.VMEM((GROUP, IMG, 256), BF16),
            pltpu.VMEM((MP, 40, SIDE), F32),
            pltpu.VMEM((MP, 40, SIDE), F32),
            pltpu.VMEM((MP, 32, SIDE), BF16),
            pltpu.VMEM((2, GROUP, IMG, 256), BF16),
            pltpu.VMEM((2, GROUP, IMG, 256), BF16),
            pltpu.VMEM((2, DP * 16, ROWS), BF16),
            pltpu.VMEM((DP * 16, 128), BF16),
            pltpu.VMEM((2, DP * 16, SLOTS), BF16),
            pltpu.VMEM((ROWS, 384), BF16),
            pltpu.VMEM((DP, 16, 128), BF16),
            pltpu.VMEM((DP, 16, 128), BF16),
            dma((10,)),
            dma((CH,)), dma((CH, 7)),
            dma((1,)), dma((1,)),
            dma((CH,)), dma((CH, 7)),
            dma((1,)), dma((1,)),
            dma((1,)), dma((1,)),
            dma((1,)), dma((1,)),
            dma((1,)), dma((1,)),
            dma((2,)), dma((2,)),
            dma((1,)), dma((1,)),
        ],
        compiler_params=pltpu.CompilerParams(
            collective_id=0, has_side_effects=True, vmem_limit_bytes=60 * 1024 * 1024
        ),
    )(
        patches.T, text_embed, patch_shard.reshape(1, ROWS), patch_image, caption_of.reshape(1, IMG),
        ln_gain, fc1_bias, fc2_bias, fc1_weight.T, fc2_weight,
    )
    packed, image_grad, text_grad = pl.pallas_call(
        hand_over,
        out_shape=shapes,
        in_specs=[vmem] * 3,
        out_specs=(vmem,) * 3,
        compiler_params=pltpu.CompilerParams(vmem_limit_bytes=60 * 1024 * 1024),
    )(*results)
    return packed.T[None], image_grad, text_grad


def solution(mesh):
    return jax.shard_map(
        shards,
        mesh=mesh,
        in_specs=(
            P("dp", "mp"),
            P("dp", None),
            P("dp", None),
            P("dp"),
            P("dp", "mp"),
            P("mp"),
            P(None, "mp"),
            P("mp"),
            P("mp", None),
            P("mp"),
        ),
        out_specs=(P("dp", None, "mp"), P("dp", "mp"), P("dp", "mp")),
        check_vma=False,
    )
```

```python
import functools

import jax
import jax.numpy as jnp
from jax import lax
from jax.experimental import pallas as pl
from jax.experimental.pallas import tpu as pltpu
from jax.sharding import PartitionSpec as P

LOGIT_SCALE = 10.0
LOGIT_BIAS = -2.0
F32 = jnp.float32
BF16 = jnp.bfloat16
I32 = jnp.int32
MESH = pl.DeviceIdType.MESH

DP, MP = 64, 8
GROUP = 8
ROWS, PART, FULL = 512, 144, 1152
FF, FFP = 538, 640
IMG, CAP = 16, 10
SLOTS = DP * CAP
CH = 2
L = ROWS // CH
SIDE = GROUP * IMG
XROWS = PART + 16


def nn(a, b):
    return jnp.dot(a, b, preferred_element_type=F32)


def nt(a, b):
    return lax.dot_general(a, b, (((1,), (1,)), ((), ())), preferred_element_type=F32)


def tn(a, b):
    return lax.dot_general(a, b, (((0,), (0,)), ((), ())), preferred_element_type=F32)


def iota(shape, axis):
    return lax.broadcasted_iota(I32, shape, axis)


def gelu(h):
    return 0.5 * h * (1.0 + jnp.tanh(0.7978845608028654 * (h + 0.044715 * (h * h * h))))


def wide(column_block):
    return jnp.concatenate([column_block] * (L // 128), axis=1)


def kernel(
    x_hbm, text_hbm, target_hbm, owner_hbm, caption_hbm, gain_hbm, b1_hbm, b2_hbm, w1_hbm, w2_hbm,
    packed_ref, image_grad_ref, text_grad_ref,
    x_ref, text_ref, target_ref, owner_ref, caption_ref, gain_ref, b1_ref, b2_ref, w1, w2,
    small_ref, w2t, xall, gain_b, b1_b, b2_b, normed, hid, shares, part_out, part_in,
    pool_out, pool_in, tbuf, ibuf, pair_out, pair_in, coef_in, grad_out, grad_in,
    earlier, pick, empty_pick, sel, rows_out, slot_out, slot_in,
    load_sem, x_send, x_recv, t_send, t_recv, p_send, p_recv,
    pool_send, pool_recv, i_send, i_recv, pair_send, pair_recv, coef_send, coef_recv,
    grad_send, grad_recv, slot_send, slot_recv,
):
    s = lax.axis_index("dp")
    m = lax.axis_index("mp")
    a = s // GROUP
    b = lax.rem(s, GROUP)
    neighbour = lax.rem(s + 1, DP)

    ring, side = m // 2, lax.rem(m, 2)
    ahead = lax.rem(ring + 1, 4) * 2 + side
    behind = lax.rem(ring + 3, 4) * 2 + side
    far = lax.rem(ring + 2, 4) * 2 + side
    across = ring * 2 + 1 - side
    ahead_across = lax.rem(ring + 1, 4) * 2 + 1 - side
    behind_across = lax.rem(ring + 3, 4) * 2 + 1 - side
    far_across = lax.rem(ring + 2, 4) * 2 + 1 - side

    loads = [
        pltpu.make_async_copy(src, dst, load_sem.at[n])
        for n, (src, dst) in enumerate(
            (
                (x_hbm, x_ref), (gain_hbm, gain_ref), (text_hbm, text_ref), (caption_hbm, caption_ref),
                (target_hbm, target_ref), (owner_hbm, owner_ref), (b1_hbm, b1_ref), (b2_hbm, b2_ref),
                (w1_hbm, w1), (w2_hbm, w2),
            )
        )
    ]
    for load in loads:
        load.start()

    barrier = pltpu.get_barrier_semaphore()

    def greet_mp(i, c):
        pl.semaphore_signal(barrier, inc=1, device_id=(s, lax.rem(m + i, MP)), device_id_type=MESH)
        return c

    def greet_dp(i, c):
        images = a * GROUP + lax.rem(b + i, GROUP)
        texts = lax.rem(a + i, GROUP) * GROUP + b
        pl.semaphore_signal(barrier, inc=1, device_id=(images, m), device_id_type=MESH)
        pl.semaphore_signal(barrier, inc=1, device_id=(texts, m), device_id_type=MESH)
        return c

    lax.fori_loop(1, MP, greet_mp, 0, unroll=True)
    lax.fori_loop(1, GROUP, greet_dp, 0, unroll=True)

    def to_member(member, src, dst, send, recv):
        return pltpu.make_async_remote_copy(
            src_ref=src, dst_ref=dst, send_sem=send, recv_sem=recv,
            device_id=(s, member), device_id_type=MESH,
        )

    def to_mp(i, src, dst, send, recv):
        return to_member(lax.rem(m + i, MP), src, dst, send, recv)

    def to_dp(peer, src, dst, send, recv):
        return pltpu.make_async_remote_copy(
            src_ref=src, dst_ref=dst, send_sem=send, recv_sem=recv,
            device_id=(peer, m), device_id_type=MESH,
        )

    small_ref[...] = jnp.zeros_like(small_ref)
    loads[0].wait()
    loads[1].wait()
    small_ref[1:2, 0:PART] = gain_ref[...].astype(F32).reshape(1, PART)
    for c in range(CH):
        xall[c, m, 0:PART] = x_ref[:, c * L : (c + 1) * L]
        xall[c, m, PART:XROWS] = jnp.broadcast_to(small_ref[1:2, 0:L], (XROWS - PART, L)).astype(BF16)

    pl.semaphore_wait(barrier, MP - 1 + 2 * (GROUP - 1))

    def block(c, member):
        return xall.at[c, member]

    def hand_on(c, owner, member, kind):
        to_member(member, block(c, owner), block(c, owner), x_send.at[c], x_recv.at[c, kind]).start()

    def expect(c, kind):
        to_member(across, block(c, m), block(c, m), x_send.at[c], x_recv.at[c, kind]).wait_recv()

    def hand_own(c, k):
        hand_on(c, m, across, 2)
        hand_on(c, m, ahead, 0)
        hand_on(c, m, behind, 1)
        return k

    lax.fori_loop(0, CH, hand_own, 0)

    for load in loads[2:8]:
        load.wait()
    small_ref[0:1, 0:FF] = b1_ref[...].astype(F32).reshape(1, FF)
    small_ref[2:3, 0:PART] = b2_ref[...].astype(F32).reshape(1, PART)
    diagonal = iota((IMG, IMG), 0) == iota((IMG, IMG), 1)
    caption_row = caption_ref[...]
    caption_high = jnp.right_shift(caption_row, 5)
    caption_low = jnp.bitwise_and(caption_row, 31)

    def as_column(row):
        return jnp.sum(jnp.where(diagonal, row.astype(F32), 0.0), axis=1, keepdims=True)

    text_own_f = jnp.concatenate([text_ref[...].astype(F32), jnp.zeros((IMG, 256 - PART), F32)], axis=1)
    tbuf[a] = text_own_f.astype(BF16)

    def send_text(i, k):
        peer = lax.rem(a + i, GROUP) * GROUP + b
        to_dp(peer, tbuf.at[a], tbuf.at[a], t_send.at[0], t_recv.at[0]).start()
        return k


    def onward(c):
        return lax.rem(ring + 1 + 2 * c, 4) * 2 + side

    def backward(c):
        return lax.rem(ring + 3 + 2 * c, 4) * 2 + side

    def hand_first(c, k):
        expect(c, c)
        hand_on(c, backward(c), onward(c), 5)
        expect(c, 2)
        hand_on(c, across, ahead, 3)
        hand_on(c, across, behind, 4)
        return k

    def hand_last(c, k):
        expect(c, 5)
        hand_on(c, far, across, 6)
        return k

    lax.fori_loop(1, GROUP, send_text, 0, unroll=True)

    lax.fori_loop(0, CH, hand_first, 0)

    loads[8].wait()
    loads[9].wait()

    def turn(n, k):
        lines = pl.ds(pl.multiple_of(n * 128, 128), 128)
        w2t[lines, 0:512] = jnp.transpose(w2[0:512, lines])
        last = jnp.concatenate([w2[512:FF, lines].astype(F32), jnp.zeros((FFP - FF, 128), F32)], axis=0)
        w2t[lines, 512:FFP] = jnp.transpose(last).astype(BF16)
        return k

    lax.fori_loop(0, FULL // 128, turn, 0)
    lax.fori_loop(0, CH, hand_last, 0)

    first_row = jnp.where(iota((16, 128), 0) == 0, 1.0, 0.0).astype(BF16)
    b1_row = jnp.broadcast_to(small_ref[0:1, :], (16, FFP))
    b1_b[...] = tn(b1_row.astype(BF16), first_row)
    b2_row = jnp.broadcast_to(small_ref[2:3, 0:256], (16, 256)).astype(BF16)
    b2_b[...] = tn(b2_row, first_row)[0:PART]
    hid[...] = jnp.zeros_like(hid)

    targets = target_ref[...]
    named = iota((DP, ROWS), 0) == targets
    named_b = jnp.where(named, 1.0, 0.0).astype(BF16)

    def build_earlier(n, k):
        lines = pl.ds(pl.multiple_of(n * 128, 128), 128)
        earlier[lines, :] = jnp.where(iota((128, ROWS), 0) + n * 128 < iota((128, ROWS), 1), 1.0, 0.0).astype(BF16)
        return k

    lax.fori_loop(0, ROWS // 128, build_earlier, 0)
    before = nn(named_b, earlier[...])
    rank = jnp.sum(jnp.where(named, before, 0.0), axis=0, keepdims=True).astype(I32)
    code = targets * 16 + rank

    def pass_on(c, value, member, kind):
        part_out[c, kind] = value.astype(BF16)
        to_member(member, part_out.at[c, kind], part_in.at[c, kind], p_send.at[c], p_recv.at[c, kind]).start()

    def arrived_sum(c, kind):
        to_member(across, part_in.at[c, kind], part_in.at[c, kind], p_send.at[c], p_recv.at[c, kind]).wait_recv()
        return part_in[c, kind].astype(F32)

    def second_sums(c):
        pass_on(c, shares[c, far] + arrived_sum(c, 0), onward(c), 3)
        pass_on(c, shares[c, across] + arrived_sum(c, 1) + arrived_sum(c, 2), across, 6)

    def third_sums(c):
        pass_on(c, shares[c, onward(c)] + arrived_sum(c, 3), onward(c), 4 + c)

    def chunk(c, k):
        for kind in (1 - c, 3, 4, 6):
            expect(c, kind)

        @pl.when(c == 0)
        def _():
            def gains(n, k):
                lines = pl.ds(pl.multiple_of(n * PART, 16), PART)
                gain_b[lines, :] = tn(xall[0, n, PART:XROWS], first_row)[0:PART]
                return k

            lax.fori_loop(0, MP, gains, 0)

        def rows(n):
            return xall[c, n, 0:PART].astype(F32)

        def add_rows(n, total):
            return total + jnp.sum(rows(n), axis=0, keepdims=True)

        mean = lax.fori_loop(0, MP, add_rows, jnp.zeros((1, L), F32)) * (1.0 / FULL)

        def add_squares(n, total):
            centre = rows(n) - mean
            return total + jnp.sum(centre * centre, axis=0, keepdims=True)

        spread = lax.fori_loop(0, MP, add_squares, jnp.zeros((1, L), F32)) * (1.0 / FULL)
        inverse = lax.rsqrt(spread + 1e-06)

        def norm_rows(n, k):
            lines = pl.ds(pl.multiple_of(n * PART, 16), PART)
            normed[lines, :] = ((rows(n) - mean) * inverse * wide(gain_b[lines, :])).astype(BF16)
            return k

        lax.fori_loop(0, MP, norm_rows, 0)
        pre = nn(w1[...], normed[...]) + wide(b1_b[0:FF, :])
        hid[c, 0:FF, :] = gelu(pre).astype(BF16)

        def share(n, k):
            member = lax.rem(ring + 2 + 3 * n, 4) * 2 + lax.rem(side + 1 + n // 4, 2)
            lines = pl.ds(pl.multiple_of(member * PART, 16), PART)
            shares[c, member] = nn(w2t[lines, :], hid[c])
            return k

        lax.fori_loop(0, MP, share, 0)
        pass_on(c, shares[c, far_across], across, 0)
        pass_on(c, shares[c, ahead_across], ahead, 1)
        pass_on(c, shares[c, behind_across], behind, 2)
        pass_on(c, shares[c, backward(c)], backward(c), 5 - c)
        return k

    lax.fori_loop(0, CH, chunk, 0)
    second_sums(0)

    member_f = jnp.where(iota((IMG, ROWS), 0) == owner_ref[...], 1.0, 0.0)
    member = member_f.astype(BF16)
    sums = nt(member[:, 0:L], hid[0]) + nt(member[:, L:ROWS], hid[1])
    high = sums.astype(BF16)
    low = (sums - high.astype(F32)).astype(BF16)
    lone = gelu(b1_row).astype(BF16)
    mixed = jnp.concatenate([high, low, lone], axis=0)

    def pool_block(i, k):
        there = lax.rem(m + i, MP)
        lines = pl.ds(pl.multiple_of(there * PART, 16), PART)
        got = nt(mixed, w2t[lines, :])
        pool_out[there, 0:16, 0:PART] = got[0:16] + got[16:32]
        pool_out[there, 16:24, 0:PART] = got[32:40]
        return k

    pool_out[...] = jnp.zeros_like(pool_out)
    lax.fori_loop(0, MP, pool_block, 0)

    def send_pool(i, k):
        there = lax.rem(m + i, MP)
        to_mp(i, pool_out.at[there], pool_in.at[m], pool_send.at[0], pool_recv.at[0]).start()
        return k

    lax.fori_loop(1, MP, send_pool, 0, unroll=True)
    pool_in[m] = pool_out[m]

    second_sums(1)
    third_sums(0)

    some = pool_in.at[pl.ds(0, MP - 1)]
    to_mp(1, some, some, pool_send.at[0], pool_recv.at[0]).wait_recv()
    pooled = pool_in[0]
    for k in range(1, MP):
        pooled = pooled + pool_in[k]
    b2_wide = jnp.where(iota((1, 256), 1) < PART, small_ref[2:3, 0:256], 0.0)
    counts = jnp.sum(member_f, axis=1, keepdims=True)
    own_sum = nt(member, x_ref[...])
    own_sum = jnp.concatenate([own_sum, jnp.zeros((IMG, 256 - PART), F32)], axis=1)
    image_own = (pooled[0:16] + own_sum) / counts + b2_wide
    empty = (pooled[16:17] + b2_wide).astype(BF16)
    lane = iota((IMG, 256), 1)
    image_note = jnp.where(lane == PART, as_column(caption_high), jnp.where(lane == PART + 1, as_column(caption_low), image_own))
    ibuf[b] = image_note.astype(BF16)

    some = tbuf.at[pl.ds(0, GROUP - 1)]
    to_dp(neighbour, some, some, t_send.at[0], t_recv.at[0]).wait_recv()

    def send_image(i, k):
        peer = a * GROUP + lax.rem(b + i, GROUP)
        to_dp(peer, ibuf.at[b], ibuf.at[b], i_send.at[0], i_recv.at[0]).start()
        return k

    lax.fori_loop(1, GROUP, send_image, 0, unroll=True)

    third_sums(1)

    def build_pick(b, k):
        row = iota((128, 1), 0) + b * 128
        slot = jnp.bitwise_and(row, 15)
        base = row - slot
        is_head = slot < CAP
        is_tail = jnp.logical_and(slot >= CAP, slot < CAP + CAP // 2)
        even = base + 2 * (slot - CAP)
        lines = pl.ds(pl.multiple_of(b * 128, 128), 128)
        lane = iota((128, 128), 1)
        main = jnp.where(jnp.where(is_head, row, jnp.where(is_tail, even, -1)) == code, 1.0, 0.0)
        odd = jnp.where(jnp.where(is_tail, even + 1, -1) == code, 1.0, 0.0)
        pick[0, lines, :] = main.astype(BF16)
        pick[1, lines, :] = odd.astype(BF16)
        lack = 1.0 - jnp.sum(main, axis=1, keepdims=True)
        lack_odd = 1.0 - jnp.sum(odd, axis=1, keepdims=True)
        lacks = jnp.where(
            lane == 0,
            jnp.where(is_head, lack, 0.0),
            jnp.where(lane == 1, jnp.where(is_tail, lack, 0.0), jnp.where(lane == 2, jnp.where(is_tail, lack_odd, 0.0), 0.0)),
        )
        empty_pick[lines, :] = lacks.astype(BF16)
        column = iota((128, SLOTS), 1)
        first = jnp.right_shift(row, 4) * CAP
        even_at = first + 2 * (slot - CAP)
        main_at = jnp.where(is_head, first + slot, jnp.where(is_tail, even_at, -1))
        odd_at = jnp.where(is_tail, even_at + 1, -1)
        sel[0, lines, :] = jnp.where(main_at == column, 1.0, 0.0).astype(BF16)
        sel[1, lines, :] = jnp.where(odd_at == column, 1.0, 0.0).astype(BF16)
        return k

    lax.fori_loop(0, DP * 16 // 128, build_pick, 0)


    some = ibuf.at[pl.ds(0, GROUP - 1)]
    to_dp(neighbour, some, some, i_send.at[0], i_recv.at[0]).wait_recv()
    dots = nt(ibuf[...].reshape(SIDE, 256), tbuf[...].reshape(SIDE, 256))
    feature = iota((1, 256), 1) < PART
    image_f = jnp.where(feature, ibuf[...].reshape(SIDE, 256).astype(F32), 0.0)
    image_sq = jnp.sum(image_f * image_f, axis=1, keepdims=True)
    image_sq = jnp.where(iota((SIDE, SIDE), 1) == 0, image_sq, 0.0)
    text_f = tbuf[...].reshape(SIDE, 256).astype(F32)
    text_f = text_f * text_f
    top = text_f.astype(BF16)
    rest = (text_f - top.astype(F32)).astype(BF16)
    ones = jnp.ones((16, 256), BF16)
    text_sq = (nt(ones, top) + nt(ones, rest))[0:8]
    for k in range(MP):
        pair_out[k, 0:16] = dots[k * IMG : (k + 1) * IMG]
        pair_out[k, 16:32] = image_sq[k * IMG : (k + 1) * IMG]
        pair_out[k, 32:40] = text_sq

    def send_pair(i, k):
        there = lax.rem(m + i, MP)
        to_mp(i, pair_out.at[there], pair_in.at[m], pair_send.at[0], pair_recv.at[0]).start()
        return k

    lax.fori_loop(1, MP, send_pair, 0, unroll=True)
    pair_in[m] = pair_out[m]


    def finish(c, k):
        total = shares[c, m] + arrived_sum(c, 4) + arrived_sum(c, 5) + arrived_sum(c, 6)
        encoded = xall[c, m, 0:PART].astype(F32) + total + wide(b2_b[...])
        by_row = jnp.transpose(jnp.concatenate([encoded, jnp.zeros((256 - PART, L), F32)], axis=0))
        lines = pl.ds(pl.multiple_of(c * L, 128), L)
        rows_out[lines, 0:256] = by_row.astype(BF16)
        rows_out[lines, 256:384] = pltpu.roll(by_row[:, 128:256], 16, 1).astype(BF16)
        return k

    lax.fori_loop(0, CH, finish, 0)
    empty_f = jnp.broadcast_to(empty.astype(F32), (128, 256))
    line = iota((128, 128), 0)
    empty_tail = empty_f[:, 128:256]
    empties = jnp.where(
        line == 0,
        empty_f[:, 0:128],
        jnp.where(line == 1, empty_tail, jnp.where(line == 2, pltpu.roll(empty_tail, 16, 1), 0.0)),
    ).astype(BF16)
    head_row = jnp.bitwise_and(iota((256, 1), 0), 15) < CAP

    def send_slot(peer):
        to_dp(peer, slot_out.at[peer], slot_in.at[s], slot_send.at[0], slot_recv.at[0]).start()

    def fill(i, k):
        block = lax.rem(s // 16 + i, DP // 16)
        lines = pl.ds(pl.multiple_of(block * 256, 256), 256)
        main = nn(pick[0, lines, :], rows_out[:, 0:256])
        odd = nn(pick[1, lines, :], rows_out[:, 256:384])
        got = jnp.where(head_row, main[:, 0:128], main[:, 128:256] + odd) + nn(empty_pick[lines, :], empties)
        slot_out[pl.ds(block * 16, 16)] = got.astype(BF16).reshape(16, 16, 128)
        for j in range(1, 16):
            send_slot(block * 16 + lax.rem(s + j, 16))
        return k

    lax.fori_loop(1, DP // 16 + 1, fill, 0)
    for i in range(1, DP // 16):
        send_slot(lax.rem(s + 16 * i, DP))
    slot_in[s] = slot_out[s]

    some = pair_in.at[pl.ds(0, MP - 1)]
    to_mp(1, some, some, pair_send.at[0], pair_recv.at[0]).wait_recv()
    total = pair_in[0]
    for k in range(1, MP):
        total = total + pair_in[k]
    image_scale = lax.rsqrt(total[16:32, 0:1] + 1e-06)
    text_scale = lax.rsqrt(total[32:33] + 1e-06)
    place = iota((1, SIDE), 1)
    text_name = (jnp.right_shift(place, 4) * (GROUP * IMG) + b * IMG + jnp.bitwise_and(place, 15)).astype(F32)
    noted = ibuf[m].astype(F32)
    caption = noted[:, PART : PART + 1] * 32.0 + noted[:, PART + 1 : PART + 2]
    logits = LOGIT_SCALE * (total[0:16] * image_scale * text_scale) + LOGIT_BIAS
    coef = 1.0 / (1.0 + jnp.exp(-logits)) - jnp.where(caption == text_name, 1.0, 0.0)
    coef_in[m] = jnp.concatenate([coef * text_scale, coef * image_scale], axis=0).astype(BF16)

    def send_coef(i, k):
        to_mp(i, coef_in.at[m], coef_in.at[m], coef_send.at[0], coef_recv.at[0]).start()
        return k

    lax.fori_loop(1, MP, send_coef, 0, unroll=True)
    some = coef_in.at[pl.ds(0, MP - 1)]
    to_mp(1, some, some, coef_send.at[0], coef_recv.at[0]).wait_recv()

    for_images = jnp.concatenate([coef_in[k, 0:16] for k in range(MP)], axis=0)
    for_texts = jnp.concatenate([coef_in[k, 16:32] for k in range(MP)], axis=0)
    part = LOGIT_SCALE * nn(for_images, tbuf[...].reshape(SIDE, 256))
    grad_out[0] = part.astype(BF16).reshape(GROUP, IMG, 256)
    part = LOGIT_SCALE * tn(for_texts, ibuf[...].reshape(SIDE, 256))
    grad_out[1] = part.astype(BF16).reshape(GROUP, IMG, 256)

    def send_grad(i, k):
        there = lax.rem(b + i, GROUP)
        to_dp(a * GROUP + there, grad_out.at[0, there], grad_in.at[0, b], grad_send.at[0], grad_recv.at[0]).start()
        there = lax.rem(a + i, GROUP)
        to_dp(there * GROUP + b, grad_out.at[1, there], grad_in.at[1, a], grad_send.at[1], grad_recv.at[1]).start()
        return k

    lax.fori_loop(1, GROUP, send_grad, 0, unroll=True)
    grad_in[0, b] = grad_out[0, b]
    grad_in[1, a] = grad_out[1, a]

    some = slot_in.at[pl.ds(0, DP - 1)]
    to_dp(neighbour, some, some, slot_send.at[0], slot_recv.at[0]).wait_recv()
    arrived = jnp.transpose(slot_in[...].reshape(DP * 16, 128))
    head_lane = jnp.bitwise_and(iota((1, DP * 16), 1), 15) < CAP
    nothing = jnp.zeros((16, DP * 16), BF16)
    main = jnp.concatenate([jnp.where(head_lane, arrived, 0), jnp.where(head_lane, nothing, arrived[0:16])], axis=0)
    odd = jnp.where(head_lane, nothing, arrived[16:32])
    placed = nn(main, sel[0])
    packed_ref[0:128, :] = placed[0:128].astype(BF16)
    packed_ref[128:PART, :] = (placed[128:PART] + nn(odd, sel[1])).astype(BF16)

    for n, result in enumerate((image_grad_ref, text_grad_ref)):
        some = grad_in.at[n, pl.ds(0, GROUP - 1)]
        to_dp(neighbour, some, some, grad_send.at[n], grad_recv.at[n]).wait_recv()
        sums = grad_in[n, 0].astype(F32)
        for k in range(1, GROUP):
            sums = sums + grad_in[n, k].astype(F32)
        result[...] = sums[:, 0:PART]

    for c in range(CH):
        some = xall.at[c, pl.ds(0, MP - 1)]
        to_mp(1, some, some, x_send.at[c], x_recv.at[c, 0]).wait_send()
        some = part_out.at[c, pl.ds(0, MP - 1)]
        to_mp(1, some, some, p_send.at[c], p_recv.at[c, 0]).wait_send()
    some = pool_out.at[pl.ds(0, MP - 1)]
    to_mp(1, some, some, pool_send.at[0], pool_recv.at[0]).wait_send()
    some = pair_out.at[pl.ds(0, MP - 1)]
    to_mp(1, some, some, pair_send.at[0], pair_recv.at[0]).wait_send()
    some = coef_in.at[pl.ds(0, MP - 1)]
    to_mp(1, some, some, coef_send.at[0], coef_recv.at[0]).wait_send()
    for buf, send, recv in (
        (tbuf, t_send.at[0], t_recv.at[0]),
        (ibuf, i_send.at[0], i_recv.at[0]),
        (grad_out.at[0], grad_send.at[0], grad_recv.at[0]),
        (grad_out.at[1], grad_send.at[1], grad_recv.at[1]),
    ):
        some = buf.at[pl.ds(0, GROUP - 1)]
        to_dp(neighbour, some, some, send, recv).wait_send()
    some = slot_out.at[pl.ds(0, DP - 1)]
    to_dp(neighbour, some, some, slot_send.at[0], slot_recv.at[0]).wait_send()


def hand_over(packed_in, image_in, text_in, packed_out, image_out, text_out):
    packed_out[...] = packed_in[...]
    image_out[...] = image_in[...]
    text_out[...] = text_in[...]


def shards(patches, patch_shard, patch_image, caption_of, text_embed, ln_gain, fc1_weight, fc1_bias, fc2_weight, fc2_bias):
    vmem = pl.BlockSpec(memory_space=pltpu.VMEM)
    hbm = pl.BlockSpec(memory_space=pltpu.HBM)
    dma = pltpu.SemaphoreType.DMA
    shapes = (
        jax.ShapeDtypeStruct((PART, SLOTS), BF16),
        jax.ShapeDtypeStruct((IMG, PART), F32),
        jax.ShapeDtypeStruct((IMG, PART), F32),
    )
    results = pl.pallas_call(
        kernel,
        out_shape=shapes,
        in_specs=[hbm] * 10,
        out_specs=(vmem, vmem, vmem),
        scratch_shapes=[
            pltpu.VMEM((PART, ROWS), BF16),
            pltpu.VMEM((IMG, PART), BF16),
            pltpu.VMEM((1, ROWS), I32),
            pltpu.VMEM((1, ROWS), I32),
            pltpu.VMEM((1, IMG), I32),
            pltpu.VMEM((PART,), BF16),
            pltpu.VMEM((FF,), BF16),
            pltpu.VMEM((PART,), BF16),
            pltpu.VMEM((FF, FULL), BF16),
            pltpu.VMEM((FF, FULL), BF16),
            pltpu.VMEM((8, FFP), F32),
            pltpu.VMEM((FULL, FFP), BF16),
            pltpu.VMEM((CH, MP, XROWS, L), BF16),
            pltpu.VMEM((FULL, 128), F32),
            pltpu.VMEM((FFP, 128), F32),
            pltpu.VMEM((PART, 128), F32),
            pltpu.VMEM((FULL, L), BF16),
            pltpu.VMEM((CH, FFP, L), BF16),
            pltpu.VMEM((CH, MP, PART, L), F32),
            pltpu.VMEM((CH, 7, PART, L), BF16),
            pltpu.VMEM((CH, 7, PART, L), BF16),
            pltpu.VMEM((MP, 24, 256), F32),
            pltpu.VMEM((MP, 24, 256), F32),
            pltpu.VMEM((GROUP, IMG, 256), BF16),
            pltpu.VMEM((GROUP, IMG, 256), BF16),
            pltpu.VMEM((MP, 40, SIDE), F32),
            pltpu.VMEM((MP, 40, SIDE), F32),
            pltpu.VMEM((MP, 32, SIDE), BF16),
            pltpu.VMEM((2, GROUP, IMG, 256), BF16),
            pltpu.VMEM((2, GROUP, IMG, 256), BF16),
            pltpu.VMEM((ROWS, ROWS), BF16),
            pltpu.VMEM((2, DP * 16, ROWS), BF16),
            pltpu.VMEM((DP * 16, 128), BF16),
            pltpu.VMEM((2, DP * 16, SLOTS), BF16),
            pltpu.VMEM((ROWS, 384), BF16),
            pltpu.VMEM((DP, 16, 128), BF16),
            pltpu.VMEM((DP, 16, 128), BF16),
            dma((10,)),
            dma((CH,)), dma((CH, 7)),
            dma((1,)), dma((1,)),
            dma((CH,)), dma((CH, 7)),
            dma((1,)), dma((1,)),
            dma((1,)), dma((1,)),
            dma((1,)), dma((1,)),
            dma((1,)), dma((1,)),
            dma((2,)), dma((2,)),
            dma((1,)), dma((1,)),
        ],
        compiler_params=pltpu.CompilerParams(
            collective_id=0, has_side_effects=True, vmem_limit_bytes=60 * 1024 * 1024
        ),
    )(
        patches.T, text_embed, patch_shard.reshape(1, ROWS), patch_image, caption_of.reshape(1, IMG),
        ln_gain, fc1_bias, fc2_bias, fc1_weight.T, fc2_weight,
    )
    packed, image_grad, text_grad = pl.pallas_call(
        hand_over,
        out_shape=shapes,
        in_specs=[vmem] * 3,
        out_specs=(vmem,) * 3,
        compiler_params=pltpu.CompilerParams(vmem_limit_bytes=60 * 1024 * 1024),
    )(*results)
    return packed.T[None], image_grad, text_grad


def solution(mesh):
    return jax.shard_map(
        shards,
        mesh=mesh,
        in_specs=(
            P("dp", "mp"),
            P("dp", None),
            P("dp", None),
            P("dp"),
            P("dp", "mp"),
            P("mp"),
            P(None, "mp"),
            P("mp"),
            P("mp", None),
            P("mp"),
        ),
        out_specs=(P("dp", None, "mp"), P("dp", "mp"), P("dp", "mp")),
        check_vma=False,
    )
```

```python
import functools

import jax
import jax.numpy as jnp
from jax import lax
from jax.experimental import pallas as pl
from jax.experimental.pallas import tpu as pltpu
from jax.sharding import PartitionSpec as P

LOGIT_SCALE = 10.0
LOGIT_BIAS = -2.0
F32 = jnp.float32
BF16 = jnp.bfloat16
I32 = jnp.int32
MESH = pl.DeviceIdType.MESH

DP, MP = 64, 8
GROUP = 8
ROWS, PART, FULL = 512, 144, 1152
FF, FFP = 538, 640
IMG, CAP = 16, 10
SLOTS = DP * CAP
CH = 2
L = ROWS // CH
SIDE = GROUP * IMG
XROWS = PART + 16


def nn(a, b):
    return jnp.dot(a, b, preferred_element_type=F32)


def nt(a, b):
    return lax.dot_general(a, b, (((1,), (1,)), ((), ())), preferred_element_type=F32)


def tn(a, b):
    return lax.dot_general(a, b, (((0,), (0,)), ((), ())), preferred_element_type=F32)


def iota(shape, axis):
    return lax.broadcasted_iota(I32, shape, axis)


def gelu(h):
    return 0.5 * h * (1.0 + jnp.tanh(0.7978845608028654 * (h + 0.044715 * (h * h * h))))


def wide(column_block):
    return jnp.concatenate([column_block] * (L // 128), axis=1)


def kernel(
    x_hbm, text_hbm, target_hbm, owner_hbm, caption_hbm, gain_hbm, b1_hbm, b2_hbm, w1_hbm, w2_hbm,
    packed_ref, image_grad_ref, text_grad_ref,
    x_ref, text_ref, target_ref, owner_ref, caption_ref, gain_ref, b1_ref, b2_ref, w1, w2,
    small_ref, w2t, xall, gain_b, b1_b, b2_b, hid, part_out, part_in,
    pool_out, pool_in, tbuf, ibuf, pair_out, pair_in, grad_out, grad_in,
    pick, empty_pick, sel, rows_out, slot_out, slot_in,
    load_sem, x_send, x_recv, t_send, t_recv, p_send, p_recv,
    pool_send, pool_recv, i_send, i_recv, pair_send, pair_recv,
    grad_send, grad_recv, slot_send, slot_recv,
):
    s = lax.axis_index("dp")
    m = lax.axis_index("mp")
    a = s // GROUP
    b = lax.rem(s, GROUP)
    neighbour = lax.rem(s + 1, DP)

    ring, side = m // 2, lax.rem(m, 2)
    ahead = lax.rem(ring + 1, 4) * 2 + side
    behind = lax.rem(ring + 3, 4) * 2 + side
    far = lax.rem(ring + 2, 4) * 2 + side
    across = ring * 2 + 1 - side
    ahead_across = lax.rem(ring + 1, 4) * 2 + 1 - side
    behind_across = lax.rem(ring + 3, 4) * 2 + 1 - side
    far_across = lax.rem(ring + 2, 4) * 2 + 1 - side

    loads = [
        pltpu.make_async_copy(src, dst, load_sem.at[n])
        for n, (src, dst) in enumerate(
            (
                (x_hbm, x_ref), (gain_hbm, gain_ref), (text_hbm, text_ref), (caption_hbm, caption_ref),
                (target_hbm, target_ref), (owner_hbm, owner_ref), (b1_hbm, b1_ref), (b2_hbm, b2_ref),
                (w1_hbm, w1), (w2_hbm, w2),
            )
        )
    ]
    for load in loads:
        load.start()

    barrier = pltpu.get_barrier_semaphore()

    def greet_mp(i, c):
        pl.semaphore_signal(barrier, inc=1, device_id=(s, lax.rem(m + i, MP)), device_id_type=MESH)
        return c

    def greet_dp(i, c):
        images = a * GROUP + lax.rem(b + i, GROUP)
        texts = lax.rem(a + i, GROUP) * GROUP + b
        pl.semaphore_signal(barrier, inc=1, device_id=(images, m), device_id_type=MESH)
        pl.semaphore_signal(barrier, inc=1, device_id=(texts, m), device_id_type=MESH)
        return c

    lax.fori_loop(1, MP, greet_mp, 0, unroll=True)
    lax.fori_loop(1, GROUP, greet_dp, 0, unroll=True)

    def to_member(member, src, dst, send, recv):
        return pltpu.make_async_remote_copy(
            src_ref=src, dst_ref=dst, send_sem=send, recv_sem=recv,
            device_id=(s, member), device_id_type=MESH,
        )

    def to_mp(i, src, dst, send, recv):
        return to_member(lax.rem(m + i, MP), src, dst, send, recv)

    def to_dp(peer, src, dst, send, recv):
        return pltpu.make_async_remote_copy(
            src_ref=src, dst_ref=dst, send_sem=send, recv_sem=recv,
            device_id=(peer, m), device_id_type=MESH,
        )

    small_ref[...] = jnp.zeros_like(small_ref)
    loads[0].wait()
    loads[1].wait()
    small_ref[1:2, 0:PART] = gain_ref[...].astype(F32).reshape(1, PART)
    for c in range(CH):
        xall[c, m, 0:PART] = x_ref[:, c * L : (c + 1) * L]
    xall[0, m, PART:XROWS] = jnp.broadcast_to(small_ref[1:2, 0:L], (XROWS - PART, L)).astype(BF16)

    pl.semaphore_wait(barrier, MP - 1 + 2 * (GROUP - 1))

    def block(c, member):
        return xall.at[c, member, pl.ds(0, XROWS if c == 0 else PART)]

    def hand_on(c, owner, member, kind):
        to_member(member, block(c, owner), block(c, owner), x_send.at[c], x_recv.at[c, kind]).start()

    def expect(c, kind):
        to_member(across, block(c, m), block(c, m), x_send.at[c], x_recv.at[c, kind]).wait_recv()

    for c in range(CH):
        hand_on(c, m, across, 2)
        hand_on(c, m, ahead, 0)
        hand_on(c, m, behind, 1)

    for load in loads[2:8]:
        load.wait()
    small_ref[0:1, 0:FF] = b1_ref[...].astype(F32).reshape(1, FF)
    small_ref[2:3, 0:PART] = b2_ref[...].astype(F32).reshape(1, PART)
    diagonal = iota((IMG, IMG), 0) == iota((IMG, IMG), 1)
    caption_row = caption_ref[...]
    caption_high = jnp.right_shift(caption_row, 5)
    caption_low = jnp.bitwise_and(caption_row, 31)

    def as_column(row):
        return jnp.sum(jnp.where(diagonal, row.astype(F32), 0.0), axis=1, keepdims=True)

    text_own_f = jnp.concatenate([text_ref[...].astype(F32), jnp.zeros((IMG, 256 - PART), F32)], axis=1)
    tbuf[a] = text_own_f.astype(BF16)

    def send_text(i, k):
        peer = lax.rem(a + i, GROUP) * GROUP + b
        to_dp(peer, tbuf.at[a], tbuf.at[a], t_send.at[0], t_recv.at[0]).start()
        return k


    for c in range(CH):
        if c == 0:
            expect(c, 0)
            hand_on(c, behind, ahead, 5)
        else:
            expect(c, 1)
            hand_on(c, ahead, behind, 5)
        expect(c, 2)
        hand_on(c, across, ahead, 3)
        hand_on(c, across, behind, 4)

    lax.fori_loop(1, GROUP, send_text, 0, unroll=True)

    targets = target_ref[...]
    named = iota((DP, ROWS), 0) == targets
    named_b = jnp.where(named, 1.0, 0.0).astype(BF16)
    earlier = jnp.where(iota((ROWS, ROWS), 0) < iota((ROWS, ROWS), 1), 1.0, 0.0).astype(BF16)
    before = nn(named_b, earlier)
    rank = jnp.sum(jnp.where(named, before, 0.0), axis=0, keepdims=True).astype(I32)
    code = targets * 16 + rank

    first_row = jnp.where(iota((16, 128), 0) == 0, 1.0, 0.0).astype(BF16)
    b1_row = jnp.broadcast_to(small_ref[0:1, :], (16, FFP))
    b1_b[...] = tn(b1_row.astype(BF16), first_row)
    b2_row = jnp.broadcast_to(small_ref[2:3, 0:256], (16, 256)).astype(BF16)
    b2_b[...] = tn(b2_row, first_row)[0:PART]
    hid[...] = jnp.zeros_like(hid)
    for c in range(CH):
        expect(c, 5)
        hand_on(c, far, across, 6)

    def build_pick(b, k):
        row = iota((128, 1), 0) + b * 128
        slot = jnp.bitwise_and(row, 15)
        base = row - slot
        is_head = slot < CAP
        is_tail = jnp.logical_and(slot >= CAP, slot < CAP + CAP // 2)
        even = base + 2 * (slot - CAP)
        lines = pl.ds(pl.multiple_of(b * 128, 128), 128)
        lane = iota((128, 128), 1)
        main = jnp.where(jnp.where(is_head, row, jnp.where(is_tail, even, -1)) == code, 1.0, 0.0)
        odd = jnp.where(jnp.where(is_tail, even + 1, -1) == code, 1.0, 0.0)
        pick[0, lines, :] = main.astype(BF16)
        pick[1, lines, :] = odd.astype(BF16)
        lack = 1.0 - jnp.sum(main, axis=1, keepdims=True)
        lack_odd = 1.0 - jnp.sum(odd, axis=1, keepdims=True)
        lacks = jnp.where(
            lane == 0,
            jnp.where(is_head, lack, 0.0),
            jnp.where(lane == 1, jnp.where(is_tail, lack, 0.0), jnp.where(lane == 2, jnp.where(is_tail, lack_odd, 0.0), 0.0)),
        )
        empty_pick[lines, :] = lacks.astype(BF16)
        column = iota((128, SLOTS), 1)
        first = jnp.right_shift(row, 4) * CAP
        even_at = first + 2 * (slot - CAP)
        main_at = jnp.where(is_head, first + slot, jnp.where(is_tail, even_at, -1))
        odd_at = jnp.where(is_tail, even_at + 1, -1)
        here = jnp.logical_or(main_at == column, odd_at == column)
        sel[lines, :] = jnp.where(here, 1.0, 0.0).astype(BF16)
        return k

    lax.fori_loop(0, DP * 16 // 128, build_pick, 0)

    loads[8].wait()
    loads[9].wait()
    w2t[:, 0:512] = jnp.transpose(w2[0:512, :])
    tail_rows = jnp.concatenate([w2[512:FF, :].astype(F32), jnp.zeros((FFP - FF, FULL), F32)], axis=0)
    w2t[:, 512:FFP] = jnp.transpose(tail_rows).astype(BF16)

    def share(c, member):
        lines = pl.ds(pl.multiple_of(member * PART, 16), PART)
        return nn(w2t[lines, :], hid[:, c * L : (c + 1) * L])

    def pass_on(c, value, member, kind):
        part_out[c, kind] = value.astype(BF16)
        to_member(member, part_out.at[c, kind], part_in.at[c, kind], p_send.at[c], p_recv.at[c, kind]).start()

    def arrived_sum(c, kind):
        to_member(across, part_in.at[c, kind], part_in.at[c, kind], p_send.at[c], p_recv.at[c, kind]).wait_recv()
        return part_in[c, kind].astype(F32)

    def first_sums(c):
        pass_on(c, share(c, far_across), across, 0)
        pass_on(c, share(c, ahead_across), ahead, 1)
        pass_on(c, share(c, behind_across), behind, 2)
        if c == 0:
            pass_on(c, share(c, behind), behind, 5)
        else:
            pass_on(c, share(c, ahead), ahead, 4)

    def second_sums(c):
        pass_on(c, share(c, far) + arrived_sum(c, 0), ahead if c == 0 else behind, 3)
        pass_on(c, share(c, across) + arrived_sum(c, 1) + arrived_sum(c, 2), across, 6)

    def third_sums(c):
        if c == 0:
            pass_on(c, share(c, ahead) + arrived_sum(c, 3), ahead, 4)
        else:
            pass_on(c, share(c, behind) + arrived_sum(c, 3), behind, 5)

    for c in range(CH):
        for kind in (1 if c == 0 else 0, 3, 4, 6):
            expect(c, kind)
        if c == 0:
            for k in range(MP):
                gain_b[k * PART : (k + 1) * PART, :] = tn(xall[0, k, PART:XROWS], first_row)[0:PART]

        rows = xall[c, :, 0:PART].reshape(FULL, L).astype(F32)
        centre = rows - jnp.sum(rows, axis=0, keepdims=True) * (1.0 / FULL)
        spread = jnp.sum(centre * centre, axis=0, keepdims=True) * (1.0 / FULL)
        normed = (centre * lax.rsqrt(spread + 1e-06) * wide(gain_b[...])).astype(BF16)
        pre = nn(w1[...], normed) + wide(b1_b[0:FF, :])
        hid[0:FF, c * L : (c + 1) * L] = gelu(pre).astype(BF16)

        if c < CH - 1:
            first_sums(c)

    first_sums(CH - 1)
    member_f = jnp.where(iota((IMG, ROWS), 0) == owner_ref[...], 1.0, 0.0)
    member = member_f.astype(BF16)
    sums = nt(member, hid[...])
    high = sums.astype(BF16)
    low = (sums - high.astype(F32)).astype(BF16)
    lone = gelu(b1_row).astype(BF16)
    mixed = jnp.concatenate([high, low, lone], axis=0)

    def pool_block(i, k):
        there = lax.rem(m + i, MP)
        lines = pl.ds(pl.multiple_of(there * PART, 16), PART)
        got = nt(mixed, w2t[lines, :])
        pool_out[there, 0:16, 0:PART] = (got[0:16] + got[16:32]).astype(BF16)
        pool_out[there, 16:32, 0:PART] = got[32:48].astype(BF16)
        return k

    pool_out[...] = jnp.zeros_like(pool_out)
    lax.fori_loop(0, MP, pool_block, 0)

    def send_pool(i, k):
        there = lax.rem(m + i, MP)
        to_mp(i, pool_out.at[there], pool_in.at[m], pool_send.at[0], pool_recv.at[0]).start()
        return k

    lax.fori_loop(1, MP, send_pool, 0, unroll=True)
    pool_in[m] = pool_out[m]

    for c in range(CH):
        second_sums(c)

    some = pool_in.at[pl.ds(0, MP - 1)]
    to_mp(1, some, some, pool_send.at[0], pool_recv.at[0]).wait_recv()
    pooled = pool_in[0].astype(F32)
    for k in range(1, MP):
        pooled = pooled + pool_in[k].astype(F32)
    b2_wide = jnp.where(iota((1, 256), 1) < PART, small_ref[2:3, 0:256], 0.0)
    counts = jnp.sum(member_f, axis=1, keepdims=True)
    own_sum = nt(member, x_ref[...])
    own_sum = jnp.concatenate([own_sum, jnp.zeros((IMG, 256 - PART), F32)], axis=1)
    image_own = (pooled[0:16] + own_sum) / counts + b2_wide
    empty = (pooled[16:17] + b2_wide).astype(BF16)
    lane = iota((IMG, 256), 1)
    image_note = jnp.where(lane == PART, as_column(caption_high), jnp.where(lane == PART + 1, as_column(caption_low), image_own))
    ibuf[b] = image_note.astype(BF16)

    some = tbuf.at[pl.ds(0, GROUP - 1)]
    to_dp(neighbour, some, some, t_send.at[0], t_recv.at[0]).wait_recv()

    def send_image(i, k):
        peer = a * GROUP + lax.rem(b + i, GROUP)
        to_dp(peer, ibuf.at[b], ibuf.at[b], i_send.at[0], i_recv.at[0]).start()
        return k

    lax.fori_loop(1, GROUP, send_image, 0, unroll=True)

    for c in range(CH):
        third_sums(c)

    some = ibuf.at[pl.ds(0, GROUP - 1)]
    to_dp(neighbour, some, some, i_send.at[0], i_recv.at[0]).wait_recv()
    dots = nt(ibuf[...].reshape(SIDE, 256), tbuf[...].reshape(SIDE, 256))
    ones = jnp.where(iota((8, 256), 1) < PART, 1.0, 0.0).astype(BF16)

    def squares(block):
        value = block.astype(F32)
        return nt(ones, (value * value).astype(BF16))

    text_sq = squares(tbuf[...].reshape(SIDE, 256))
    image_sq = squares(ibuf[...].reshape(SIDE, 256))
    pair_out[0:SIDE] = dots.astype(BF16)
    pair_out[SIDE : SIDE + 16] = jnp.concatenate([text_sq, image_sq], axis=0).astype(BF16)

    def send_pair(i, k):
        to_mp(i, pair_out, pair_in.at[m], pair_send.at[0], pair_recv.at[0]).start()
        return k

    lax.fori_loop(1, MP, send_pair, 0, unroll=True)
    pair_in[m] = pair_out[...]


    encoded = []
    for c in range(CH):
        total = share(c, m) + arrived_sum(c, 4) + arrived_sum(c, 5) + arrived_sum(c, 6)
        own = x_ref[:, c * L : (c + 1) * L].astype(F32)
        encoded.append(own + total + wide(b2_b[...]))
    encoded = jnp.concatenate(encoded, axis=1)
    by_row = jnp.transpose(jnp.concatenate([encoded, jnp.zeros((256 - PART, ROWS), F32)], axis=0))
    rows_out[:, 0:256] = by_row.astype(BF16)
    rows_out[:, 256:384] = pltpu.roll(by_row[:, 128:256], 16, 1).astype(BF16)
    empty_f = jnp.broadcast_to(empty.astype(F32), (128, 256))
    line = iota((128, 128), 0)
    empty_tail = empty_f[:, 128:256]
    empties = jnp.where(
        line == 0,
        empty_f[:, 0:128],
        jnp.where(line == 1, empty_tail, jnp.where(line == 2, pltpu.roll(empty_tail, 16, 1), 0.0)),
    ).astype(BF16)
    head_row = jnp.bitwise_and(iota((256, 1), 0), 15) < CAP

    def fill(block):
        lines = pl.ds(pl.multiple_of(block * 256, 256), 256)
        main = nn(pick[0, lines, :], rows_out[:, 0:256])
        odd = nn(pick[1, lines, :], rows_out[:, 256:384])
        got = jnp.where(head_row, main[:, 0:128], main[:, 128:256] + odd) + nn(empty_pick[lines, :], empties)
        slot_out[pl.ds(block * 16, 16)] = got.astype(BF16).reshape(16, 16, 128)

    def send_slot(peer):
        to_dp(peer, slot_out.at[peer], slot_in.at[s], slot_send.at[0], slot_recv.at[0]).start()

    def fill_other(i, k):
        block = lax.rem(s // 16 + i, DP // 16)
        fill(block)
        for j in range(16):
            send_slot(block * 16 + j)
        return k

    lax.fori_loop(1, DP // 16, fill_other, 0)
    fill(s // 16)
    for j in range(1, 16):
        send_slot(s // 16 * 16 + lax.rem(s + j, 16))
    slot_in[s] = slot_out[s]

    some = pair_in.at[pl.ds(0, MP - 1)]
    to_mp(1, some, some, pair_send.at[0], pair_recv.at[0]).wait_recv()
    total = pair_in[0].astype(F32)
    for k in range(1, MP):
        total = total + pair_in[k].astype(F32)
    text_scale = lax.rsqrt(total[SIDE : SIDE + 1] + 1e-06)
    image_row = lax.rsqrt(total[SIDE + 8 : SIDE + 9] + 1e-06)
    image_scale = jnp.transpose(jnp.broadcast_to(image_row, (SIDE, SIDE)))
    place = iota((1, SIDE), 1)
    text_name = (jnp.right_shift(place, 4) * (GROUP * IMG) + b * IMG + jnp.bitwise_and(place, 15)).astype(F32)
    noted = ibuf[...].reshape(SIDE, 256)[:, 128:256].astype(F32)
    caption = noted[:, PART - 128 : PART - 127] * 32.0 + noted[:, PART - 127 : PART - 126]
    logits = LOGIT_SCALE * (total[0:SIDE] * image_scale * text_scale) + LOGIT_BIAS
    coef = 1.0 / (1.0 + jnp.exp(-logits)) - jnp.where(caption == text_name, 1.0, 0.0)
    for_images = (coef * text_scale).astype(BF16)
    for_texts = (coef * image_scale).astype(BF16)

    part = LOGIT_SCALE * nn(for_images, tbuf[...].reshape(SIDE, 256))
    grad_out[0] = part.astype(BF16).reshape(GROUP, IMG, 256)
    part = LOGIT_SCALE * tn(for_texts, ibuf[...].reshape(SIDE, 256))
    grad_out[1] = part.astype(BF16).reshape(GROUP, IMG, 256)

    def send_grad(i, k):
        there = lax.rem(b + i, GROUP)
        to_dp(a * GROUP + there, grad_out.at[0, there], grad_in.at[0, b], grad_send.at[0], grad_recv.at[0]).start()
        there = lax.rem(a + i, GROUP)
        to_dp(there * GROUP + b, grad_out.at[1, there], grad_in.at[1, a], grad_send.at[1], grad_recv.at[1]).start()
        return k

    lax.fori_loop(1, GROUP, send_grad, 0, unroll=True)
    grad_in[0, b] = grad_out[0, b]
    grad_in[1, a] = grad_out[1, a]

    some = slot_in.at[pl.ds(0, DP - 1)]
    to_dp(neighbour, some, some, slot_send.at[0], slot_recv.at[0]).wait_recv()
    arrived = jnp.transpose(slot_in[...].reshape(DP * 16, 128))
    head_lane = jnp.bitwise_and(iota((1, DP * 16), 1), 15) < CAP
    nothing = jnp.zeros((32, DP * 16), BF16)
    both = jnp.concatenate([jnp.where(head_lane, arrived, 0), jnp.where(head_lane, nothing, arrived[0:32])], axis=0)
    placed = nn(both, sel[...])
    even_slot = jnp.bitwise_and(iota((1, SLOTS), 1), 1) == 0
    packed_ref[0:128, :] = placed[0:128].astype(BF16)
    packed_ref[128:PART, :] = jnp.where(even_slot, placed[128:PART], placed[PART : PART + 16]).astype(BF16)

    for n, result in enumerate((image_grad_ref, text_grad_ref)):
        some = grad_in.at[n, pl.ds(0, GROUP - 1)]
        to_dp(neighbour, some, some, grad_send.at[n], grad_recv.at[n]).wait_recv()
        sums = grad_in[n, 0].astype(F32)
        for k in range(1, GROUP):
            sums = sums + grad_in[n, k].astype(F32)
        result[...] = sums[:, 0:PART]

    for c in range(CH):
        some = xall.at[c, pl.ds(0, MP - 1), pl.ds(0, XROWS if c == 0 else PART)]
        to_mp(1, some, some, x_send.at[c], x_recv.at[c, 0]).wait_send()
        some = part_out.at[c, pl.ds(0, MP - 1)]
        to_mp(1, some, some, p_send.at[c], p_recv.at[c, 0]).wait_send()
    some = pool_out.at[pl.ds(0, MP - 1)]
    to_mp(1, some, some, pool_send.at[0], pool_recv.at[0]).wait_send()
    some = pair_in.at[pl.ds(0, MP - 1)]
    to_mp(1, some, some, pair_send.at[0], pair_recv.at[0]).wait_send()
    for buf, send, recv in (
        (tbuf, t_send.at[0], t_recv.at[0]),
        (ibuf, i_send.at[0], i_recv.at[0]),
        (grad_out.at[0], grad_send.at[0], grad_recv.at[0]),
        (grad_out.at[1], grad_send.at[1], grad_recv.at[1]),
    ):
        some = buf.at[pl.ds(0, GROUP - 1)]
        to_dp(neighbour, some, some, send, recv).wait_send()
    some = slot_out.at[pl.ds(0, DP - 1)]
    to_dp(neighbour, some, some, slot_send.at[0], slot_recv.at[0]).wait_send()


def hand_over(packed_in, image_in, text_in, packed_out, image_out, text_out):
    packed_out[...] = packed_in[...]
    image_out[...] = image_in[...]
    text_out[...] = text_in[...]


def shards(patches, patch_shard, patch_image, caption_of, text_embed, ln_gain, fc1_weight, fc1_bias, fc2_weight, fc2_bias):
    vmem = pl.BlockSpec(memory_space=pltpu.VMEM)
    hbm = pl.BlockSpec(memory_space=pltpu.HBM)
    dma = pltpu.SemaphoreType.DMA
    shapes = (
        jax.ShapeDtypeStruct((PART, SLOTS), BF16),
        jax.ShapeDtypeStruct((IMG, PART), F32),
        jax.ShapeDtypeStruct((IMG, PART), F32),
    )
    results = pl.pallas_call(
        kernel,
        out_shape=shapes,
        in_specs=[hbm] * 10,
        out_specs=(vmem, vmem, vmem),
        scratch_shapes=[
            pltpu.VMEM((PART, ROWS), BF16),
            pltpu.VMEM((IMG, PART), BF16),
            pltpu.VMEM((1, ROWS), I32),
            pltpu.VMEM((1, ROWS), I32),
            pltpu.VMEM((1, IMG), I32),
            pltpu.VMEM((PART,), BF16),
            pltpu.VMEM((FF,), BF16),
            pltpu.VMEM((PART,), BF16),
            pltpu.VMEM((FF, FULL), BF16),
            pltpu.VMEM((FF, FULL), BF16),
            pltpu.VMEM((8, FFP), F32),
            pltpu.VMEM((FULL, FFP), BF16),
            pltpu.VMEM((CH, MP, XROWS, L), BF16),
            pltpu.VMEM((FULL, 128), F32),
            pltpu.VMEM((FFP, 128), F32),
            pltpu.VMEM((PART, 128), F32),
            pltpu.VMEM((FFP, ROWS), BF16),
            pltpu.VMEM((CH, 7, PART, L), BF16),
            pltpu.VMEM((CH, 7, PART, L), BF16),
            pltpu.VMEM((MP, 32, 256), BF16),
            pltpu.VMEM((MP, 32, 256), BF16),
            pltpu.VMEM((GROUP, IMG, 256), BF16),
            pltpu.VMEM((GROUP, IMG, 256), BF16),
            pltpu.VMEM((SIDE + 16, SIDE), BF16),
            pltpu.VMEM((MP, SIDE + 16, SIDE), BF16),
            pltpu.VMEM((2, GROUP, IMG, 256), BF16),
            pltpu.VMEM((2, GROUP, IMG, 256), BF16),
            pltpu.VMEM((2, DP * 16, ROWS), BF16),
            pltpu.VMEM((DP * 16, 128), BF16),
            pltpu.VMEM((DP * 16, SLOTS), BF16),
            pltpu.VMEM((ROWS, 384), BF16),
            pltpu.VMEM((DP, 16, 128), BF16),
            pltpu.VMEM((DP, 16, 128), BF16),
            dma((10,)),
            dma((CH,)), dma((CH, 7)),
            dma((1,)), dma((1,)),
            dma((CH,)), dma((CH, 7)),
            dma((1,)), dma((1,)),
            dma((1,)), dma((1,)),
            dma((1,)), dma((1,)),
            dma((2,)), dma((2,)),
            dma((1,)), dma((1,)),
        ],
        compiler_params=pltpu.CompilerParams(
            collective_id=0, has_side_effects=True, vmem_limit_bytes=60 * 1024 * 1024
        ),
    )(
        patches.T, text_embed, patch_shard.reshape(1, ROWS), patch_image, caption_of.reshape(1, IMG),
        ln_gain, fc1_bias, fc2_bias, fc1_weight.T, fc2_weight,
    )
    packed, image_grad, text_grad = pl.pallas_call(
        hand_over,
        out_shape=shapes,
        in_specs=[vmem] * 3,
        out_specs=(vmem,) * 3,
        compiler_params=pltpu.CompilerParams(vmem_limit_bytes=60 * 1024 * 1024),
    )(*results)
    return packed.T[None], image_grad, text_grad


def solution(mesh):
    return jax.shard_map(
        shards,
        mesh=mesh,
        in_specs=(
            P("dp", "mp"),
            P("dp", None),
            P("dp", None),
            P("dp"),
            P("dp", "mp"),
            P("mp"),
            P(None, "mp"),
            P("mp"),
            P("mp", None),
            P("mp"),
        ),
        out_specs=(P("dp", None, "mp"), P("dp", "mp"), P("dp", "mp")),
        check_vma=False,
    )
```

```python
import functools

import jax
import jax.numpy as jnp
from jax import lax
from jax.experimental import pallas as pl
from jax.experimental.pallas import tpu as pltpu
from jax.sharding import PartitionSpec as P

LOGIT_SCALE = 10.0
LOGIT_BIAS = -2.0
F32 = jnp.float32
BF16 = jnp.bfloat16
I32 = jnp.int32
MESH = pl.DeviceIdType.MESH

DP, MP = 64, 8
GROUP = 8
ROWS, PART, FULL = 512, 144, 1152
FF, FFP = 538, 640
IMG, CAP = 16, 10
SLOTS = DP * CAP
CH = 2
L = ROWS // CH
SIDE = GROUP * IMG
XROWS = PART + 16


def nn(a, b):
    return jnp.dot(a, b, preferred_element_type=F32)


def nt(a, b):
    return lax.dot_general(a, b, (((1,), (1,)), ((), ())), preferred_element_type=F32)


def tn(a, b):
    return lax.dot_general(a, b, (((0,), (0,)), ((), ())), preferred_element_type=F32)


def iota(shape, axis):
    return lax.broadcasted_iota(I32, shape, axis)


def gelu(h):
    return 0.5 * h * (1.0 + jnp.tanh(0.7978845608028654 * (h + 0.044715 * (h * h * h))))


def wide(column_block):
    return jnp.concatenate([column_block] * (L // 128), axis=1)


def kernel(
    x_hbm, text_hbm, target_hbm, owner_hbm, caption_hbm, gain_hbm, b1_hbm, b2_hbm, w1_hbm, w2_hbm,
    packed_ref, image_grad_ref, text_grad_ref,
    x_ref, text_ref, target_ref, owner_ref, caption_ref, gain_ref, b1_ref, b2_ref, w1, w2,
    small_ref, w2t, xall, gain_b, b1_b, b2_b, hid, part_out, part_in,
    pool_out, pool_in, tbuf, ibuf, pair_out, pair_in, grad_out, grad_in,
    pick, empty_pick, sel, rows_out, slot_out, slot_in,
    load_sem, x_send, x_recv, t_send, t_recv, p_send, p_recv,
    pool_send, pool_recv, i_send, i_recv, pair_send, pair_recv,
    grad_send, grad_recv, slot_send, slot_recv,
):
    s = lax.axis_index("dp")
    m = lax.axis_index("mp")
    a = s // GROUP
    b = lax.rem(s, GROUP)
    neighbour = lax.rem(s + 1, DP)

    ring, side = m // 2, lax.rem(m, 2)
    ahead = lax.rem(ring + 1, 4) * 2 + side
    behind = lax.rem(ring + 3, 4) * 2 + side
    far = lax.rem(ring + 2, 4) * 2 + side
    across = ring * 2 + 1 - side
    ahead_across = lax.rem(ring + 1, 4) * 2 + 1 - side
    behind_across = lax.rem(ring + 3, 4) * 2 + 1 - side
    far_across = lax.rem(ring + 2, 4) * 2 + 1 - side

    loads = [
        pltpu.make_async_copy(src, dst, load_sem.at[n])
        for n, (src, dst) in enumerate(
            (
                (x_hbm, x_ref), (gain_hbm, gain_ref), (text_hbm, text_ref), (caption_hbm, caption_ref),
                (target_hbm, target_ref), (owner_hbm, owner_ref), (b1_hbm, b1_ref), (b2_hbm, b2_ref),
                (w1_hbm, w1), (w2_hbm, w2),
            )
        )
    ]
    for load in loads:
        load.start()

    barrier = pltpu.get_barrier_semaphore()

    def greet_mp(i, c):
        pl.semaphore_signal(barrier, inc=1, device_id=(s, lax.rem(m + i, MP)), device_id_type=MESH)
        return c

    def greet_dp(i, c):
        images = a * GROUP + lax.rem(b + i, GROUP)
        texts = lax.rem(a + i, GROUP) * GROUP + b
        pl.semaphore_signal(barrier, inc=1, device_id=(images, m), device_id_type=MESH)
        pl.semaphore_signal(barrier, inc=1, device_id=(texts, m), device_id_type=MESH)
        return c

    lax.fori_loop(1, MP, greet_mp, 0, unroll=True)
    lax.fori_loop(1, GROUP, greet_dp, 0, unroll=True)

    def to_member(member, src, dst, send, recv):
        return pltpu.make_async_remote_copy(
            src_ref=src, dst_ref=dst, send_sem=send, recv_sem=recv,
            device_id=(s, member), device_id_type=MESH,
        )

    def to_mp(i, src, dst, send, recv):
        return to_member(lax.rem(m + i, MP), src, dst, send, recv)

    def to_dp(peer, src, dst, send, recv):
        return pltpu.make_async_remote_copy(
            src_ref=src, dst_ref=dst, send_sem=send, recv_sem=recv,
            device_id=(peer, m), device_id_type=MESH,
        )

    small_ref[...] = jnp.zeros_like(small_ref)
    loads[0].wait()
    loads[1].wait()
    small_ref[1:2, 0:PART] = gain_ref[...].astype(F32).reshape(1, PART)
    for c in range(CH):
        xall[c, m, 0:PART] = x_ref[:, c * L : (c + 1) * L]
    xall[0, m, PART:XROWS] = jnp.broadcast_to(small_ref[1:2, 0:L], (XROWS - PART, L)).astype(BF16)

    pl.semaphore_wait(barrier, MP - 1 + 2 * (GROUP - 1))

    def block(c, member):
        return xall.at[c, member, pl.ds(0, XROWS if c == 0 else PART)]

    def hand_on(c, owner, member, kind):
        to_member(member, block(c, owner), block(c, owner), x_send.at[c], x_recv.at[c, kind]).start()

    def expect(c, kind):
        to_member(across, block(c, m), block(c, m), x_send.at[c], x_recv.at[c, kind]).wait_recv()

    for c in range(CH):
        hand_on(c, m, across, 2)
        hand_on(c, m, ahead, 0)
        hand_on(c, m, behind, 1)

    for load in loads[2:8]:
        load.wait()
    small_ref[0:1, 0:FF] = b1_ref[...].astype(F32).reshape(1, FF)
    small_ref[2:3, 0:PART] = b2_ref[...].astype(F32).reshape(1, PART)
    diagonal = iota((IMG, IMG), 0) == iota((IMG, IMG), 1)
    caption_row = caption_ref[...]
    caption_high = jnp.right_shift(caption_row, 5)
    caption_low = jnp.bitwise_and(caption_row, 31)

    def as_column(row):
        return jnp.sum(jnp.where(diagonal, row.astype(F32), 0.0), axis=1, keepdims=True)

    text_own_f = jnp.concatenate([text_ref[...].astype(F32), jnp.zeros((IMG, 256 - PART), F32)], axis=1)
    tbuf[a] = text_own_f.astype(BF16)

    def send_text(i, k):
        peer = lax.rem(a + i, GROUP) * GROUP + b
        to_dp(peer, tbuf.at[a], tbuf.at[a], t_send.at[0], t_recv.at[0]).start()
        return k


    for c in range(CH):
        if c == 0:
            expect(c, 0)
            hand_on(c, behind, ahead, 5)
        else:
            expect(c, 1)
            hand_on(c, ahead, behind, 5)
        expect(c, 2)
        hand_on(c, across, ahead, 3)
        hand_on(c, across, behind, 4)

    lax.fori_loop(1, GROUP, send_text, 0, unroll=True)

    targets = target_ref[...]
    named = iota((DP, ROWS), 0) == targets
    named_b = jnp.where(named, 1.0, 0.0).astype(BF16)
    earlier = jnp.where(iota((ROWS, ROWS), 0) < iota((ROWS, ROWS), 1), 1.0, 0.0).astype(BF16)
    before = nn(named_b, earlier)
    rank = jnp.sum(jnp.where(named, before, 0.0), axis=0, keepdims=True).astype(I32)
    code = targets * 16 + rank

    first_row = jnp.where(iota((16, 128), 0) == 0, 1.0, 0.0).astype(BF16)
    b1_row = jnp.broadcast_to(small_ref[0:1, :], (16, FFP))
    b1_b[...] = tn(b1_row.astype(BF16), first_row)
    b2_row = jnp.broadcast_to(small_ref[2:3, 0:256], (16, 256)).astype(BF16)
    b2_b[...] = tn(b2_row, first_row)[0:PART]
    hid[...] = jnp.zeros_like(hid)
    for c in range(CH):
        expect(c, 5)
        hand_on(c, far, across, 6)

    def build_pick(b, k):
        row = iota((128, 1), 0) + b * 128
        slot = jnp.bitwise_and(row, 15)
        base = row - slot
        is_head = slot < CAP
        is_tail = jnp.logical_and(slot >= CAP, slot < CAP + CAP // 2)
        even = base + 2 * (slot - CAP)
        lines = pl.ds(pl.multiple_of(b * 128, 128), 128)
        lane = iota((128, 128), 1)
        main = jnp.where(jnp.where(is_head, row, jnp.where(is_tail, even, -1)) == code, 1.0, 0.0)
        odd = jnp.where(jnp.where(is_tail, even + 1, -1) == code, 1.0, 0.0)
        pick[0, lines, :] = main.astype(BF16)
        pick[1, lines, :] = odd.astype(BF16)
        lack = 1.0 - jnp.sum(main, axis=1, keepdims=True)
        lack_odd = 1.0 - jnp.sum(odd, axis=1, keepdims=True)
        lacks = jnp.where(
            lane == 0,
            jnp.where(is_head, lack, 0.0),
            jnp.where(lane == 1, jnp.where(is_tail, lack, 0.0), jnp.where(lane == 2, jnp.where(is_tail, lack_odd, 0.0), 0.0)),
        )
        empty_pick[lines, :] = lacks.astype(BF16)
        column = iota((128, SLOTS), 1)
        first = jnp.right_shift(row, 4) * CAP
        even_at = first + 2 * (slot - CAP)
        main_at = jnp.where(is_head, first + slot, jnp.where(is_tail, even_at, -1))
        odd_at = jnp.where(is_tail, even_at + 1, -1)
        here = jnp.logical_or(main_at == column, odd_at == column)
        sel[lines, :] = jnp.where(here, 1.0, 0.0).astype(BF16)
        return k

    lax.fori_loop(0, DP * 16 // 128, build_pick, 0)

    loads[8].wait()
    loads[9].wait()
    w2t[:, 0:512] = jnp.transpose(w2[0:512, :])
    tail_rows = jnp.concatenate([w2[512:FF, :].astype(F32), jnp.zeros((FFP - FF, FULL), F32)], axis=0)
    w2t[:, 512:FFP] = jnp.transpose(tail_rows).astype(BF16)

    def share(c, member):
        lines = pl.ds(pl.multiple_of(member * PART, 16), PART)
        return nn(w2t[lines, :], hid[:, c * L : (c + 1) * L])

    def pass_on(c, value, member, kind):
        part_out[c, kind] = value.astype(BF16)
        to_member(member, part_out.at[c, kind], part_in.at[c, kind], p_send.at[c], p_recv.at[c, kind]).start()

    def arrived_sum(c, kind):
        to_member(across, part_in.at[c, kind], part_in.at[c, kind], p_send.at[c], p_recv.at[c, kind]).wait_recv()
        return part_in[c, kind].astype(F32)

    def first_sums(c):
        pass_on(c, share(c, far_across), across, 0)
        pass_on(c, share(c, ahead_across), ahead, 1)
        pass_on(c, share(c, behind_across), behind, 2)
        if c == 0:
            pass_on(c, share(c, behind), behind, 5)
        else:
            pass_on(c, share(c, ahead), ahead, 4)

    def second_sums(c):
        pass_on(c, share(c, far) + arrived_sum(c, 0), ahead if c == 0 else behind, 3)
        pass_on(c, share(c, across) + arrived_sum(c, 1) + arrived_sum(c, 2), across, 6)

    def third_sums(c):
        if c == 0:
            pass_on(c, share(c, ahead) + arrived_sum(c, 3), ahead, 4)
        else:
            pass_on(c, share(c, behind) + arrived_sum(c, 3), behind, 5)

    for c in range(CH):
        for kind in (1 if c == 0 else 0, 3, 4, 6):
            expect(c, kind)
        if c == 0:
            for k in range(MP):
                gain_b[k * PART : (k + 1) * PART, :] = tn(xall[0, k, PART:XROWS], first_row)[0:PART]

        rows = xall[c, :, 0:PART].reshape(FULL, L).astype(F32)
        centre = rows - jnp.sum(rows, axis=0, keepdims=True) * (1.0 / FULL)
        spread = jnp.sum(centre * centre, axis=0, keepdims=True) * (1.0 / FULL)
        normed = (centre * lax.rsqrt(spread + 1e-06) * wide(gain_b[...])).astype(BF16)
        pre = nn(w1[...], normed) + wide(b1_b[0:FF, :])
        hid[0:FF, c * L : (c + 1) * L] = gelu(pre).astype(BF16)

        if c < CH - 1:
            first_sums(c)

    first_sums(CH - 1)
    second_sums(0)

    member_f = jnp.where(iota((IMG, ROWS), 0) == owner_ref[...], 1.0, 0.0)
    member = member_f.astype(BF16)
    sums = nt(member, hid[...])
    high = sums.astype(BF16)
    low = (sums - high.astype(F32)).astype(BF16)
    lone = gelu(b1_row).astype(BF16)
    mixed = jnp.concatenate([high, low, lone], axis=0)

    def pool_block(i, k):
        there = lax.rem(m + i, MP)
        lines = pl.ds(pl.multiple_of(there * PART, 16), PART)
        got = nt(mixed, w2t[lines, :])
        pool_out[there, 0:16, 0:PART] = (got[0:16] + got[16:32]).astype(BF16)
        pool_out[there, 16:32, 0:PART] = got[32:48].astype(BF16)
        return k

    pool_out[...] = jnp.zeros_like(pool_out)
    lax.fori_loop(0, MP, pool_block, 0)

    def send_pool(i, k):
        there = lax.rem(m + i, MP)
        to_mp(i, pool_out.at[there], pool_in.at[m], pool_send.at[0], pool_recv.at[0]).start()
        return k

    lax.fori_loop(1, MP, send_pool, 0, unroll=True)
    pool_in[m] = pool_out[m]

    second_sums(1)
    third_sums(0)

    some = pool_in.at[pl.ds(0, MP - 1)]
    to_mp(1, some, some, pool_send.at[0], pool_recv.at[0]).wait_recv()
    pooled = pool_in[0].astype(F32)
    for k in range(1, MP):
        pooled = pooled + pool_in[k].astype(F32)
    b2_wide = jnp.where(iota((1, 256), 1) < PART, small_ref[2:3, 0:256], 0.0)
    counts = jnp.sum(member_f, axis=1, keepdims=True)
    own_sum = nt(member, x_ref[...])
    own_sum = jnp.concatenate([own_sum, jnp.zeros((IMG, 256 - PART), F32)], axis=1)
    image_own = (pooled[0:16] + own_sum) / counts + b2_wide
    empty = (pooled[16:17] + b2_wide).astype(BF16)
    lane = iota((IMG, 256), 1)
    image_note = jnp.where(lane == PART, as_column(caption_high), jnp.where(lane == PART + 1, as_column(caption_low), image_own))
    ibuf[b] = image_note.astype(BF16)

    some = tbuf.at[pl.ds(0, GROUP - 1)]
    to_dp(neighbour, some, some, t_send.at[0], t_recv.at[0]).wait_recv()

    def send_image(i, k):
        peer = a * GROUP + lax.rem(b + i, GROUP)
        to_dp(peer, ibuf.at[b], ibuf.at[b], i_send.at[0], i_recv.at[0]).start()
        return k

    lax.fori_loop(1, GROUP, send_image, 0, unroll=True)

    third_sums(1)

    def finish(c):
        total = share(c, m) + arrived_sum(c, 4) + arrived_sum(c, 5) + arrived_sum(c, 6)
        encoded = x_ref[:, c * L : (c + 1) * L].astype(F32) + total + wide(b2_b[...])
        by_row = jnp.transpose(jnp.concatenate([encoded, jnp.zeros((256 - PART, L), F32)], axis=0))
        rows_out[c * L : (c + 1) * L, 0:256] = by_row.astype(BF16)
        rows_out[c * L : (c + 1) * L, 256:384] = pltpu.roll(by_row[:, 128:256], 16, 1).astype(BF16)

    finish(0)

    some = ibuf.at[pl.ds(0, GROUP - 1)]
    to_dp(neighbour, some, some, i_send.at[0], i_recv.at[0]).wait_recv()
    dots = nt(ibuf[...].reshape(SIDE, 256), tbuf[...].reshape(SIDE, 256))
    ones = jnp.where(iota((8, 256), 1) < PART, 1.0, 0.0).astype(BF16)

    def squares(block):
        value = block.astype(F32)
        return nt(ones, (value * value).astype(BF16))

    text_sq = squares(tbuf[...].reshape(SIDE, 256))
    image_sq = squares(ibuf[...].reshape(SIDE, 256))
    pair_out[0:SIDE] = dots.astype(BF16)
    pair_out[SIDE : SIDE + 16] = jnp.concatenate([text_sq, image_sq], axis=0).astype(BF16)

    def send_pair(i, k):
        to_mp(i, pair_out, pair_in.at[m], pair_send.at[0], pair_recv.at[0]).start()
        return k

    lax.fori_loop(1, MP, send_pair, 0, unroll=True)
    pair_in[m] = pair_out[...]


    finish(1)

    empty_f = jnp.broadcast_to(empty.astype(F32), (128, 256))
    line = iota((128, 128), 0)
    empty_tail = empty_f[:, 128:256]
    empties = jnp.where(
        line == 0,
        empty_f[:, 0:128],
        jnp.where(line == 1, empty_tail, jnp.where(line == 2, pltpu.roll(empty_tail, 16, 1), 0.0)),
    ).astype(BF16)
    head_row = jnp.bitwise_and(iota((256, 1), 0), 15) < CAP

    def fill(block):
        lines = pl.ds(pl.multiple_of(block * 256, 256), 256)
        main = nn(pick[0, lines, :], rows_out[:, 0:256])
        odd = nn(pick[1, lines, :], rows_out[:, 256:384])
        got = jnp.where(head_row, main[:, 0:128], main[:, 128:256] + odd) + nn(empty_pick[lines, :], empties)
        slot_out[pl.ds(block * 16, 16)] = got.astype(BF16).reshape(16, 16, 128)

    def send_slot(peer):
        to_dp(peer, slot_out.at[peer], slot_in.at[s], slot_send.at[0], slot_recv.at[0]).start()

    def fill_other(i, k):
        block = lax.rem(s // 16 + i, DP // 16)
        fill(block)
        for j in range(16):
            send_slot(block * 16 + j)
        return k

    lax.fori_loop(1, DP // 16, fill_other, 0)
    fill(s // 16)
    for j in range(1, 16):
        send_slot(s // 16 * 16 + lax.rem(s + j, 16))
    slot_in[s] = slot_out[s]

    some = pair_in.at[pl.ds(0, MP - 1)]
    to_mp(1, some, some, pair_send.at[0], pair_recv.at[0]).wait_recv()
    total = pair_in[0].astype(F32)
    for k in range(1, MP):
        total = total + pair_in[k].astype(F32)
    text_scale = lax.rsqrt(total[SIDE : SIDE + 1] + 1e-06)
    image_row = lax.rsqrt(total[SIDE + 8 : SIDE + 9] + 1e-06)
    image_scale = jnp.transpose(jnp.broadcast_to(image_row, (SIDE, SIDE)))
    place = iota((1, SIDE), 1)
    text_name = (jnp.right_shift(place, 4) * (GROUP * IMG) + b * IMG + jnp.bitwise_and(place, 15)).astype(F32)
    noted = ibuf[...].reshape(SIDE, 256)[:, 128:256].astype(F32)
    caption = noted[:, PART - 128 : PART - 127] * 32.0 + noted[:, PART - 127 : PART - 126]
    logits = LOGIT_SCALE * (total[0:SIDE] * image_scale * text_scale) + LOGIT_BIAS
    coef = 1.0 / (1.0 + jnp.exp(-logits)) - jnp.where(caption == text_name, 1.0, 0.0)
    for_images = (coef * text_scale).astype(BF16)
    for_texts = (coef * image_scale).astype(BF16)

    part = LOGIT_SCALE * nn(for_images, tbuf[...].reshape(SIDE, 256))
    grad_out[0] = part.astype(BF16).reshape(GROUP, IMG, 256)
    part = LOGIT_SCALE * tn(for_texts, ibuf[...].reshape(SIDE, 256))
    grad_out[1] = part.astype(BF16).reshape(GROUP, IMG, 256)

    def send_grad(i, k):
        there = lax.rem(b + i, GROUP)
        to_dp(a * GROUP + there, grad_out.at[0, there], grad_in.at[0, b], grad_send.at[0], grad_recv.at[0]).start()
        there = lax.rem(a + i, GROUP)
        to_dp(there * GROUP + b, grad_out.at[1, there], grad_in.at[1, a], grad_send.at[1], grad_recv.at[1]).start()
        return k

    lax.fori_loop(1, GROUP, send_grad, 0, unroll=True)
    grad_in[0, b] = grad_out[0, b]
    grad_in[1, a] = grad_out[1, a]

    some = slot_in.at[pl.ds(0, DP - 1)]
    to_dp(neighbour, some, some, slot_send.at[0], slot_recv.at[0]).wait_recv()
    arrived = jnp.transpose(slot_in[...].reshape(DP * 16, 128))
    head_lane = jnp.bitwise_and(iota((1, DP * 16), 1), 15) < CAP
    nothing = jnp.zeros((32, DP * 16), BF16)
    both = jnp.concatenate([jnp.where(head_lane, arrived, 0), jnp.where(head_lane, nothing, arrived[0:32])], axis=0)
    placed = nn(both, sel[...])
    even_slot = jnp.bitwise_and(iota((1, SLOTS), 1), 1) == 0
    packed_ref[0:128, :] = placed[0:128].astype(BF16)
    packed_ref[128:PART, :] = jnp.where(even_slot, placed[128:PART], placed[PART : PART + 16]).astype(BF16)

    for n, result in enumerate((image_grad_ref, text_grad_ref)):
        some = grad_in.at[n, pl.ds(0, GROUP - 1)]
        to_dp(neighbour, some, some, grad_send.at[n], grad_recv.at[n]).wait_recv()
        sums = grad_in[n, 0].astype(F32)
        for k in range(1, GROUP):
            sums = sums + grad_in[n, k].astype(F32)
        result[...] = sums[:, 0:PART]

    for c in range(CH):
        some = xall.at[c, pl.ds(0, MP - 1), pl.ds(0, XROWS if c == 0 else PART)]
        to_mp(1, some, some, x_send.at[c], x_recv.at[c, 0]).wait_send()
        some = part_out.at[c, pl.ds(0, MP - 1)]
        to_mp(1, some, some, p_send.at[c], p_recv.at[c, 0]).wait_send()
    some = pool_out.at[pl.ds(0, MP - 1)]
    to_mp(1, some, some, pool_send.at[0], pool_recv.at[0]).wait_send()
    some = pair_in.at[pl.ds(0, MP - 1)]
    to_mp(1, some, some, pair_send.at[0], pair_recv.at[0]).wait_send()
    for buf, send, recv in (
        (tbuf, t_send.at[0], t_recv.at[0]),
        (ibuf, i_send.at[0], i_recv.at[0]),
        (grad_out.at[0], grad_send.at[0], grad_recv.at[0]),
        (grad_out.at[1], grad_send.at[1], grad_recv.at[1]),
    ):
        some = buf.at[pl.ds(0, GROUP - 1)]
        to_dp(neighbour, some, some, send, recv).wait_send()
    some = slot_out.at[pl.ds(0, DP - 1)]
    to_dp(neighbour, some, some, slot_send.at[0], slot_recv.at[0]).wait_send()


def hand_over(packed_in, image_in, text_in, packed_out, image_out, text_out):
    packed_out[...] = packed_in[...]
    image_out[...] = image_in[...]
    text_out[...] = text_in[...]


def shards(patches, patch_shard, patch_image, caption_of, text_embed, ln_gain, fc1_weight, fc1_bias, fc2_weight, fc2_bias):
    vmem = pl.BlockSpec(memory_space=pltpu.VMEM)
    hbm = pl.BlockSpec(memory_space=pltpu.HBM)
    dma = pltpu.SemaphoreType.DMA
    shapes = (
        jax.ShapeDtypeStruct((PART, SLOTS), BF16),
        jax.ShapeDtypeStruct((IMG, PART), F32),
        jax.ShapeDtypeStruct((IMG, PART), F32),
    )
    results = pl.pallas_call(
        kernel,
        out_shape=shapes,
        in_specs=[hbm] * 10,
        out_specs=(vmem, vmem, vmem),
        scratch_shapes=[
            pltpu.VMEM((PART, ROWS), BF16),
            pltpu.VMEM((IMG, PART), BF16),
            pltpu.VMEM((1, ROWS), I32),
            pltpu.VMEM((1, ROWS), I32),
            pltpu.VMEM((1, IMG), I32),
            pltpu.VMEM((PART,), BF16),
            pltpu.VMEM((FF,), BF16),
            pltpu.VMEM((PART,), BF16),
            pltpu.VMEM((FF, FULL), BF16),
            pltpu.VMEM((FF, FULL), BF16),
            pltpu.VMEM((8, FFP), F32),
            pltpu.VMEM((FULL, FFP), BF16),
            pltpu.VMEM((CH, MP, XROWS, L), BF16),
            pltpu.VMEM((FULL, 128), F32),
            pltpu.VMEM((FFP, 128), F32),
            pltpu.VMEM((PART, 128), F32),
            pltpu.VMEM((FFP, ROWS), BF16),
            pltpu.VMEM((CH, 7, PART, L), BF16),
            pltpu.VMEM((CH, 7, PART, L), BF16),
            pltpu.VMEM((MP, 32, 256), BF16),
            pltpu.VMEM((MP, 32, 256), BF16),
            pltpu.VMEM((GROUP, IMG, 256), BF16),
            pltpu.VMEM((GROUP, IMG, 256), BF16),
            pltpu.VMEM((SIDE + 16, SIDE), BF16),
            pltpu.VMEM((MP, SIDE + 16, SIDE), BF16),
            pltpu.VMEM((2, GROUP, IMG, 256), BF16),
            pltpu.VMEM((2, GROUP, IMG, 256), BF16),
            pltpu.VMEM((2, DP * 16, ROWS), BF16),
            pltpu.VMEM((DP * 16, 128), BF16),
            pltpu.VMEM((DP * 16, SLOTS), BF16),
            pltpu.VMEM((ROWS, 384), BF16),
            pltpu.VMEM((DP, 16, 128), BF16),
            pltpu.VMEM((DP, 16, 128), BF16),
            dma((10,)),
            dma((CH,)), dma((CH, 7)),
            dma((1,)), dma((1,)),
            dma((CH,)), dma((CH, 7)),
            dma((1,)), dma((1,)),
            dma((1,)), dma((1,)),
            dma((1,)), dma((1,)),
            dma((2,)), dma((2,)),
            dma((1,)), dma((1,)),
        ],
        compiler_params=pltpu.CompilerParams(
            collective_id=0, has_side_effects=True, vmem_limit_bytes=60 * 1024 * 1024
        ),
    )(
        patches.T, text_embed, patch_shard.reshape(1, ROWS), patch_image, caption_of.reshape(1, IMG),
        ln_gain, fc1_bias, fc2_bias, fc1_weight.T, fc2_weight,
    )
    packed, image_grad, text_grad = pl.pallas_call(
        hand_over,
        out_shape=shapes,
        in_specs=[vmem] * 3,
        out_specs=(vmem,) * 3,
        compiler_params=pltpu.CompilerParams(vmem_limit_bytes=60 * 1024 * 1024),
    )(*results)
    return packed.T[None], image_grad, text_grad


def solution(mesh):
    return jax.shard_map(
        shards,
        mesh=mesh,
        in_specs=(
            P("dp", "mp"),
            P("dp", None),
            P("dp", None),
            P("dp"),
            P("dp", "mp"),
            P("mp"),
            P(None, "mp"),
            P("mp"),
            P("mp", None),
            P("mp"),
        ),
        out_specs=(P("dp", None, "mp"), P("dp", "mp"), P("dp", "mp")),
        check_vma=False,
    )
```

```python
import functools

import jax
import jax.numpy as jnp
from jax import lax
from jax.experimental import pallas as pl
from jax.experimental.pallas import tpu as pltpu
from jax.sharding import PartitionSpec as P

LOGIT_SCALE = 10.0
LOGIT_BIAS = -2.0
F32 = jnp.float32
BF16 = jnp.bfloat16
I32 = jnp.int32
MESH = pl.DeviceIdType.MESH

DP, MP = 64, 8
GROUP = 8
ROWS, PART, FULL = 512, 144, 1152
FF, FFP = 538, 640
IMG, CAP = 16, 10
SLOTS = DP * CAP
CH = 2
L = ROWS // CH
SIDE = GROUP * IMG
XROWS = PART + 16


def nn(a, b):
    return jnp.dot(a, b, preferred_element_type=F32)


def nt(a, b):
    return lax.dot_general(a, b, (((1,), (1,)), ((), ())), preferred_element_type=F32)


def tn(a, b):
    return lax.dot_general(a, b, (((0,), (0,)), ((), ())), preferred_element_type=F32)


def iota(shape, axis):
    return lax.broadcasted_iota(I32, shape, axis)


def gelu(h):
    return 0.5 * h * (1.0 + jnp.tanh(0.7978845608028654 * (h + 0.044715 * (h * h * h))))


def wide(column_block):
    return jnp.concatenate([column_block] * (L // 128), axis=1)


def kernel(
    x_hbm, text_hbm, target_hbm, owner_hbm, caption_hbm, gain_hbm, b1_hbm, b2_hbm, w1_hbm, w2_hbm,
    packed_ref, image_grad_ref, text_grad_ref,
    x_ref, text_ref, target_ref, owner_ref, caption_ref, gain_ref, b1_ref, b2_ref, w1, w2,
    small_ref, w2t, xall, gain_b, b1_b, b2_b, hid, part_out, part_in,
    pool_out, pool_in, tbuf, ibuf, pair_out, pair_in, grad_out, grad_in,
    pick, empty_pick, sel, rows_out, slot_out, slot_in,
    load_sem, x_send, x_recv, t_send, t_recv, p_send, p_recv,
    pool_send, pool_recv, i_send, i_recv, pair_send, pair_recv,
    grad_send, grad_recv, slot_send, slot_recv, ready_sem,
):
    s = lax.axis_index("dp")
    m = lax.axis_index("mp")
    a = s // GROUP
    b = lax.rem(s, GROUP)
    neighbour = lax.rem(s + 1, DP)

    ring, side = m // 2, lax.rem(m, 2)
    ahead = lax.rem(ring + 1, 4) * 2 + side
    behind = lax.rem(ring + 3, 4) * 2 + side
    far = lax.rem(ring + 2, 4) * 2 + side
    across = ring * 2 + 1 - side
    ahead_across = lax.rem(ring + 1, 4) * 2 + 1 - side
    behind_across = lax.rem(ring + 3, 4) * 2 + 1 - side
    far_across = lax.rem(ring + 2, 4) * 2 + 1 - side

    loads = [
        pltpu.make_async_copy(src, dst, load_sem.at[n])
        for n, (src, dst) in enumerate(
            (
                (x_hbm, x_ref), (gain_hbm, gain_ref), (text_hbm, text_ref), (caption_hbm, caption_ref),
                (target_hbm, target_ref), (owner_hbm, owner_ref), (b1_hbm, b1_ref), (b2_hbm, b2_ref),
                (w1_hbm, w1), (w2_hbm, w2),
            )
        )
    ]
    for load in loads:
        load.start()

    barrier = pltpu.get_barrier_semaphore()

    def greet_mp(i, c):
        pl.semaphore_signal(barrier, inc=1, device_id=(s, lax.rem(m + i, MP)), device_id_type=MESH)
        return c

    def greet_dp(i, c):
        images = a * GROUP + lax.rem(b + i, GROUP)
        texts = lax.rem(a + i, GROUP) * GROUP + b
        pl.semaphore_signal(barrier, inc=1, device_id=(images, m), device_id_type=MESH)
        pl.semaphore_signal(barrier, inc=1, device_id=(texts, m), device_id_type=MESH)
        return c

    lax.fori_loop(1, MP, greet_mp, 0, unroll=True)
    lax.fori_loop(1, GROUP, greet_dp, 0, unroll=True)

    def to_member(member, src, dst, send, recv):
        return pltpu.make_async_remote_copy(
            src_ref=src, dst_ref=dst, send_sem=send, recv_sem=recv,
            device_id=(s, member), device_id_type=MESH,
        )

    def to_mp(i, src, dst, send, recv):
        return to_member(lax.rem(m + i, MP), src, dst, send, recv)

    def to_dp(peer, src, dst, send, recv):
        return pltpu.make_async_remote_copy(
            src_ref=src, dst_ref=dst, send_sem=send, recv_sem=recv,
            device_id=(peer, m), device_id_type=MESH,
        )

    small_ref[...] = jnp.zeros_like(small_ref)
    loads[0].wait()
    loads[1].wait()
    small_ref[1:2, 0:PART] = gain_ref[...].astype(F32).reshape(1, PART)
    for c in range(CH):
        xall[c, m, 0:PART] = x_ref[:, c * L : (c + 1) * L]
    xall[0, m, PART:XROWS] = jnp.broadcast_to(small_ref[1:2, 0:L], (XROWS - PART, L)).astype(BF16)

    pl.semaphore_wait(barrier, MP - 1 + 2 * (GROUP - 1))

    def block(c, member):
        return xall.at[c, member, pl.ds(0, XROWS if c == 0 else PART)]

    def hand_on(c, owner, member, kind):
        to_member(member, block(c, owner), block(c, owner), x_send.at[c], x_recv.at[c, kind]).start()

    def expect(c, kind):
        to_member(across, block(c, m), block(c, m), x_send.at[c], x_recv.at[c, kind]).wait_recv()

    for c in range(CH):
        hand_on(c, m, across, 2)
        hand_on(c, m, ahead, 0)
        hand_on(c, m, behind, 1)

    for load in loads[2:8]:
        load.wait()
    small_ref[0:1, 0:FF] = b1_ref[...].astype(F32).reshape(1, FF)
    small_ref[2:3, 0:PART] = b2_ref[...].astype(F32).reshape(1, PART)
    diagonal = iota((IMG, IMG), 0) == iota((IMG, IMG), 1)
    caption_row = caption_ref[...]
    caption_high = jnp.right_shift(caption_row, 5)
    caption_low = jnp.bitwise_and(caption_row, 31)

    def as_column(row):
        return jnp.sum(jnp.where(diagonal, row.astype(F32), 0.0), axis=1, keepdims=True)

    text_own_f = jnp.concatenate([text_ref[...].astype(F32), jnp.zeros((IMG, 256 - PART), F32)], axis=1)
    tbuf[a] = text_own_f.astype(BF16)

    def send_text(i, k):
        peer = lax.rem(a + i, GROUP) * GROUP + b
        to_dp(peer, tbuf.at[a], tbuf.at[a], t_send.at[0], t_recv.at[0]).start()
        return k


    for c in range(CH):
        if c == 0:
            expect(c, 0)
            hand_on(c, behind, ahead, 5)
        else:
            expect(c, 1)
            hand_on(c, ahead, behind, 5)
        expect(c, 2)
        hand_on(c, across, ahead, 3)
        hand_on(c, across, behind, 4)

    lax.fori_loop(1, GROUP, send_text, 0, unroll=True)

    targets = target_ref[...]
    named = iota((DP, ROWS), 0) == targets
    named_b = jnp.where(named, 1.0, 0.0).astype(BF16)
    earlier = jnp.where(iota((ROWS, ROWS), 0) < iota((ROWS, ROWS), 1), 1.0, 0.0).astype(BF16)
    before = nn(named_b, earlier)
    rank = jnp.sum(jnp.where(named, before, 0.0), axis=0, keepdims=True).astype(I32)
    code = targets * 16 + rank

    first_row = jnp.where(iota((16, 128), 0) == 0, 1.0, 0.0).astype(BF16)
    b1_row = jnp.broadcast_to(small_ref[0:1, :], (16, FFP))
    b1_b[...] = tn(b1_row.astype(BF16), first_row)
    b2_row = jnp.broadcast_to(small_ref[2:3, 0:256], (16, 256)).astype(BF16)
    b2_b[...] = tn(b2_row, first_row)[0:PART]
    hid[...] = jnp.zeros_like(hid)
    for c in range(CH):
        expect(c, 5)
        hand_on(c, far, across, 6)

    def build_pick(b, k):
        row = iota((128, 1), 0) + b * 128
        slot = jnp.bitwise_and(row, 15)
        base = row - slot
        is_head = slot < CAP
        is_tail = jnp.logical_and(slot >= CAP, slot < CAP + CAP // 2)
        even = base + 2 * (slot - CAP)
        lines = pl.ds(pl.multiple_of(b * 128, 128), 128)
        lane = iota((128, 128), 1)
        main = jnp.where(jnp.where(is_head, row, jnp.where(is_tail, even, -1)) == code, 1.0, 0.0)
        odd = jnp.where(jnp.where(is_tail, even + 1, -1) == code, 1.0, 0.0)
        pick[0, lines, :] = main.astype(BF16)
        pick[1, lines, :] = odd.astype(BF16)
        lack = 1.0 - jnp.sum(main, axis=1, keepdims=True)
        lack_odd = 1.0 - jnp.sum(odd, axis=1, keepdims=True)
        lacks = jnp.where(
            lane == 0,
            jnp.where(is_head, lack, 0.0),
            jnp.where(lane == 1, jnp.where(is_tail, lack, 0.0), jnp.where(lane == 2, jnp.where(is_tail, lack_odd, 0.0), 0.0)),
        )
        empty_pick[lines, :] = lacks.astype(BF16)
        column = iota((128, SLOTS), 1)
        first = jnp.right_shift(row, 4) * CAP
        even_at = first + 2 * (slot - CAP)
        main_at = jnp.where(is_head, first + slot, jnp.where(is_tail, even_at, -1))
        odd_at = jnp.where(is_tail, even_at + 1, -1)
        here = jnp.logical_or(main_at == column, odd_at == column)
        sel[lines, :] = jnp.where(here, 1.0, 0.0).astype(BF16)
        return k

    lax.fori_loop(0, DP * 16 // 128, build_pick, 0)

    loads[8].wait()
    loads[9].wait()
    w2t[:, 0:512] = jnp.transpose(w2[0:512, :])
    tail_rows = jnp.concatenate([w2[512:FF, :].astype(F32), jnp.zeros((FFP - FF, FULL), F32)], axis=0)
    w2t[:, 512:FFP] = jnp.transpose(tail_rows).astype(BF16)

    def share(c, member):
        lines = pl.ds(pl.multiple_of(member * PART, 16), PART)
        return nn(w2t[lines, :], hid[:, c * L : (c + 1) * L])

    def pass_on(c, value, member, kind):
        part_out[c, kind] = value.astype(BF16)
        to_member(member, part_out.at[c, kind], part_in.at[c, kind], p_send.at[c], p_recv.at[c, kind]).start()

    def arrived_sum(c, kind):
        to_member(across, part_in.at[c, kind], part_in.at[c, kind], p_send.at[c], p_recv.at[c, kind]).wait_recv()
        return part_in[c, kind].astype(F32)

    def first_sums(c):
        pass_on(c, share(c, far_across), across, 0)
        pass_on(c, share(c, ahead_across), ahead, 1)
        pass_on(c, share(c, behind_across), behind, 2)
        if c == 0:
            pass_on(c, share(c, behind), behind, 5)
        else:
            pass_on(c, share(c, ahead), ahead, 4)

    def second_sums(c):
        pass_on(c, share(c, far) + arrived_sum(c, 0), ahead if c == 0 else behind, 3)
        pass_on(c, share(c, across) + arrived_sum(c, 1) + arrived_sum(c, 2), across, 6)

    def third_sums(c):
        if c == 0:
            pass_on(c, share(c, ahead) + arrived_sum(c, 3), ahead, 4)
        else:
            pass_on(c, share(c, behind) + arrived_sum(c, 3), behind, 5)

    for c in range(CH):
        for kind in (1 if c == 0 else 0, 3, 4, 6):
            expect(c, kind)
        if c == 0:
            for k in range(MP):
                gain_b[k * PART : (k + 1) * PART, :] = tn(xall[0, k, PART:XROWS], first_row)[0:PART]

        rows = xall[c, :, 0:PART].reshape(FULL, L).astype(F32)
        centre = rows - jnp.sum(rows, axis=0, keepdims=True) * (1.0 / FULL)
        spread = jnp.sum(centre * centre, axis=0, keepdims=True) * (1.0 / FULL)
        normed = (centre * lax.rsqrt(spread + 1e-06) * wide(gain_b[...])).astype(BF16)
        pre = nn(w1[...], normed) + wide(b1_b[0:FF, :])
        hid[0:FF, c * L : (c + 1) * L] = gelu(pre).astype(BF16)

        if c < CH - 1:
            first_sums(c)

    first_sums(CH - 1)
    member_f = jnp.where(iota((IMG, ROWS), 0) == owner_ref[...], 1.0, 0.0)
    member = member_f.astype(BF16)
    sums = nt(member, hid[...])
    high = sums.astype(BF16)
    low = (sums - high.astype(F32)).astype(BF16)
    lone = gelu(b1_row).astype(BF16)
    mixed = jnp.concatenate([high, low, lone], axis=0)

    def pool_block(i, k):
        there = lax.rem(m + i, MP)
        lines = pl.ds(pl.multiple_of(there * PART, 16), PART)
        got = nt(mixed, w2t[lines, :])
        pool_out[there, 0:16, 0:PART] = (got[0:16] + got[16:32]).astype(BF16)
        pool_out[there, 16:32, 0:PART] = got[32:48].astype(BF16)
        return k

    pool_out[...] = jnp.zeros_like(pool_out)
    lax.fori_loop(0, MP, pool_block, 0)

    def send_pool(i, k):
        there = lax.rem(m + i, MP)
        to_mp(i, pool_out.at[there], pool_in.at[m], pool_send.at[0], pool_recv.at[0]).start()
        return k

    lax.fori_loop(1, MP, send_pool, 0, unroll=True)
    pool_in[m] = pool_out[m]

    for c in range(CH):
        second_sums(c)

    some = pool_in.at[pl.ds(0, MP - 1)]
    to_mp(1, some, some, pool_send.at[0], pool_recv.at[0]).wait_recv()
    pooled = pool_in[0].astype(F32)
    for k in range(1, MP):
        pooled = pooled + pool_in[k].astype(F32)
    b2_wide = jnp.where(iota((1, 256), 1) < PART, small_ref[2:3, 0:256], 0.0)
    counts = jnp.sum(member_f, axis=1, keepdims=True)
    own_sum = nt(member, x_ref[...])
    own_sum = jnp.concatenate([own_sum, jnp.zeros((IMG, 256 - PART), F32)], axis=1)
    image_own = (pooled[0:16] + own_sum) / counts + b2_wide
    empty = (pooled[16:17] + b2_wide).astype(BF16)
    lane = iota((IMG, 256), 1)
    image_note = jnp.where(lane == PART, as_column(caption_high), jnp.where(lane == PART + 1, as_column(caption_low), image_own))
    ibuf[b] = image_note.astype(BF16)

    some = tbuf.at[pl.ds(0, GROUP - 1)]
    to_dp(neighbour, some, some, t_send.at[0], t_recv.at[0]).wait_recv()

    def tell(i, k):
        peer = a * GROUP + lax.rem(b + i, GROUP)
        pl.semaphore_signal(ready_sem, inc=1, device_id=(peer, m), device_id_type=MESH)
        return k

    lax.fori_loop(1, GROUP, tell, 0, unroll=True)

    def send_image(i, k):
        peer = a * GROUP + lax.rem(b + i, GROUP)
        to_dp(peer, ibuf.at[b], ibuf.at[b], i_send.at[0], i_recv.at[0]).start()
        return k

    lax.fori_loop(1, GROUP, send_image, 0, unroll=True)

    for c in range(CH):
        third_sums(c)

    encoded = []
    for c in range(CH):
        total = share(c, m) + arrived_sum(c, 4) + arrived_sum(c, 5) + arrived_sum(c, 6)
        own = x_ref[:, c * L : (c + 1) * L].astype(F32)
        encoded.append(own + total + wide(b2_b[...]))
    encoded = jnp.concatenate(encoded, axis=1)
    by_row = jnp.transpose(jnp.concatenate([encoded, jnp.zeros((256 - PART, ROWS), F32)], axis=0))
    rows_out[:, 0:256] = by_row.astype(BF16)
    rows_out[:, 256:384] = pltpu.roll(by_row[:, 128:256], 16, 1).astype(BF16)
    empty_f = jnp.broadcast_to(empty.astype(F32), (128, 256))
    line = iota((128, 128), 0)
    empty_tail = empty_f[:, 128:256]
    empties = jnp.where(
        line == 0,
        empty_f[:, 0:128],
        jnp.where(line == 1, empty_tail, jnp.where(line == 2, pltpu.roll(empty_tail, 16, 1), 0.0)),
    ).astype(BF16)
    head_row = jnp.bitwise_and(iota((256, 1), 0), 15) < CAP

    def fill(block):
        lines = pl.ds(pl.multiple_of(block * 256, 256), 256)
        main = nn(pick[0, lines, :], rows_out[:, 0:256])
        odd = nn(pick[1, lines, :], rows_out[:, 256:384])
        got = jnp.where(head_row, main[:, 0:128], main[:, 128:256] + odd) + nn(empty_pick[lines, :], empties)
        slot_out[pl.ds(block * 16, 16)] = got.astype(BF16).reshape(16, 16, 128)

    def send_slot(peer):
        to_dp(peer, slot_out.at[peer], slot_in.at[s], slot_send.at[0], slot_recv.at[0]).start()

    def fill_other(i, k):
        block = lax.rem(s // 16 + i, DP // 16)
        fill(block)
        for j in range(16):
            send_slot(block * 16 + j)
        return k

    pl.semaphore_wait(ready_sem, GROUP - 1)
    lax.fori_loop(1, 3, fill_other, 0)

    some = ibuf.at[pl.ds(0, GROUP - 1)]
    to_dp(neighbour, some, some, i_send.at[0], i_recv.at[0]).wait_recv()
    dots = nt(ibuf[...].reshape(SIDE, 256), tbuf[...].reshape(SIDE, 256))
    ones = jnp.where(iota((8, 256), 1) < PART, 1.0, 0.0).astype(BF16)

    def squares(block):
        value = block.astype(F32)
        return nt(ones, (value * value).astype(BF16))

    text_sq = squares(tbuf[...].reshape(SIDE, 256))
    image_sq = squares(ibuf[...].reshape(SIDE, 256))
    pair_out[0:SIDE] = dots.astype(BF16)
    pair_out[SIDE : SIDE + 16] = jnp.concatenate([text_sq, image_sq], axis=0).astype(BF16)

    def send_pair(i, k):
        to_mp(i, pair_out, pair_in.at[m], pair_send.at[0], pair_recv.at[0]).start()
        return k

    lax.fori_loop(1, MP, send_pair, 0, unroll=True)
    pair_in[m] = pair_out[...]


    lax.fori_loop(3, DP // 16, fill_other, 0)
    fill(s // 16)
    for j in range(1, 16):
        send_slot(s // 16 * 16 + lax.rem(s + j, 16))
    slot_in[s] = slot_out[s]

    some = pair_in.at[pl.ds(0, MP - 1)]
    to_mp(1, some, some, pair_send.at[0], pair_recv.at[0]).wait_recv()
    total = pair_in[0].astype(F32)
    for k in range(1, MP):
        total = total + pair_in[k].astype(F32)
    text_scale = lax.rsqrt(total[SIDE : SIDE + 1] + 1e-06)
    image_row = lax.rsqrt(total[SIDE + 8 : SIDE + 9] + 1e-06)
    image_scale = jnp.transpose(jnp.broadcast_to(image_row, (SIDE, SIDE)))
    place = iota((1, SIDE), 1)
    text_name = (jnp.right_shift(place, 4) * (GROUP * IMG) + b * IMG + jnp.bitwise_and(place, 15)).astype(F32)
    noted = ibuf[...].reshape(SIDE, 256)[:, 128:256].astype(F32)
    caption = noted[:, PART - 128 : PART - 127] * 32.0 + noted[:, PART - 127 : PART - 126]
    logits = LOGIT_SCALE * (total[0:SIDE] * image_scale * text_scale) + LOGIT_BIAS
    coef = 1.0 / (1.0 + jnp.exp(-logits)) - jnp.where(caption == text_name, 1.0, 0.0)
    for_images = (coef * text_scale).astype(BF16)
    for_texts = (coef * image_scale).astype(BF16)

    part = LOGIT_SCALE * nn(for_images, tbuf[...].reshape(SIDE, 256))
    grad_out[0] = part.astype(BF16).reshape(GROUP, IMG, 256)
    part = LOGIT_SCALE * tn(for_texts, ibuf[...].reshape(SIDE, 256))
    grad_out[1] = part.astype(BF16).reshape(GROUP, IMG, 256)

    def send_grad(i, k):
        there = lax.rem(b + i, GROUP)
        to_dp(a * GROUP + there, grad_out.at[0, there], grad_in.at[0, b], grad_send.at[0], grad_recv.at[0]).start()
        there = lax.rem(a + i, GROUP)
        to_dp(there * GROUP + b, grad_out.at[1, there], grad_in.at[1, a], grad_send.at[1], grad_recv.at[1]).start()
        return k

    lax.fori_loop(1, GROUP, send_grad, 0, unroll=True)
    grad_in[0, b] = grad_out[0, b]
    grad_in[1, a] = grad_out[1, a]

    some = slot_in.at[pl.ds(0, DP - 1)]
    to_dp(neighbour, some, some, slot_send.at[0], slot_recv.at[0]).wait_recv()
    arrived = jnp.transpose(slot_in[...].reshape(DP * 16, 128))
    head_lane = jnp.bitwise_and(iota((1, DP * 16), 1), 15) < CAP
    nothing = jnp.zeros((32, DP * 16), BF16)
    both = jnp.concatenate([jnp.where(head_lane, arrived, 0), jnp.where(head_lane, nothing, arrived[0:32])], axis=0)
    placed = nn(both, sel[...])
    even_slot = jnp.bitwise_and(iota((1, SLOTS), 1), 1) == 0
    packed_ref[0:128, :] = placed[0:128].astype(BF16)
    packed_ref[128:PART, :] = jnp.where(even_slot, placed[128:PART], placed[PART : PART + 16]).astype(BF16)

    for n, result in enumerate((image_grad_ref, text_grad_ref)):
        some = grad_in.at[n, pl.ds(0, GROUP - 1)]
        to_dp(neighbour, some, some, grad_send.at[n], grad_recv.at[n]).wait_recv()
        sums = grad_in[n, 0].astype(F32)
        for k in range(1, GROUP):
            sums = sums + grad_in[n, k].astype(F32)
        result[...] = sums[:, 0:PART]

    for c in range(CH):
        some = xall.at[c, pl.ds(0, MP - 1), pl.ds(0, XROWS if c == 0 else PART)]
        to_mp(1, some, some, x_send.at[c], x_recv.at[c, 0]).wait_send()
        some = part_out.at[c, pl.ds(0, MP - 1)]
        to_mp(1, some, some, p_send.at[c], p_recv.at[c, 0]).wait_send()
    some = pool_out.at[pl.ds(0, MP - 1)]
    to_mp(1, some, some, pool_send.at[0], pool_recv.at[0]).wait_send()
    some = pair_in.at[pl.ds(0, MP - 1)]
    to_mp(1, some, some, pair_send.at[0], pair_recv.at[0]).wait_send()
    for buf, send, recv in (
        (tbuf, t_send.at[0], t_recv.at[0]),
        (ibuf, i_send.at[0], i_recv.at[0]),
        (grad_out.at[0], grad_send.at[0], grad_recv.at[0]),
        (grad_out.at[1], grad_send.at[1], grad_recv.at[1]),
    ):
        some = buf.at[pl.ds(0, GROUP - 1)]
        to_dp(neighbour, some, some, send, recv).wait_send()
    some = slot_out.at[pl.ds(0, DP - 1)]
    to_dp(neighbour, some, some, slot_send.at[0], slot_recv.at[0]).wait_send()


def hand_over(packed_in, image_in, text_in, packed_out, image_out, text_out):
    packed_out[...] = packed_in[...]
    image_out[...] = image_in[...]
    text_out[...] = text_in[...]


def shards(patches, patch_shard, patch_image, caption_of, text_embed, ln_gain, fc1_weight, fc1_bias, fc2_weight, fc2_bias):
    vmem = pl.BlockSpec(memory_space=pltpu.VMEM)
    hbm = pl.BlockSpec(memory_space=pltpu.HBM)
    dma = pltpu.SemaphoreType.DMA
    shapes = (
        jax.ShapeDtypeStruct((PART, SLOTS), BF16),
        jax.ShapeDtypeStruct((IMG, PART), F32),
        jax.ShapeDtypeStruct((IMG, PART), F32),
    )
    results = pl.pallas_call(
        kernel,
        out_shape=shapes,
        in_specs=[hbm] * 10,
        out_specs=(vmem, vmem, vmem),
        scratch_shapes=[
            pltpu.VMEM((PART, ROWS), BF16),
            pltpu.VMEM((IMG, PART), BF16),
            pltpu.VMEM((1, ROWS), I32),
            pltpu.VMEM((1, ROWS), I32),
            pltpu.VMEM((1, IMG), I32),
            pltpu.VMEM((PART,), BF16),
            pltpu.VMEM((FF,), BF16),
            pltpu.VMEM((PART,), BF16),
            pltpu.VMEM((FF, FULL), BF16),
            pltpu.VMEM((FF, FULL), BF16),
            pltpu.VMEM((8, FFP), F32),
            pltpu.VMEM((FULL, FFP), BF16),
            pltpu.VMEM((CH, MP, XROWS, L), BF16),
            pltpu.VMEM((FULL, 128), F32),
            pltpu.VMEM((FFP, 128), F32),
            pltpu.VMEM((PART, 128), F32),
            pltpu.VMEM((FFP, ROWS), BF16),
            pltpu.VMEM((CH, 7, PART, L), BF16),
            pltpu.VMEM((CH, 7, PART, L), BF16),
            pltpu.VMEM((MP, 32, 256), BF16),
            pltpu.VMEM((MP, 32, 256), BF16),
            pltpu.VMEM((GROUP, IMG, 256), BF16),
            pltpu.VMEM((GROUP, IMG, 256), BF16),
            pltpu.VMEM((SIDE + 16, SIDE), BF16),
            pltpu.VMEM((MP, SIDE + 16, SIDE), BF16),
            pltpu.VMEM((2, GROUP, IMG, 256), BF16),
            pltpu.VMEM((2, GROUP, IMG, 256), BF16),
            pltpu.VMEM((2, DP * 16, ROWS), BF16),
            pltpu.VMEM((DP * 16, 128), BF16),
            pltpu.VMEM((DP * 16, SLOTS), BF16),
            pltpu.VMEM((ROWS, 384), BF16),
            pltpu.VMEM((DP, 16, 128), BF16),
            pltpu.VMEM((DP, 16, 128), BF16),
            dma((10,)),
            dma((CH,)), dma((CH, 7)),
            dma((1,)), dma((1,)),
            dma((CH,)), dma((CH, 7)),
            dma((1,)), dma((1,)),
            dma((1,)), dma((1,)),
            dma((1,)), dma((1,)),
            dma((2,)), dma((2,)),
            dma((1,)), dma((1,)),
            pltpu.SemaphoreType.REGULAR,
        ],
        compiler_params=pltpu.CompilerParams(
            collective_id=0, has_side_effects=True, vmem_limit_bytes=60 * 1024 * 1024
        ),
    )(
        patches.T, text_embed, patch_shard.reshape(1, ROWS), patch_image, caption_of.reshape(1, IMG),
        ln_gain, fc1_bias, fc2_bias, fc1_weight.T, fc2_weight,
    )
    packed, image_grad, text_grad = pl.pallas_call(
        hand_over,
        out_shape=shapes,
        in_specs=[vmem] * 3,
        out_specs=(vmem,) * 3,
        compiler_params=pltpu.CompilerParams(vmem_limit_bytes=60 * 1024 * 1024),
    )(*results)
    return packed.T[None], image_grad, text_grad


def solution(mesh):
    return jax.shard_map(
        shards,
        mesh=mesh,
        in_specs=(
            P("dp", "mp"),
            P("dp", None),
            P("dp", None),
            P("dp"),
            P("dp", "mp"),
            P("mp"),
            P(None, "mp"),
            P("mp"),
            P("mp", None),
            P("mp"),
        ),
        out_specs=(P("dp", None, "mp"), P("dp", "mp"), P("dp", "mp")),
        check_vma=False,
    )
```

```python
import functools

import jax
import jax.numpy as jnp
from jax import lax
from jax.experimental import pallas as pl
from jax.experimental.pallas import tpu as pltpu
from jax.sharding import PartitionSpec as P

LOGIT_SCALE = 10.0
LOGIT_BIAS = -2.0
F32 = jnp.float32
BF16 = jnp.bfloat16
I32 = jnp.int32
MESH = pl.DeviceIdType.MESH

DP, MP = 64, 8
GROUP = 8
ROWS, PART, FULL = 512, 144, 1152
FF, FFP = 538, 640
IMG, CAP = 16, 10
SLOTS = DP * CAP
CH = 2
L = ROWS // CH
SIDE = GROUP * IMG
XROWS = PART + 16


def nn(a, b):
    return jnp.dot(a, b, preferred_element_type=F32)


def nt(a, b):
    return lax.dot_general(a, b, (((1,), (1,)), ((), ())), preferred_element_type=F32)


def tn(a, b):
    return lax.dot_general(a, b, (((0,), (0,)), ((), ())), preferred_element_type=F32)


def iota(shape, axis):
    return lax.broadcasted_iota(I32, shape, axis)


def gelu(h):
    return 0.5 * h * (1.0 + jnp.tanh(0.7978845608028654 * (h + 0.044715 * (h * h * h))))


def wide(column_block):
    return jnp.concatenate([column_block] * (L // 128), axis=1)


def kernel(
    x_hbm, text_hbm, target_hbm, owner_hbm, caption_hbm, gain_hbm, b1_hbm, b2_hbm, w1_hbm, w2_hbm,
    packed_ref, image_grad_ref, text_grad_ref,
    x_ref, text_ref, target_ref, owner_ref, caption_ref, gain_ref, b1_ref, b2_ref, w1, w2,
    small_ref, w2t, xall, gain_b, b1_b, b2_b, hid, part_out, part_in,
    pool_out, pool_in, tbuf, ibuf, pair_out, pair_in, grad_out, grad_in,
    pick, empty_pick, sel, rows_out, slot_out, slot_in,
    load_sem, x_send, x_recv, t_send, t_recv, p_send, p_recv,
    pool_send, pool_recv, i_send, i_recv, pair_send, pair_recv,
    grad_send, grad_recv, slot_send, slot_recv, ready_sem,
):
    s = lax.axis_index("dp")
    m = lax.axis_index("mp")
    a = s // GROUP
    b = lax.rem(s, GROUP)
    neighbour = lax.rem(s + 1, DP)

    ring, side = m // 2, lax.rem(m, 2)
    ahead = lax.rem(ring + 1, 4) * 2 + side
    behind = lax.rem(ring + 3, 4) * 2 + side
    far = lax.rem(ring + 2, 4) * 2 + side
    across = ring * 2 + 1 - side
    ahead_across = lax.rem(ring + 1, 4) * 2 + 1 - side
    behind_across = lax.rem(ring + 3, 4) * 2 + 1 - side
    far_across = lax.rem(ring + 2, 4) * 2 + 1 - side

    loads = [
        pltpu.make_async_copy(src, dst, load_sem.at[n])
        for n, (src, dst) in enumerate(
            (
                (x_hbm, x_ref), (gain_hbm, gain_ref), (text_hbm, text_ref), (caption_hbm, caption_ref),
                (target_hbm, target_ref), (owner_hbm, owner_ref), (b1_hbm, b1_ref), (b2_hbm, b2_ref),
                (w1_hbm, w1), (w2_hbm, w2),
            )
        )
    ]
    for load in loads:
        load.start()

    barrier = pltpu.get_barrier_semaphore()

    def greet_mp(i, c):
        pl.semaphore_signal(barrier, inc=1, device_id=(s, lax.rem(m + i, MP)), device_id_type=MESH)
        return c

    def greet_dp(i, c):
        images = a * GROUP + lax.rem(b + i, GROUP)
        texts = lax.rem(a + i, GROUP) * GROUP + b
        pl.semaphore_signal(barrier, inc=1, device_id=(images, m), device_id_type=MESH)
        pl.semaphore_signal(barrier, inc=1, device_id=(texts, m), device_id_type=MESH)
        return c

    lax.fori_loop(1, MP, greet_mp, 0, unroll=True)
    lax.fori_loop(1, GROUP, greet_dp, 0, unroll=True)

    def to_member(member, src, dst, send, recv):
        return pltpu.make_async_remote_copy(
            src_ref=src, dst_ref=dst, send_sem=send, recv_sem=recv,
            device_id=(s, member), device_id_type=MESH,
        )

    def to_mp(i, src, dst, send, recv):
        return to_member(lax.rem(m + i, MP), src, dst, send, recv)

    def to_dp(peer, src, dst, send, recv):
        return pltpu.make_async_remote_copy(
            src_ref=src, dst_ref=dst, send_sem=send, recv_sem=recv,
            device_id=(peer, m), device_id_type=MESH,
        )

    small_ref[...] = jnp.zeros_like(small_ref)
    loads[0].wait()
    loads[1].wait()
    small_ref[1:2, 0:PART] = gain_ref[...].astype(F32).reshape(1, PART)
    for c in range(CH):
        xall[c, m, 0:PART] = x_ref[:, c * L : (c + 1) * L]
    xall[0, m, PART:XROWS] = jnp.broadcast_to(small_ref[1:2, 0:L], (XROWS - PART, L)).astype(BF16)

    pl.semaphore_wait(barrier, MP - 1 + 2 * (GROUP - 1))

    def block(c, member):
        return xall.at[c, member, pl.ds(0, XROWS if c == 0 else PART)]

    def hand_on(c, owner, member, kind):
        to_member(member, block(c, owner), block(c, owner), x_send.at[c], x_recv.at[c, kind]).start()

    def expect(c, kind):
        to_member(across, block(c, m), block(c, m), x_send.at[c], x_recv.at[c, kind]).wait_recv()

    for c in range(CH):
        hand_on(c, m, across, 2)
        hand_on(c, m, ahead, 0)
        hand_on(c, m, behind, 1)

    for load in loads[2:8]:
        load.wait()
    small_ref[0:1, 0:FF] = b1_ref[...].astype(F32).reshape(1, FF)
    small_ref[2:3, 0:PART] = b2_ref[...].astype(F32).reshape(1, PART)
    diagonal = iota((IMG, IMG), 0) == iota((IMG, IMG), 1)
    caption_row = caption_ref[...]
    caption_high = jnp.right_shift(caption_row, 5)
    caption_low = jnp.bitwise_and(caption_row, 31)

    def as_column(row):
        return jnp.sum(jnp.where(diagonal, row.astype(F32), 0.0), axis=1, keepdims=True)

    text_own_f = jnp.concatenate([text_ref[...].astype(F32), jnp.zeros((IMG, 256 - PART), F32)], axis=1)
    tbuf[a] = text_own_f.astype(BF16)

    def send_text(i, k):
        peer = lax.rem(a + i, GROUP) * GROUP + b
        to_dp(peer, tbuf.at[a], tbuf.at[a], t_send.at[0], t_recv.at[0]).start()
        return k


    for c in range(CH):
        if c == 0:
            expect(c, 0)
            hand_on(c, behind, ahead, 5)
        else:
            expect(c, 1)
            hand_on(c, ahead, behind, 5)
        expect(c, 2)
        hand_on(c, across, ahead, 3)
        hand_on(c, across, behind, 4)

    lax.fori_loop(1, GROUP, send_text, 0, unroll=True)

    targets = target_ref[...]
    named = iota((DP, ROWS), 0) == targets
    named_b = jnp.where(named, 1.0, 0.0).astype(BF16)
    earlier = jnp.where(iota((ROWS, ROWS), 0) < iota((ROWS, ROWS), 1), 1.0, 0.0).astype(BF16)
    before = nn(named_b, earlier)
    rank = jnp.sum(jnp.where(named, before, 0.0), axis=0, keepdims=True).astype(I32)
    code = targets * 16 + rank

    first_row = jnp.where(iota((16, 128), 0) == 0, 1.0, 0.0).astype(BF16)
    b1_row = jnp.broadcast_to(small_ref[0:1, :], (16, FFP))
    b1_b[...] = tn(b1_row.astype(BF16), first_row)
    b2_row = jnp.broadcast_to(small_ref[2:3, 0:256], (16, 256)).astype(BF16)
    b2_b[...] = tn(b2_row, first_row)[0:PART]
    hid[...] = jnp.zeros_like(hid)
    for c in range(CH):
        expect(c, 5)
        hand_on(c, far, across, 6)

    def build_pick(b, k):
        row = iota((128, 1), 0) + b * 128
        slot = jnp.bitwise_and(row, 15)
        base = row - slot
        is_head = slot < CAP
        is_tail = jnp.logical_and(slot >= CAP, slot < CAP + CAP // 2)
        even = base + 2 * (slot - CAP)
        lines = pl.ds(pl.multiple_of(b * 128, 128), 128)
        lane = iota((128, 128), 1)
        main = jnp.where(jnp.where(is_head, row, jnp.where(is_tail, even, -1)) == code, 1.0, 0.0)
        odd = jnp.where(jnp.where(is_tail, even + 1, -1) == code, 1.0, 0.0)
        pick[0, lines, :] = main.astype(BF16)
        pick[1, lines, :] = odd.astype(BF16)
        lack = 1.0 - jnp.sum(main, axis=1, keepdims=True)
        lack_odd = 1.0 - jnp.sum(odd, axis=1, keepdims=True)
        lacks = jnp.where(
            lane == 0,
            jnp.where(is_head, lack, 0.0),
            jnp.where(lane == 1, jnp.where(is_tail, lack, 0.0), jnp.where(lane == 2, jnp.where(is_tail, lack_odd, 0.0), 0.0)),
        )
        empty_pick[lines, :] = lacks.astype(BF16)
        column = iota((128, SLOTS), 1)
        first = jnp.right_shift(row, 4) * CAP
        even_at = first + 2 * (slot - CAP)
        main_at = jnp.where(is_head, first + slot, jnp.where(is_tail, even_at, -1))
        odd_at = jnp.where(is_tail, even_at + 1, -1)
        here = jnp.logical_or(main_at == column, odd_at == column)
        sel[lines, :] = jnp.where(here, 1.0, 0.0).astype(BF16)
        return k

    lax.fori_loop(0, DP * 16 // 128, build_pick, 0)

    loads[8].wait()
    loads[9].wait()
    w2t[:, 0:512] = jnp.transpose(w2[0:512, :])
    tail_rows = jnp.concatenate([w2[512:FF, :].astype(F32), jnp.zeros((FFP - FF, FULL), F32)], axis=0)
    w2t[:, 512:FFP] = jnp.transpose(tail_rows).astype(BF16)

    def share(c, member):
        lines = pl.ds(pl.multiple_of(member * PART, 16), PART)
        return nn(w2t[lines, :], hid[:, c * L : (c + 1) * L])

    def pass_on(c, value, member, kind):
        part_out[c, kind] = value.astype(BF16)
        to_member(member, part_out.at[c, kind], part_in.at[c, kind], p_send.at[c], p_recv.at[c, kind]).start()

    def arrived_sum(c, kind):
        to_member(across, part_in.at[c, kind], part_in.at[c, kind], p_send.at[c], p_recv.at[c, kind]).wait_recv()
        return part_in[c, kind].astype(F32)

    def first_sums(c):
        pass_on(c, share(c, far_across), across, 0)
        pass_on(c, share(c, ahead_across), ahead, 1)
        pass_on(c, share(c, behind_across), behind, 2)
        if c == 0:
            pass_on(c, share(c, behind), behind, 5)
        else:
            pass_on(c, share(c, ahead), ahead, 4)

    def second_sums(c):
        pass_on(c, share(c, far) + arrived_sum(c, 0), ahead if c == 0 else behind, 3)
        pass_on(c, share(c, across) + arrived_sum(c, 1) + arrived_sum(c, 2), across, 6)

    def third_sums(c):
        if c == 0:
            pass_on(c, share(c, ahead) + arrived_sum(c, 3), ahead, 4)
        else:
            pass_on(c, share(c, behind) + arrived_sum(c, 3), behind, 5)

    for c in range(CH):
        for kind in (1 if c == 0 else 0, 3, 4, 6):
            expect(c, kind)
        if c == 0:
            for k in range(MP):
                gain_b[k * PART : (k + 1) * PART, :] = tn(xall[0, k, PART:XROWS], first_row)[0:PART]

        rows = xall[c, :, 0:PART].reshape(FULL, L).astype(F32)
        centre = rows - jnp.sum(rows, axis=0, keepdims=True) * (1.0 / FULL)
        spread = jnp.sum(centre * centre, axis=0, keepdims=True) * (1.0 / FULL)
        normed = (centre * lax.rsqrt(spread + 1e-06) * wide(gain_b[...])).astype(BF16)
        pre = nn(w1[...], normed) + wide(b1_b[0:FF, :])
        hid[0:FF, c * L : (c + 1) * L] = gelu(pre).astype(BF16)

        if c < CH - 1:
            first_sums(c)

    first_sums(CH - 1)
    second_sums(0)

    member_f = jnp.where(iota((IMG, ROWS), 0) == owner_ref[...], 1.0, 0.0)
    member = member_f.astype(BF16)
    sums = nt(member, hid[...])
    high = sums.astype(BF16)
    low = (sums - high.astype(F32)).astype(BF16)
    lone = gelu(b1_row).astype(BF16)
    mixed = jnp.concatenate([high, low, lone], axis=0)

    def pool_block(i, k):
        there = lax.rem(m + i, MP)
        lines = pl.ds(pl.multiple_of(there * PART, 16), PART)
        got = nt(mixed, w2t[lines, :])
        pool_out[there, 0:16, 0:PART] = (got[0:16] + got[16:32]).astype(BF16)
        pool_out[there, 16:32, 0:PART] = got[32:48].astype(BF16)
        return k

    pool_out[...] = jnp.zeros_like(pool_out)
    lax.fori_loop(0, MP, pool_block, 0)

    def send_pool(i, k):
        there = lax.rem(m + i, MP)
        to_mp(i, pool_out.at[there], pool_in.at[m], pool_send.at[0], pool_recv.at[0]).start()
        return k

    lax.fori_loop(1, MP, send_pool, 0, unroll=True)
    pool_in[m] = pool_out[m]

    second_sums(1)
    third_sums(0)

    some = pool_in.at[pl.ds(0, MP - 1)]
    to_mp(1, some, some, pool_send.at[0], pool_recv.at[0]).wait_recv()
    pooled = pool_in[0].astype(F32)
    for k in range(1, MP):
        pooled = pooled + pool_in[k].astype(F32)
    b2_wide = jnp.where(iota((1, 256), 1) < PART, small_ref[2:3, 0:256], 0.0)
    counts = jnp.sum(member_f, axis=1, keepdims=True)
    own_sum = nt(member, x_ref[...])
    own_sum = jnp.concatenate([own_sum, jnp.zeros((IMG, 256 - PART), F32)], axis=1)
    image_own = (pooled[0:16] + own_sum) / counts + b2_wide
    empty = (pooled[16:17] + b2_wide).astype(BF16)
    lane = iota((IMG, 256), 1)
    image_note = jnp.where(lane == PART, as_column(caption_high), jnp.where(lane == PART + 1, as_column(caption_low), image_own))
    ibuf[b] = image_note.astype(BF16)

    some = tbuf.at[pl.ds(0, GROUP - 1)]
    to_dp(neighbour, some, some, t_send.at[0], t_recv.at[0]).wait_recv()

    def tell(i, k):
        peer = a * GROUP + lax.rem(b + i, GROUP)
        pl.semaphore_signal(ready_sem, inc=1, device_id=(peer, m), device_id_type=MESH)
        return k

    lax.fori_loop(1, GROUP, tell, 0, unroll=True)

    def send_image(i, k):
        peer = a * GROUP + lax.rem(b + i, GROUP)
        to_dp(peer, ibuf.at[b], ibuf.at[b], i_send.at[0], i_recv.at[0]).start()
        return k

    lax.fori_loop(1, GROUP, send_image, 0, unroll=True)

    third_sums(1)

    def finish(c):
        total = share(c, m) + arrived_sum(c, 4) + arrived_sum(c, 5) + arrived_sum(c, 6)
        encoded = x_ref[:, c * L : (c + 1) * L].astype(F32) + total + wide(b2_b[...])
        by_row = jnp.transpose(jnp.concatenate([encoded, jnp.zeros((256 - PART, L), F32)], axis=0))
        rows_out[c * L : (c + 1) * L, 0:256] = by_row.astype(BF16)
        rows_out[c * L : (c + 1) * L, 256:384] = pltpu.roll(by_row[:, 128:256], 16, 1).astype(BF16)

    for c in range(CH):
        finish(c)


    empty_f = jnp.broadcast_to(empty.astype(F32), (128, 256))
    line = iota((128, 128), 0)
    empty_tail = empty_f[:, 128:256]
    empties = jnp.where(
        line == 0,
        empty_f[:, 0:128],
        jnp.where(line == 1, empty_tail, jnp.where(line == 2, pltpu.roll(empty_tail, 16, 1), 0.0)),
    ).astype(BF16)
    head_row = jnp.bitwise_and(iota((256, 1), 0), 15) < CAP

    def fill(block):
        lines = pl.ds(pl.multiple_of(block * 256, 256), 256)
        main = nn(pick[0, lines, :], rows_out[:, 0:256])
        odd = nn(pick[1, lines, :], rows_out[:, 256:384])
        got = jnp.where(head_row, main[:, 0:128], main[:, 128:256] + odd) + nn(empty_pick[lines, :], empties)
        slot_out[pl.ds(block * 16, 16)] = got.astype(BF16).reshape(16, 16, 128)

    def send_slot(peer):
        to_dp(peer, slot_out.at[peer], slot_in.at[s], slot_send.at[0], slot_recv.at[0]).start()

    def fill_other(i, k):
        block = lax.rem(s // 16 + i, DP // 16)
        fill(block)
        for j in range(16):
            send_slot(block * 16 + j)
        return k

    pl.semaphore_wait(ready_sem, GROUP - 1)
    lax.fori_loop(1, 3, fill_other, 0)

    some = ibuf.at[pl.ds(0, GROUP - 1)]
    to_dp(neighbour, some, some, i_send.at[0], i_recv.at[0]).wait_recv()
    dots = nt(ibuf[...].reshape(SIDE, 256), tbuf[...].reshape(SIDE, 256))
    ones = jnp.where(iota((8, 256), 1) < PART, 1.0, 0.0).astype(BF16)

    def squares(block):
        value = block.astype(F32)
        return nt(ones, (value * value).astype(BF16))

    text_sq = squares(tbuf[...].reshape(SIDE, 256))
    image_sq = squares(ibuf[...].reshape(SIDE, 256))
    pair_out[0:SIDE] = dots.astype(BF16)
    pair_out[SIDE : SIDE + 16] = jnp.concatenate([text_sq, image_sq], axis=0).astype(BF16)

    def send_pair(i, k):
        to_mp(i, pair_out, pair_in.at[m], pair_send.at[0], pair_recv.at[0]).start()
        return k

    lax.fori_loop(1, MP, send_pair, 0, unroll=True)
    pair_in[m] = pair_out[...]


    lax.fori_loop(3, DP // 16, fill_other, 0)
    fill(s // 16)
    for j in range(1, 16):
        send_slot(s // 16 * 16 + lax.rem(s + j, 16))
    slot_in[s] = slot_out[s]

    some = pair_in.at[pl.ds(0, MP - 1)]
    to_mp(1, some, some, pair_send.at[0], pair_recv.at[0]).wait_recv()
    total = pair_in[0].astype(F32)
    for k in range(1, MP):
        total = total + pair_in[k].astype(F32)
    text_scale = lax.rsqrt(total[SIDE : SIDE + 1] + 1e-06)
    image_row = lax.rsqrt(total[SIDE + 8 : SIDE + 9] + 1e-06)
    image_scale = jnp.transpose(jnp.broadcast_to(image_row, (SIDE, SIDE)))
    place = iota((1, SIDE), 1)
    text_name = (jnp.right_shift(place, 4) * (GROUP * IMG) + b * IMG + jnp.bitwise_and(place, 15)).astype(F32)
    noted = ibuf[...].reshape(SIDE, 256)[:, 128:256].astype(F32)
    caption = noted[:, PART - 128 : PART - 127] * 32.0 + noted[:, PART - 127 : PART - 126]
    logits = LOGIT_SCALE * (total[0:SIDE] * image_scale * text_scale) + LOGIT_BIAS
    coef = 1.0 / (1.0 + jnp.exp(-logits)) - jnp.where(caption == text_name, 1.0, 0.0)
    for_images = (coef * text_scale).astype(BF16)
    for_texts = (coef * image_scale).astype(BF16)

    part = LOGIT_SCALE * nn(for_images, tbuf[...].reshape(SIDE, 256))
    grad_out[0] = part.astype(BF16).reshape(GROUP, IMG, 256)
    part = LOGIT_SCALE * tn(for_texts, ibuf[...].reshape(SIDE, 256))
    grad_out[1] = part.astype(BF16).reshape(GROUP, IMG, 256)

    def send_grad(i, k):
        there = lax.rem(b + i, GROUP)
        to_dp(a * GROUP + there, grad_out.at[0, there], grad_in.at[0, b], grad_send.at[0], grad_recv.at[0]).start()
        there = lax.rem(a + i, GROUP)
        to_dp(there * GROUP + b, grad_out.at[1, there], grad_in.at[1, a], grad_send.at[1], grad_recv.at[1]).start()
        return k

    lax.fori_loop(1, GROUP, send_grad, 0, unroll=True)
    grad_in[0, b] = grad_out[0, b]
    grad_in[1, a] = grad_out[1, a]

    some = slot_in.at[pl.ds(0, DP - 1)]
    to_dp(neighbour, some, some, slot_send.at[0], slot_recv.at[0]).wait_recv()
    arrived = jnp.transpose(slot_in[...].reshape(DP * 16, 128))
    head_lane = jnp.bitwise_and(iota((1, DP * 16), 1), 15) < CAP
    nothing = jnp.zeros((32, DP * 16), BF16)
    both = jnp.concatenate([jnp.where(head_lane, arrived, 0), jnp.where(head_lane, nothing, arrived[0:32])], axis=0)
    placed = nn(both, sel[...])
    even_slot = jnp.bitwise_and(iota((1, SLOTS), 1), 1) == 0
    packed_ref[0:128, :] = placed[0:128].astype(BF16)
    packed_ref[128:PART, :] = jnp.where(even_slot, placed[128:PART], placed[PART : PART + 16]).astype(BF16)

    for n, result in enumerate((image_grad_ref, text_grad_ref)):
        some = grad_in.at[n, pl.ds(0, GROUP - 1)]
        to_dp(neighbour, some, some, grad_send.at[n], grad_recv.at[n]).wait_recv()
        sums = grad_in[n, 0].astype(F32)
        for k in range(1, GROUP):
            sums = sums + grad_in[n, k].astype(F32)
        result[...] = sums[:, 0:PART]

    for c in range(CH):
        some = xall.at[c, pl.ds(0, MP - 1), pl.ds(0, XROWS if c == 0 else PART)]
        to_mp(1, some, some, x_send.at[c], x_recv.at[c, 0]).wait_send()
        some = part_out.at[c, pl.ds(0, MP - 1)]
        to_mp(1, some, some, p_send.at[c], p_recv.at[c, 0]).wait_send()
    some = pool_out.at[pl.ds(0, MP - 1)]
    to_mp(1, some, some, pool_send.at[0], pool_recv.at[0]).wait_send()
    some = pair_in.at[pl.ds(0, MP - 1)]
    to_mp(1, some, some, pair_send.at[0], pair_recv.at[0]).wait_send()
    for buf, send, recv in (
        (tbuf, t_send.at[0], t_recv.at[0]),
        (ibuf, i_send.at[0], i_recv.at[0]),
        (grad_out.at[0], grad_send.at[0], grad_recv.at[0]),
        (grad_out.at[1], grad_send.at[1], grad_recv.at[1]),
    ):
        some = buf.at[pl.ds(0, GROUP - 1)]
        to_dp(neighbour, some, some, send, recv).wait_send()
    some = slot_out.at[pl.ds(0, DP - 1)]
    to_dp(neighbour, some, some, slot_send.at[0], slot_recv.at[0]).wait_send()


def hand_over(packed_in, image_in, text_in, packed_out, image_out, text_out):
    packed_out[...] = packed_in[...]
    image_out[...] = image_in[...]
    text_out[...] = text_in[...]


def shards(patches, patch_shard, patch_image, caption_of, text_embed, ln_gain, fc1_weight, fc1_bias, fc2_weight, fc2_bias):
    vmem = pl.BlockSpec(memory_space=pltpu.VMEM)
    hbm = pl.BlockSpec(memory_space=pltpu.HBM)
    dma = pltpu.SemaphoreType.DMA
    shapes = (
        jax.ShapeDtypeStruct((PART, SLOTS), BF16),
        jax.ShapeDtypeStruct((IMG, PART), F32),
        jax.ShapeDtypeStruct((IMG, PART), F32),
    )
    results = pl.pallas_call(
        kernel,
        out_shape=shapes,
        in_specs=[hbm] * 10,
        out_specs=(vmem, vmem, vmem),
        scratch_shapes=[
            pltpu.VMEM((PART, ROWS), BF16),
            pltpu.VMEM((IMG, PART), BF16),
            pltpu.VMEM((1, ROWS), I32),
            pltpu.VMEM((1, ROWS), I32),
            pltpu.VMEM((1, IMG), I32),
            pltpu.VMEM((PART,), BF16),
            pltpu.VMEM((FF,), BF16),
            pltpu.VMEM((PART,), BF16),
            pltpu.VMEM((FF, FULL), BF16),
            pltpu.VMEM((FF, FULL), BF16),
            pltpu.VMEM((8, FFP), F32),
            pltpu.VMEM((FULL, FFP), BF16),
            pltpu.VMEM((CH, MP, XROWS, L), BF16),
            pltpu.VMEM((FULL, 128), F32),
            pltpu.VMEM((FFP, 128), F32),
            pltpu.VMEM((PART, 128), F32),
            pltpu.VMEM((FFP, ROWS), BF16),
            pltpu.VMEM((CH, 7, PART, L), BF16),
            pltpu.VMEM((CH, 7, PART, L), BF16),
            pltpu.VMEM((MP, 32, 256), BF16),
            pltpu.VMEM((MP, 32, 256), BF16),
            pltpu.VMEM((GROUP, IMG, 256), BF16),
            pltpu.VMEM((GROUP, IMG, 256), BF16),
            pltpu.VMEM((SIDE + 16, SIDE), BF16),
            pltpu.VMEM((MP, SIDE + 16, SIDE), BF16),
            pltpu.VMEM((2, GROUP, IMG, 256), BF16),
            pltpu.VMEM((2, GROUP, IMG, 256), BF16),
            pltpu.VMEM((2, DP * 16, ROWS), BF16),
            pltpu.VMEM((DP * 16, 128), BF16),
            pltpu.VMEM((DP * 16, SLOTS), BF16),
            pltpu.VMEM((ROWS, 384), BF16),
            pltpu.VMEM((DP, 16, 128), BF16),
            pltpu.VMEM((DP, 16, 128), BF16),
            dma((10,)),
            dma((CH,)), dma((CH, 7)),
            dma((1,)), dma((1,)),
            dma((CH,)), dma((CH, 7)),
            dma((1,)), dma((1,)),
            dma((1,)), dma((1,)),
            dma((1,)), dma((1,)),
            dma((2,)), dma((2,)),
            dma((1,)), dma((1,)),
            pltpu.SemaphoreType.REGULAR,
        ],
        compiler_params=pltpu.CompilerParams(
            collective_id=0, has_side_effects=True, vmem_limit_bytes=60 * 1024 * 1024
        ),
    )(
        patches.T, text_embed, patch_shard.reshape(1, ROWS), patch_image, caption_of.reshape(1, IMG),
        ln_gain, fc1_bias, fc2_bias, fc1_weight.T, fc2_weight,
    )
    packed, image_grad, text_grad = pl.pallas_call(
        hand_over,
        out_shape=shapes,
        in_specs=[vmem] * 3,
        out_specs=(vmem,) * 3,
        compiler_params=pltpu.CompilerParams(vmem_limit_bytes=60 * 1024 * 1024),
    )(*results)
    return packed.T[None], image_grad, text_grad


def solution(mesh):
    return jax.shard_map(
        shards,
        mesh=mesh,
        in_specs=(
            P("dp", "mp"),
            P("dp", None),
            P("dp", None),
            P("dp"),
            P("dp", "mp"),
            P("mp"),
            P(None, "mp"),
            P("mp"),
            P("mp", None),
            P("mp"),
        ),
        out_specs=(P("dp", None, "mp"), P("dp", "mp"), P("dp", "mp")),
        check_vma=False,
    )
```

```python
import functools

import jax
import jax.numpy as jnp
from jax import lax
from jax.experimental import pallas as pl
from jax.experimental.pallas import tpu as pltpu
from jax.sharding import PartitionSpec as P

LOGIT_SCALE = 10.0
LOGIT_BIAS = -2.0
F32 = jnp.float32
BF16 = jnp.bfloat16
I32 = jnp.int32
MESH = pl.DeviceIdType.MESH

DP, MP = 64, 8
GROUP = 8
ROWS, PART, FULL = 512, 144, 1152
FF, FFP = 538, 640
IMG, CAP = 16, 10
SLOTS = DP * CAP
CH = 2
L = ROWS // CH
SIDE = GROUP * IMG
XROWS = PART + 16


def nn(a, b):
    return jnp.dot(a, b, preferred_element_type=F32)


def nt(a, b):
    return lax.dot_general(a, b, (((1,), (1,)), ((), ())), preferred_element_type=F32)


def tn(a, b):
    return lax.dot_general(a, b, (((0,), (0,)), ((), ())), preferred_element_type=F32)


def iota(shape, axis):
    return lax.broadcasted_iota(I32, shape, axis)


def gelu(h):
    return 0.5 * h * (1.0 + jnp.tanh(0.7978845608028654 * (h + 0.044715 * (h * h * h))))


def wide(column_block):
    return jnp.concatenate([column_block] * (L // 128), axis=1)


def kernel(
    x_hbm, text_hbm, target_hbm, owner_hbm, caption_hbm, gain_hbm, b1_hbm, b2_hbm, w1_hbm, w2_hbm,
    packed_ref, image_grad_ref, text_grad_ref,
    x_ref, text_ref, target_ref, owner_ref, caption_ref, gain_ref, b1_ref, b2_ref, w1, w2,
    small_ref, w2t, xall, gain_b, b1_b, b2_b, hid, part_out, part_in,
    pool_out, pool_in, tbuf, ibuf, pair_out, pair_in, grad_out, grad_in,
    pick, empty_pick, sel, rows_out, slot_out, slot_in,
    load_sem, x_send, x_recv, t_send, t_recv, p_send, p_recv,
    pool_send, pool_recv, i_send, i_recv, pair_send, pair_recv,
    grad_send, grad_recv, slot_send, slot_recv, ready_sem,
):
    s = lax.axis_index("dp")
    m = lax.axis_index("mp")
    a = s // GROUP
    b = lax.rem(s, GROUP)
    neighbour = lax.rem(s + 1, DP)

    ring, side = m // 2, lax.rem(m, 2)
    ahead = lax.rem(ring + 1, 4) * 2 + side
    behind = lax.rem(ring + 3, 4) * 2 + side
    far = lax.rem(ring + 2, 4) * 2 + side
    across = ring * 2 + 1 - side
    ahead_across = lax.rem(ring + 1, 4) * 2 + 1 - side
    behind_across = lax.rem(ring + 3, 4) * 2 + 1 - side
    far_across = lax.rem(ring + 2, 4) * 2 + 1 - side

    loads = [
        pltpu.make_async_copy(src, dst, load_sem.at[n])
        for n, (src, dst) in enumerate(
            (
                (x_hbm, x_ref), (gain_hbm, gain_ref), (text_hbm, text_ref), (caption_hbm, caption_ref),
                (target_hbm, target_ref), (owner_hbm, owner_ref), (b1_hbm, b1_ref), (b2_hbm, b2_ref),
                (w1_hbm, w1), (w2_hbm, w2),
            )
        )
    ]
    for load in loads:
        load.start()

    barrier = pltpu.get_barrier_semaphore()

    def greet_mp(i, c):
        pl.semaphore_signal(barrier, inc=1, device_id=(s, lax.rem(m + i, MP)), device_id_type=MESH)
        return c

    def greet_dp(i, c):
        images = a * GROUP + lax.rem(b + i, GROUP)
        texts = lax.rem(a + i, GROUP) * GROUP + b
        pl.semaphore_signal(barrier, inc=1, device_id=(images, m), device_id_type=MESH)
        pl.semaphore_signal(barrier, inc=1, device_id=(texts, m), device_id_type=MESH)
        return c

    lax.fori_loop(1, MP, greet_mp, 0, unroll=True)
    lax.fori_loop(1, GROUP, greet_dp, 0, unroll=True)

    def to_member(member, src, dst, send, recv):
        return pltpu.make_async_remote_copy(
            src_ref=src, dst_ref=dst, send_sem=send, recv_sem=recv,
            device_id=(s, member), device_id_type=MESH,
        )

    def to_mp(i, src, dst, send, recv):
        return to_member(lax.rem(m + i, MP), src, dst, send, recv)

    def to_dp(peer, src, dst, send, recv):
        return pltpu.make_async_remote_copy(
            src_ref=src, dst_ref=dst, send_sem=send, recv_sem=recv,
            device_id=(peer, m), device_id_type=MESH,
        )

    small_ref[...] = jnp.zeros_like(small_ref)
    loads[0].wait()
    loads[1].wait()
    small_ref[1:2, 0:PART] = gain_ref[...].astype(F32).reshape(1, PART)
    for c in range(CH):
        xall[c, m, 0:PART] = x_ref[:, c * L : (c + 1) * L]
    xall[0, m, PART:XROWS] = jnp.broadcast_to(small_ref[1:2, 0:L], (XROWS - PART, L)).astype(BF16)

    pl.semaphore_wait(barrier, MP - 1 + 2 * (GROUP - 1))

    def block(c, member):
        return xall.at[c, member, pl.ds(0, XROWS if c == 0 else PART)]

    def hand_on(c, owner, member, kind):
        to_member(member, block(c, owner), block(c, owner), x_send.at[c], x_recv.at[c, kind]).start()

    def expect(c, kind):
        to_member(across, block(c, m), block(c, m), x_send.at[c], x_recv.at[c, kind]).wait_recv()

    for c in range(CH):
        hand_on(c, m, across, 2)
        hand_on(c, m, ahead, 0)
        hand_on(c, m, behind, 1)

    for load in loads[2:8]:
        load.wait()
    small_ref[0:1, 0:FF] = b1_ref[...].astype(F32).reshape(1, FF)
    small_ref[2:3, 0:PART] = b2_ref[...].astype(F32).reshape(1, PART)
    diagonal = iota((IMG, IMG), 0) == iota((IMG, IMG), 1)
    caption_row = caption_ref[...]
    caption_high = jnp.right_shift(caption_row, 5)
    caption_low = jnp.bitwise_and(caption_row, 31)

    def as_column(row):
        return jnp.sum(jnp.where(diagonal, row.astype(F32), 0.0), axis=1, keepdims=True)

    text_own_f = jnp.concatenate([text_ref[...].astype(F32), jnp.zeros((IMG, 256 - PART), F32)], axis=1)
    tbuf[a] = text_own_f.astype(BF16)

    def send_text(i, k):
        peer = lax.rem(a + i, GROUP) * GROUP + b
        to_dp(peer, tbuf.at[a], tbuf.at[a], t_send.at[0], t_recv.at[0]).start()
        return k


    for c in range(CH):
        if c == 0:
            expect(c, 0)
            hand_on(c, behind, ahead, 5)
        else:
            expect(c, 1)
            hand_on(c, ahead, behind, 5)
        expect(c, 2)
        hand_on(c, across, ahead, 3)
        hand_on(c, across, behind, 4)

    lax.fori_loop(1, GROUP, send_text, 0, unroll=True)

    targets = target_ref[...]
    named = iota((DP, ROWS), 0) == targets
    named_b = jnp.where(named, 1.0, 0.0).astype(BF16)
    earlier = jnp.where(iota((ROWS, ROWS), 0) < iota((ROWS, ROWS), 1), 1.0, 0.0).astype(BF16)
    before = nn(named_b, earlier)
    rank = jnp.sum(jnp.where(named, before, 0.0), axis=0, keepdims=True).astype(I32)
    code = targets * 16 + rank

    first_row = jnp.where(iota((16, 128), 0) == 0, 1.0, 0.0).astype(BF16)
    b1_row = jnp.broadcast_to(small_ref[0:1, :], (16, FFP))
    b1_b[...] = tn(b1_row.astype(BF16), first_row)
    b2_row = jnp.broadcast_to(small_ref[2:3, 0:256], (16, 256)).astype(BF16)
    b2_b[...] = tn(b2_row, first_row)[0:PART]
    hid[...] = jnp.zeros_like(hid)
    for c in range(CH):
        expect(c, 5)
        hand_on(c, far, across, 6)

    def build_pick(b, k):
        row = iota((128, 1), 0) + b * 128
        slot = jnp.bitwise_and(row, 15)
        base = row - slot
        is_head = slot < CAP
        is_tail = jnp.logical_and(slot >= CAP, slot < CAP + CAP // 2)
        even = base + 2 * (slot - CAP)
        lines = pl.ds(pl.multiple_of(b * 128, 128), 128)
        lane = iota((128, 128), 1)
        main = jnp.where(jnp.where(is_head, row, jnp.where(is_tail, even, -1)) == code, 1.0, 0.0)
        odd = jnp.where(jnp.where(is_tail, even + 1, -1) == code, 1.0, 0.0)
        pick[0, lines, :] = main.astype(BF16)
        pick[1, lines, :] = odd.astype(BF16)
        lack = 1.0 - jnp.sum(main, axis=1, keepdims=True)
        lack_odd = 1.0 - jnp.sum(odd, axis=1, keepdims=True)
        lacks = jnp.where(
            lane == 0,
            jnp.where(is_head, lack, 0.0),
            jnp.where(lane == 1, jnp.where(is_tail, lack, 0.0), jnp.where(lane == 2, jnp.where(is_tail, lack_odd, 0.0), 0.0)),
        )
        empty_pick[lines, :] = lacks.astype(BF16)
        column = iota((128, SLOTS), 1)
        first = jnp.right_shift(row, 4) * CAP
        even_at = first + 2 * (slot - CAP)
        main_at = jnp.where(is_head, first + slot, jnp.where(is_tail, even_at, -1))
        odd_at = jnp.where(is_tail, even_at + 1, -1)
        here = jnp.logical_or(main_at == column, odd_at == column)
        sel[lines, :] = jnp.where(here, 1.0, 0.0).astype(BF16)
        return k

    lax.fori_loop(0, DP * 16 // 128, build_pick, 0)

    loads[8].wait()
    loads[9].wait()
    w2t[:, 0:512] = jnp.transpose(w2[0:512, :])
    tail_rows = jnp.concatenate([w2[512:FF, :].astype(F32), jnp.zeros((FFP - FF, FULL), F32)], axis=0)
    w2t[:, 512:FFP] = jnp.transpose(tail_rows).astype(BF16)

    def share(c, member):
        lines = pl.ds(pl.multiple_of(member * PART, 16), PART)
        return nn(w2t[lines, :], hid[:, c * L : (c + 1) * L])

    def pass_on(c, value, member, kind):
        part_out[c, kind] = value.astype(BF16)
        to_member(member, part_out.at[c, kind], part_in.at[c, kind], p_send.at[c], p_recv.at[c, kind]).start()

    def arrived_sum(c, kind):
        to_member(across, part_in.at[c, kind], part_in.at[c, kind], p_send.at[c], p_recv.at[c, kind]).wait_recv()
        return part_in[c, kind].astype(F32)

    def first_sums(c):
        pass_on(c, share(c, far_across), across, 0)
        pass_on(c, share(c, ahead_across), ahead, 1)
        pass_on(c, share(c, behind_across), behind, 2)
        if c == 0:
            pass_on(c, share(c, behind), behind, 5)
        else:
            pass_on(c, share(c, ahead), ahead, 4)

    def second_sums(c):
        pass_on(c, share(c, far) + arrived_sum(c, 0), ahead if c == 0 else behind, 3)
        pass_on(c, share(c, across) + arrived_sum(c, 1) + arrived_sum(c, 2), across, 6)

    def third_sums(c):
        if c == 0:
            pass_on(c, share(c, ahead) + arrived_sum(c, 3), ahead, 4)
        else:
            pass_on(c, share(c, behind) + arrived_sum(c, 3), behind, 5)

    for c in range(CH):
        for kind in (1 if c == 0 else 0, 3, 4, 6):
            expect(c, kind)
        if c == 0:
            for k in range(MP):
                gain_b[k * PART : (k + 1) * PART, :] = tn(xall[0, k, PART:XROWS], first_row)[0:PART]

        rows = xall[c, :, 0:PART].reshape(FULL, L).astype(F32)
        centre = rows - jnp.sum(rows, axis=0, keepdims=True) * (1.0 / FULL)
        spread = jnp.sum(centre * centre, axis=0, keepdims=True) * (1.0 / FULL)
        normed = (centre * lax.rsqrt(spread + 1e-06) * wide(gain_b[...])).astype(BF16)
        pre = nn(w1[...], normed) + wide(b1_b[0:FF, :])
        hid[0:FF, c * L : (c + 1) * L] = gelu(pre).astype(BF16)

        if c < CH - 1:
            first_sums(c)

    first_sums(CH - 1)
    member_f = jnp.where(iota((IMG, ROWS), 0) == owner_ref[...], 1.0, 0.0)
    member = member_f.astype(BF16)
    sums = nt(member, hid[...])
    high = sums.astype(BF16)
    low = (sums - high.astype(F32)).astype(BF16)
    lone = gelu(b1_row).astype(BF16)
    mixed = jnp.concatenate([high, low, lone], axis=0)

    def pool_block(i, k):
        there = lax.rem(m + i, MP)
        lines = pl.ds(pl.multiple_of(there * PART, 16), PART)
        got = nt(mixed, w2t[lines, :])
        pool_out[there, 0:16, 0:PART] = (got[0:16] + got[16:32]).astype(BF16)
        pool_out[there, 16:32, 0:PART] = got[32:48].astype(BF16)
        return k

    pool_out[...] = jnp.zeros_like(pool_out)
    lax.fori_loop(0, MP, pool_block, 0)

    def send_pool(i, k):
        there = lax.rem(m + i, MP)
        to_mp(i, pool_out.at[there], pool_in.at[m], pool_send.at[0], pool_recv.at[0]).start()
        return k

    lax.fori_loop(1, MP, send_pool, 0, unroll=True)
    pool_in[m] = pool_out[m]

    for c in range(CH):
        second_sums(c)

    some = pool_in.at[pl.ds(0, MP - 1)]
    to_mp(1, some, some, pool_send.at[0], pool_recv.at[0]).wait_recv()
    pooled = pool_in[0].astype(F32)
    for k in range(1, MP):
        pooled = pooled + pool_in[k].astype(F32)
    b2_wide = jnp.where(iota((1, 256), 1) < PART, small_ref[2:3, 0:256], 0.0)
    counts = jnp.sum(member_f, axis=1, keepdims=True)
    own_sum = nt(member, x_ref[...])
    own_sum = jnp.concatenate([own_sum, jnp.zeros((IMG, 256 - PART), F32)], axis=1)
    image_own = (pooled[0:16] + own_sum) / counts + b2_wide
    empty = (pooled[16:17] + b2_wide).astype(BF16)
    lane = iota((IMG, 256), 1)
    image_note = jnp.where(lane == PART, as_column(caption_high), jnp.where(lane == PART + 1, as_column(caption_low), image_own))
    ibuf[b] = image_note.astype(BF16)

    some = tbuf.at[pl.ds(0, GROUP - 1)]
    to_dp(neighbour, some, some, t_send.at[0], t_recv.at[0]).wait_recv()

    def tell(i, k):
        peer = a * GROUP + lax.rem(b + i, GROUP)
        pl.semaphore_signal(ready_sem, inc=1, device_id=(peer, m), device_id_type=MESH)
        return k

    lax.fori_loop(1, GROUP, tell, 0, unroll=True)

    def send_image(i, k):
        peer = a * GROUP + lax.rem(b + i, GROUP)
        to_dp(peer, ibuf.at[b], ibuf.at[b], i_send.at[0], i_recv.at[0]).start()
        return k

    lax.fori_loop(1, GROUP, send_image, 0, unroll=True)

    for c in range(CH):
        third_sums(c)

    encoded = []
    for c in range(CH):
        total = share(c, m) + arrived_sum(c, 4) + arrived_sum(c, 5) + arrived_sum(c, 6)
        own = x_ref[:, c * L : (c + 1) * L].astype(F32)
        encoded.append(own + total + wide(b2_b[...]))
    encoded = jnp.concatenate(encoded, axis=1)
    by_row = jnp.transpose(jnp.concatenate([encoded, jnp.zeros((256 - PART, ROWS), F32)], axis=0))
    rows_out[:, 0:256] = by_row.astype(BF16)
    rows_out[:, 256:384] = pltpu.roll(by_row[:, 128:256], 16, 1).astype(BF16)
    empty_f = jnp.broadcast_to(empty.astype(F32), (128, 256))
    line = iota((128, 128), 0)
    empty_tail = empty_f[:, 128:256]
    empties = jnp.where(
        line == 0,
        empty_f[:, 0:128],
        jnp.where(line == 1, empty_tail, jnp.where(line == 2, pltpu.roll(empty_tail, 16, 1), 0.0)),
    ).astype(BF16)
    head_row = jnp.bitwise_and(iota((256, 1), 0), 15) < CAP

    def fill(block):
        lines = pl.ds(pl.multiple_of(block * 256, 256), 256)
        main = nn(pick[0, lines, :], rows_out[:, 0:256])
        odd = nn(pick[1, lines, :], rows_out[:, 256:384])
        got = jnp.where(head_row, main[:, 0:128], main[:, 128:256] + odd) + nn(empty_pick[lines, :], empties)
        slot_out[pl.ds(block * 16, 16)] = got.astype(BF16).reshape(16, 16, 128)

    def send_slot(peer):
        to_dp(peer, slot_out.at[peer], slot_in.at[s], slot_send.at[0], slot_recv.at[0]).start()

    def fill_other(i, k):
        block = lax.rem(s // 16 + i, DP // 16)
        fill(block)
        for j in range(16):
            send_slot(block * 16 + j)
        return k

    pl.semaphore_wait(ready_sem, GROUP - 1)
    lax.fori_loop(1, 2, fill_other, 0)

    some = ibuf.at[pl.ds(0, GROUP - 1)]
    to_dp(neighbour, some, some, i_send.at[0], i_recv.at[0]).wait_recv()
    dots = nt(ibuf[...].reshape(SIDE, 256), tbuf[...].reshape(SIDE, 256))
    ones = jnp.where(iota((8, 256), 1) < PART, 1.0, 0.0).astype(BF16)

    def squares(block):
        value = block.astype(F32)
        return nt(ones, (value * value).astype(BF16))

    text_sq = squares(tbuf[...].reshape(SIDE, 256))
    image_sq = squares(ibuf[...].reshape(SIDE, 256))
    pair_out[0:SIDE] = dots.astype(BF16)
    pair_out[SIDE : SIDE + 16] = jnp.concatenate([text_sq, image_sq], axis=0).astype(BF16)

    def send_pair(i, k):
        to_mp(i, pair_out, pair_in.at[m], pair_send.at[0], pair_recv.at[0]).start()
        return k

    lax.fori_loop(1, MP, send_pair, 0, unroll=True)
    pair_in[m] = pair_out[...]


    lax.fori_loop(2, DP // 16, fill_other, 0)
    fill(s // 16)
    for j in range(1, 16):
        send_slot(s // 16 * 16 + lax.rem(s + j, 16))
    slot_in[s] = slot_out[s]

    some = pair_in.at[pl.ds(0, MP - 1)]
    to_mp(1, some, some, pair_send.at[0], pair_recv.at[0]).wait_recv()
    total = pair_in[0].astype(F32)
    for k in range(1, MP):
        total = total + pair_in[k].astype(F32)
    text_scale = lax.rsqrt(total[SIDE : SIDE + 1] + 1e-06)
    image_row = lax.rsqrt(total[SIDE + 8 : SIDE + 9] + 1e-06)
    image_scale = jnp.transpose(jnp.broadcast_to(image_row, (SIDE, SIDE)))
    place = iota((1, SIDE), 1)
    text_name = (jnp.right_shift(place, 4) * (GROUP * IMG) + b * IMG + jnp.bitwise_and(place, 15)).astype(F32)
    noted = ibuf[...].reshape(SIDE, 256)[:, 128:256].astype(F32)
    caption = noted[:, PART - 128 : PART - 127] * 32.0 + noted[:, PART - 127 : PART - 126]
    logits = LOGIT_SCALE * (total[0:SIDE] * image_scale * text_scale) + LOGIT_BIAS
    coef = 1.0 / (1.0 + jnp.exp(-logits)) - jnp.where(caption == text_name, 1.0, 0.0)
    for_images = (coef * text_scale).astype(BF16)
    for_texts = (coef * image_scale).astype(BF16)

    part = LOGIT_SCALE * nn(for_images, tbuf[...].reshape(SIDE, 256))
    grad_out[0] = part.astype(BF16).reshape(GROUP, IMG, 256)
    part = LOGIT_SCALE * tn(for_texts, ibuf[...].reshape(SIDE, 256))
    grad_out[1] = part.astype(BF16).reshape(GROUP, IMG, 256)

    def send_grad(i, k):
        there = lax.rem(b + i, GROUP)
        to_dp(a * GROUP + there, grad_out.at[0, there], grad_in.at[0, b], grad_send.at[0], grad_recv.at[0]).start()
        there = lax.rem(a + i, GROUP)
        to_dp(there * GROUP + b, grad_out.at[1, there], grad_in.at[1, a], grad_send.at[1], grad_recv.at[1]).start()
        return k

    lax.fori_loop(1, GROUP, send_grad, 0, unroll=True)
    grad_in[0, b] = grad_out[0, b]
    grad_in[1, a] = grad_out[1, a]

    some = slot_in.at[pl.ds(0, DP - 1)]
    to_dp(neighbour, some, some, slot_send.at[0], slot_recv.at[0]).wait_recv()
    arrived = jnp.transpose(slot_in[...].reshape(DP * 16, 128))
    head_lane = jnp.bitwise_and(iota((1, DP * 16), 1), 15) < CAP
    nothing = jnp.zeros((32, DP * 16), BF16)
    both = jnp.concatenate([jnp.where(head_lane, arrived, 0), jnp.where(head_lane, nothing, arrived[0:32])], axis=0)
    placed = nn(both, sel[...])
    even_slot = jnp.bitwise_and(iota((1, SLOTS), 1), 1) == 0
    packed_ref[0:128, :] = placed[0:128].astype(BF16)
    packed_ref[128:PART, :] = jnp.where(even_slot, placed[128:PART], placed[PART : PART + 16]).astype(BF16)

    for n, result in enumerate((image_grad_ref, text_grad_ref)):
        some = grad_in.at[n, pl.ds(0, GROUP - 1)]
        to_dp(neighbour, some, some, grad_send.at[n], grad_recv.at[n]).wait_recv()
        sums = grad_in[n, 0].astype(F32)
        for k in range(1, GROUP):
            sums = sums + grad_in[n, k].astype(F32)
        result[...] = sums[:, 0:PART]

    for c in range(CH):
        some = xall.at[c, pl.ds(0, MP - 1), pl.ds(0, XROWS if c == 0 else PART)]
        to_mp(1, some, some, x_send.at[c], x_recv.at[c, 0]).wait_send()
        some = part_out.at[c, pl.ds(0, MP - 1)]
        to_mp(1, some, some, p_send.at[c], p_recv.at[c, 0]).wait_send()
    some = pool_out.at[pl.ds(0, MP - 1)]
    to_mp(1, some, some, pool_send.at[0], pool_recv.at[0]).wait_send()
    some = pair_in.at[pl.ds(0, MP - 1)]
    to_mp(1, some, some, pair_send.at[0], pair_recv.at[0]).wait_send()
    for buf, send, recv in (
        (tbuf, t_send.at[0], t_recv.at[0]),
        (ibuf, i_send.at[0], i_recv.at[0]),
        (grad_out.at[0], grad_send.at[0], grad_recv.at[0]),
        (grad_out.at[1], grad_send.at[1], grad_recv.at[1]),
    ):
        some = buf.at[pl.ds(0, GROUP - 1)]
        to_dp(neighbour, some, some, send, recv).wait_send()
    some = slot_out.at[pl.ds(0, DP - 1)]
    to_dp(neighbour, some, some, slot_send.at[0], slot_recv.at[0]).wait_send()


def hand_over(packed_in, image_in, text_in, packed_out, image_out, text_out):
    packed_out[...] = packed_in[...]
    image_out[...] = image_in[...]
    text_out[...] = text_in[...]


def shards(patches, patch_shard, patch_image, caption_of, text_embed, ln_gain, fc1_weight, fc1_bias, fc2_weight, fc2_bias):
    vmem = pl.BlockSpec(memory_space=pltpu.VMEM)
    hbm = pl.BlockSpec(memory_space=pltpu.HBM)
    dma = pltpu.SemaphoreType.DMA
    shapes = (
        jax.ShapeDtypeStruct((PART, SLOTS), BF16),
        jax.ShapeDtypeStruct((IMG, PART), F32),
        jax.ShapeDtypeStruct((IMG, PART), F32),
    )
    results = pl.pallas_call(
        kernel,
        out_shape=shapes,
        in_specs=[hbm] * 10,
        out_specs=(vmem, vmem, vmem),
        scratch_shapes=[
            pltpu.VMEM((PART, ROWS), BF16),
            pltpu.VMEM((IMG, PART), BF16),
            pltpu.VMEM((1, ROWS), I32),
            pltpu.VMEM((1, ROWS), I32),
            pltpu.VMEM((1, IMG), I32),
            pltpu.VMEM((PART,), BF16),
            pltpu.VMEM((FF,), BF16),
            pltpu.VMEM((PART,), BF16),
            pltpu.VMEM((FF, FULL), BF16),
            pltpu.VMEM((FF, FULL), BF16),
            pltpu.VMEM((8, FFP), F32),
            pltpu.VMEM((FULL, FFP), BF16),
            pltpu.VMEM((CH, MP, XROWS, L), BF16),
            pltpu.VMEM((FULL, 128), F32),
            pltpu.VMEM((FFP, 128), F32),
            pltpu.VMEM((PART, 128), F32),
            pltpu.VMEM((FFP, ROWS), BF16),
            pltpu.VMEM((CH, 7, PART, L), BF16),
            pltpu.VMEM((CH, 7, PART, L), BF16),
            pltpu.VMEM((MP, 32, 256), BF16),
            pltpu.VMEM((MP, 32, 256), BF16),
            pltpu.VMEM((GROUP, IMG, 256), BF16),
            pltpu.VMEM((GROUP, IMG, 256), BF16),
            pltpu.VMEM((SIDE + 16, SIDE), BF16),
            pltpu.VMEM((MP, SIDE + 16, SIDE), BF16),
            pltpu.VMEM((2, GROUP, IMG, 256), BF16),
            pltpu.VMEM((2, GROUP, IMG, 256), BF16),
            pltpu.VMEM((2, DP * 16, ROWS), BF16),
            pltpu.VMEM((DP * 16, 128), BF16),
            pltpu.VMEM((DP * 16, SLOTS), BF16),
            pltpu.VMEM((ROWS, 384), BF16),
            pltpu.VMEM((DP, 16, 128), BF16),
            pltpu.VMEM((DP, 16, 128), BF16),
            dma((10,)),
            dma((CH,)), dma((CH, 7)),
            dma((1,)), dma((1,)),
            dma((CH,)), dma((CH, 7)),
            dma((1,)), dma((1,)),
            dma((1,)), dma((1,)),
            dma((1,)), dma((1,)),
            dma((2,)), dma((2,)),
            dma((1,)), dma((1,)),
            pltpu.SemaphoreType.REGULAR,
        ],
        compiler_params=pltpu.CompilerParams(
            collective_id=0, has_side_effects=True, vmem_limit_bytes=60 * 1024 * 1024
        ),
    )(
        patches.T, text_embed, patch_shard.reshape(1, ROWS), patch_image, caption_of.reshape(1, IMG),
        ln_gain, fc1_bias, fc2_bias, fc1_weight.T, fc2_weight,
    )
    packed, image_grad, text_grad = pl.pallas_call(
        hand_over,
        out_shape=shapes,
        in_specs=[vmem] * 3,
        out_specs=(vmem,) * 3,
        compiler_params=pltpu.CompilerParams(vmem_limit_bytes=60 * 1024 * 1024),
    )(*results)
    return packed.T[None], image_grad, text_grad


def solution(mesh):
    return jax.shard_map(
        shards,
        mesh=mesh,
        in_specs=(
            P("dp", "mp"),
            P("dp", None),
            P("dp", None),
            P("dp"),
            P("dp", "mp"),
            P("mp"),
            P(None, "mp"),
            P("mp"),
            P("mp", None),
            P("mp"),
        ),
        out_specs=(P("dp", None, "mp"), P("dp", "mp"), P("dp", "mp")),
        check_vma=False,
    )
```

```python
import functools

import jax
import jax.numpy as jnp
from jax import lax
from jax.experimental import pallas as pl
from jax.experimental.pallas import tpu as pltpu
from jax.sharding import PartitionSpec as P

LOGIT_SCALE = 10.0
LOGIT_BIAS = -2.0
F32 = jnp.float32
BF16 = jnp.bfloat16
I32 = jnp.int32
MESH = pl.DeviceIdType.MESH

DP, MP = 64, 8
GROUP = 8
ROWS, PART, FULL = 512, 144, 1152
FF, FFP = 538, 640
IMG, CAP = 16, 10
SLOTS = DP * CAP
CH = 2
L = ROWS // CH
SIDE = GROUP * IMG
XROWS = PART + 16


def nn(a, b):
    return jnp.dot(a, b, preferred_element_type=F32)


def nt(a, b):
    return lax.dot_general(a, b, (((1,), (1,)), ((), ())), preferred_element_type=F32)


def tn(a, b):
    return lax.dot_general(a, b, (((0,), (0,)), ((), ())), preferred_element_type=F32)


def iota(shape, axis):
    return lax.broadcasted_iota(I32, shape, axis)


def gelu(h):
    return 0.5 * h * (1.0 + jnp.tanh(0.7978845608028654 * (h + 0.044715 * (h * h * h))))


def wide(column_block):
    return jnp.concatenate([column_block] * (L // 128), axis=1)


def kernel(
    x_hbm, text_hbm, target_hbm, owner_hbm, caption_hbm, gain_hbm, b1_hbm, b2_hbm, w1_hbm, w2_hbm,
    packed_ref, image_grad_ref, text_grad_ref,
    x_ref, text_ref, target_ref, owner_ref, caption_ref, gain_ref, b1_ref, b2_ref, w1, w2,
    small_ref, w2t, xall, gain_b, b1_b, b2_b, hid, own_ref, part_out, part_in,
    pool_out, pool_in, tbuf, ibuf, pair_out, pair_in, grad_out, grad_in,
    pick, empty_pick, sel, rows_out, slot_out, slot_in,
    load_sem, x_send, x_recv, t_send, t_recv, p_send, p_recv,
    pool_send, pool_recv, i_send, i_recv, pair_send, pair_recv,
    grad_send, grad_recv, slot_send, slot_recv, ready_sem,
):
    s = lax.axis_index("dp")
    m = lax.axis_index("mp")
    a = s // GROUP
    b = lax.rem(s, GROUP)
    neighbour = lax.rem(s + 1, DP)

    ring, side = m // 2, lax.rem(m, 2)
    ahead = lax.rem(ring + 1, 4) * 2 + side
    behind = lax.rem(ring + 3, 4) * 2 + side
    far = lax.rem(ring + 2, 4) * 2 + side
    across = ring * 2 + 1 - side
    ahead_across = lax.rem(ring + 1, 4) * 2 + 1 - side
    behind_across = lax.rem(ring + 3, 4) * 2 + 1 - side
    far_across = lax.rem(ring + 2, 4) * 2 + 1 - side

    loads = [
        pltpu.make_async_copy(src, dst, load_sem.at[n])
        for n, (src, dst) in enumerate(
            (
                (x_hbm, x_ref), (gain_hbm, gain_ref), (text_hbm, text_ref), (caption_hbm, caption_ref),
                (target_hbm, target_ref), (owner_hbm, owner_ref), (b1_hbm, b1_ref), (b2_hbm, b2_ref),
                (w1_hbm, w1), (w2_hbm, w2),
            )
        )
    ]
    for load in loads:
        load.start()

    barrier = pltpu.get_barrier_semaphore()

    def greet_mp(i, c):
        pl.semaphore_signal(barrier, inc=1, device_id=(s, lax.rem(m + i, MP)), device_id_type=MESH)
        return c

    def greet_dp(i, c):
        images = a * GROUP + lax.rem(b + i, GROUP)
        texts = lax.rem(a + i, GROUP) * GROUP + b
        pl.semaphore_signal(barrier, inc=1, device_id=(images, m), device_id_type=MESH)
        pl.semaphore_signal(barrier, inc=1, device_id=(texts, m), device_id_type=MESH)
        return c

    lax.fori_loop(1, MP, greet_mp, 0, unroll=True)
    lax.fori_loop(1, GROUP, greet_dp, 0, unroll=True)

    def to_member(member, src, dst, send, recv):
        return pltpu.make_async_remote_copy(
            src_ref=src, dst_ref=dst, send_sem=send, recv_sem=recv,
            device_id=(s, member), device_id_type=MESH,
        )

    def to_mp(i, src, dst, send, recv):
        return to_member(lax.rem(m + i, MP), src, dst, send, recv)

    def to_dp(peer, src, dst, send, recv):
        return pltpu.make_async_remote_copy(
            src_ref=src, dst_ref=dst, send_sem=send, recv_sem=recv,
            device_id=(peer, m), device_id_type=MESH,
        )

    small_ref[...] = jnp.zeros_like(small_ref)
    loads[0].wait()
    loads[1].wait()
    small_ref[1:2, 0:PART] = gain_ref[...].astype(F32).reshape(1, PART)
    for c in range(CH):
        xall[c, m, 0:PART] = x_ref[:, c * L : (c + 1) * L]
    xall[0, m, PART:XROWS] = jnp.broadcast_to(small_ref[1:2, 0:L], (XROWS - PART, L)).astype(BF16)

    pl.semaphore_wait(barrier, MP - 1 + 2 * (GROUP - 1))

    def block(c, member):
        return xall.at[c, member, pl.ds(0, XROWS if c == 0 else PART)]

    def hand_on(c, owner, member, kind):
        to_member(member, block(c, owner), block(c, owner), x_send.at[c], x_recv.at[c, kind]).start()

    def expect(c, kind):
        to_member(across, block(c, m), block(c, m), x_send.at[c], x_recv.at[c, kind]).wait_recv()

    for c in range(CH):
        hand_on(c, m, across, 2)
        hand_on(c, m, ahead, 0)
        hand_on(c, m, behind, 1)

    for load in loads[2:8]:
        load.wait()
    small_ref[0:1, 0:FF] = b1_ref[...].astype(F32).reshape(1, FF)
    small_ref[2:3, 0:PART] = b2_ref[...].astype(F32).reshape(1, PART)
    diagonal = iota((IMG, IMG), 0) == iota((IMG, IMG), 1)
    caption_row = caption_ref[...]
    caption_high = jnp.right_shift(caption_row, 5)
    caption_low = jnp.bitwise_and(caption_row, 31)

    def as_column(row):
        return jnp.sum(jnp.where(diagonal, row.astype(F32), 0.0), axis=1, keepdims=True)

    text_own_f = jnp.concatenate([text_ref[...].astype(F32), jnp.zeros((IMG, 256 - PART), F32)], axis=1)
    tbuf[a] = text_own_f.astype(BF16)

    def send_text(i, k):
        peer = lax.rem(a + i, GROUP) * GROUP + b
        to_dp(peer, tbuf.at[a], tbuf.at[a], t_send.at[0], t_recv.at[0]).start()
        return k


    for c in range(CH):
        if c == 0:
            expect(c, 0)
            hand_on(c, behind, ahead, 5)
        else:
            expect(c, 1)
            hand_on(c, ahead, behind, 5)
        expect(c, 2)
        hand_on(c, across, ahead, 3)
        hand_on(c, across, behind, 4)

    lax.fori_loop(1, GROUP, send_text, 0, unroll=True)

    targets = target_ref[...]
    named = iota((DP, ROWS), 0) == targets
    named_b = jnp.where(named, 1.0, 0.0).astype(BF16)
    earlier = jnp.where(iota((ROWS, ROWS), 0) < iota((ROWS, ROWS), 1), 1.0, 0.0).astype(BF16)
    before = nn(named_b, earlier)
    rank = jnp.sum(jnp.where(named, before, 0.0), axis=0, keepdims=True).astype(I32)
    code = targets * 16 + rank

    first_row = jnp.where(iota((16, 128), 0) == 0, 1.0, 0.0).astype(BF16)
    b1_row = jnp.broadcast_to(small_ref[0:1, :], (16, FFP))
    b1_b[...] = tn(b1_row.astype(BF16), first_row)
    b2_row = jnp.broadcast_to(small_ref[2:3, 0:256], (16, 256)).astype(BF16)
    b2_b[...] = tn(b2_row, first_row)[0:PART]
    hid[...] = jnp.zeros_like(hid)
    for c in range(CH):
        expect(c, 5)
        hand_on(c, far, across, 6)

    def build_pick(b, k):
        row = iota((128, 1), 0) + b * 128
        slot = jnp.bitwise_and(row, 15)
        base = row - slot
        is_head = slot < CAP
        is_tail = jnp.logical_and(slot >= CAP, slot < CAP + CAP // 2)
        even = base + 2 * (slot - CAP)
        lines = pl.ds(pl.multiple_of(b * 128, 128), 128)
        lane = iota((128, 128), 1)
        main = jnp.where(jnp.where(is_head, row, jnp.where(is_tail, even, -1)) == code, 1.0, 0.0)
        odd = jnp.where(jnp.where(is_tail, even + 1, -1) == code, 1.0, 0.0)
        pick[0, lines, :] = main.astype(BF16)
        pick[1, lines, :] = odd.astype(BF16)
        lack = 1.0 - jnp.sum(main, axis=1, keepdims=True)
        lack_odd = 1.0 - jnp.sum(odd, axis=1, keepdims=True)
        lacks = jnp.where(
            lane == 0,
            jnp.where(is_head, lack, 0.0),
            jnp.where(lane == 1, jnp.where(is_tail, lack, 0.0), jnp.where(lane == 2, jnp.where(is_tail, lack_odd, 0.0), 0.0)),
        )
        empty_pick[lines, :] = lacks.astype(BF16)
        column = iota((128, SLOTS), 1)
        first = jnp.right_shift(row, 4) * CAP
        even_at = first + 2 * (slot - CAP)
        main_at = jnp.where(is_head, first + slot, jnp.where(is_tail, even_at, -1))
        odd_at = jnp.where(is_tail, even_at + 1, -1)
        here = jnp.logical_or(main_at == column, odd_at == column)
        sel[lines, :] = jnp.where(here, 1.0, 0.0).astype(BF16)
        return k

    lax.fori_loop(0, DP * 16 // 128, build_pick, 0)

    loads[8].wait()
    loads[9].wait()
    w2t[:, 0:512] = jnp.transpose(w2[0:512, :])
    tail_rows = jnp.concatenate([w2[512:FF, :].astype(F32), jnp.zeros((FFP - FF, FULL), F32)], axis=0)
    w2t[:, 512:FFP] = jnp.transpose(tail_rows).astype(BF16)

    def share(c, member):
        lines = pl.ds(pl.multiple_of(member * PART, 16), PART)
        return nn(w2t[lines, :], hid[:, c * L : (c + 1) * L])

    def pass_on(c, value, member, kind):
        part_out[c, kind] = value.astype(BF16)
        to_member(member, part_out.at[c, kind], part_in.at[c, kind], p_send.at[c], p_recv.at[c, kind]).start()

    def arrived_sum(c, kind):
        to_member(across, part_in.at[c, kind], part_in.at[c, kind], p_send.at[c], p_recv.at[c, kind]).wait_recv()
        return part_in[c, kind].astype(F32)

    def first_sums(c):
        pass_on(c, share(c, far_across), across, 0)
        pass_on(c, share(c, ahead_across), ahead, 1)
        pass_on(c, share(c, behind_across), behind, 2)
        if c == 0:
            pass_on(c, share(c, behind), behind, 5)
        else:
            pass_on(c, share(c, ahead), ahead, 4)

    def second_sums(c):
        pass_on(c, share(c, far) + arrived_sum(c, 0), ahead if c == 0 else behind, 3)
        pass_on(c, share(c, across) + arrived_sum(c, 1) + arrived_sum(c, 2), across, 6)

    def third_sums(c):
        if c == 0:
            pass_on(c, share(c, ahead) + arrived_sum(c, 3), ahead, 4)
        else:
            pass_on(c, share(c, behind) + arrived_sum(c, 3), behind, 5)

    for c in range(CH):
        for kind in (1 if c == 0 else 0, 3, 4, 6):
            expect(c, kind)
        if c == 0:
            for k in range(MP):
                gain_b[k * PART : (k + 1) * PART, :] = tn(xall[0, k, PART:XROWS], first_row)[0:PART]

        rows = xall[c, :, 0:PART].reshape(FULL, L).astype(F32)
        centre = rows - jnp.sum(rows, axis=0, keepdims=True) * (1.0 / FULL)
        spread = jnp.sum(centre * centre, axis=0, keepdims=True) * (1.0 / FULL)
        normed = (centre * lax.rsqrt(spread + 1e-06) * wide(gain_b[...])).astype(BF16)
        pre = nn(w1[...], normed) + wide(b1_b[0:FF, :])
        hid[0:FF, c * L : (c + 1) * L] = gelu(pre).astype(BF16)

        if c < CH - 1:
            first_sums(c)

    first_sums(CH - 1)
    member_f = jnp.where(iota((IMG, ROWS), 0) == owner_ref[...], 1.0, 0.0)
    member = member_f.astype(BF16)
    sums = nt(member, hid[...])
    high = sums.astype(BF16)
    low = (sums - high.astype(F32)).astype(BF16)
    lone = gelu(b1_row).astype(BF16)
    mixed = jnp.concatenate([high, low, lone], axis=0)

    def pool_block(i, k):
        there = lax.rem(m + i, MP)
        lines = pl.ds(pl.multiple_of(there * PART, 16), PART)
        got = nt(mixed, w2t[lines, :])
        pool_out[there, 0:16, 0:PART] = (got[0:16] + got[16:32]).astype(BF16)
        pool_out[there, 16:32, 0:PART] = got[32:48].astype(BF16)
        return k

    pool_out[...] = jnp.zeros_like(pool_out)
    lax.fori_loop(0, MP, pool_block, 0)

    def send_pool(i, k):
        there = lax.rem(m + i, MP)
        to_mp(i, pool_out.at[there], pool_in.at[m], pool_send.at[0], pool_recv.at[0]).start()
        return k

    lax.fori_loop(1, MP, send_pool, 0, unroll=True)
    pool_in[m] = pool_out[m]

    for c in range(CH):
        second_sums(c)

    some = tbuf.at[pl.ds(0, GROUP - 1)]
    to_dp(neighbour, some, some, t_send.at[0], t_recv.at[0]).wait_recv()

    def tell(i, k):
        peer = a * GROUP + lax.rem(b + i, GROUP)
        pl.semaphore_signal(ready_sem, inc=1, device_id=(peer, m), device_id_type=MESH)
        return k

    lax.fori_loop(1, GROUP, tell, 0, unroll=True)

    counts = jnp.sum(member_f, axis=1, keepdims=True)
    own_sum = nt(member, x_ref[...])
    own_ref[...] = jnp.concatenate([own_sum, jnp.zeros((IMG, 256 - PART), F32)], axis=1)

    some = pool_in.at[pl.ds(0, MP - 1)]
    to_mp(1, some, some, pool_send.at[0], pool_recv.at[0]).wait_recv()
    pooled = pool_in[0].astype(F32)
    for k in range(1, MP):
        pooled = pooled + pool_in[k].astype(F32)
    b2_wide = jnp.where(iota((1, 256), 1) < PART, small_ref[2:3, 0:256], 0.0)
    image_own = (pooled[0:16] + own_ref[...]) / counts + b2_wide
    empty = (pooled[16:17] + b2_wide).astype(BF16)
    lane = iota((IMG, 256), 1)
    image_note = jnp.where(lane == PART, as_column(caption_high), jnp.where(lane == PART + 1, as_column(caption_low), image_own))
    ibuf[b] = image_note.astype(BF16)

    def send_image(i, k):
        peer = a * GROUP + lax.rem(b + i, GROUP)
        to_dp(peer, ibuf.at[b], ibuf.at[b], i_send.at[0], i_recv.at[0]).start()
        return k

    lax.fori_loop(1, GROUP, send_image, 0, unroll=True)

    for c in range(CH):
        third_sums(c)

    encoded = []
    for c in range(CH):
        total = share(c, m) + arrived_sum(c, 4) + arrived_sum(c, 5) + arrived_sum(c, 6)
        own = x_ref[:, c * L : (c + 1) * L].astype(F32)
        encoded.append(own + total + wide(b2_b[...]))
    encoded = jnp.concatenate(encoded, axis=1)
    by_row = jnp.transpose(jnp.concatenate([encoded, jnp.zeros((256 - PART, ROWS), F32)], axis=0))
    rows_out[:, 0:256] = by_row.astype(BF16)
    rows_out[:, 256:384] = pltpu.roll(by_row[:, 128:256], 16, 1).astype(BF16)
    empty_f = jnp.broadcast_to(empty.astype(F32), (128, 256))
    line = iota((128, 128), 0)
    empty_tail = empty_f[:, 128:256]
    empties = jnp.where(
        line == 0,
        empty_f[:, 0:128],
        jnp.where(line == 1, empty_tail, jnp.where(line == 2, pltpu.roll(empty_tail, 16, 1), 0.0)),
    ).astype(BF16)
    head_row = jnp.bitwise_and(iota((256, 1), 0), 15) < CAP

    def fill(block):
        lines = pl.ds(pl.multiple_of(block * 256, 256), 256)
        main = nn(pick[0, lines, :], rows_out[:, 0:256])
        odd = nn(pick[1, lines, :], rows_out[:, 256:384])
        got = jnp.where(head_row, main[:, 0:128], main[:, 128:256] + odd) + nn(empty_pick[lines, :], empties)
        slot_out[pl.ds(block * 16, 16)] = got.astype(BF16).reshape(16, 16, 128)

    def send_slot(peer):
        to_dp(peer, slot_out.at[peer], slot_in.at[s], slot_send.at[0], slot_recv.at[0]).start()

    def fill_other(i, k):
        block = lax.rem(s // 16 + i, DP // 16)
        fill(block)
        for j in range(16):
            send_slot(block * 16 + j)
        return k

    pl.semaphore_wait(ready_sem, GROUP - 1)
    lax.fori_loop(1, 2, fill_other, 0)

    some = ibuf.at[pl.ds(0, GROUP - 1)]
    to_dp(neighbour, some, some, i_send.at[0], i_recv.at[0]).wait_recv()
    dots = nt(ibuf[...].reshape(SIDE, 256), tbuf[...].reshape(SIDE, 256))
    ones = jnp.where(iota((8, 256), 1) < PART, 1.0, 0.0).astype(BF16)

    def squares(block):
        value = block.astype(F32)
        return nt(ones, (value * value).astype(BF16))

    text_sq = squares(tbuf[...].reshape(SIDE, 256))
    image_sq = squares(ibuf[...].reshape(SIDE, 256))
    pair_out[0:SIDE] = dots.astype(BF16)
    pair_out[SIDE : SIDE + 16] = jnp.concatenate([text_sq, image_sq], axis=0).astype(BF16)

    def send_pair(i, k):
        to_mp(i, pair_out, pair_in.at[m], pair_send.at[0], pair_recv.at[0]).start()
        return k

    lax.fori_loop(1, MP, send_pair, 0, unroll=True)
    pair_in[m] = pair_out[...]


    lax.fori_loop(2, DP // 16, fill_other, 0)
    fill(s // 16)
    for j in range(1, 16):
        send_slot(s // 16 * 16 + lax.rem(s + j, 16))
    slot_in[s] = slot_out[s]

    some = pair_in.at[pl.ds(0, MP - 1)]
    to_mp(1, some, some, pair_send.at[0], pair_recv.at[0]).wait_recv()
    total = pair_in[0].astype(F32)
    for k in range(1, MP):
        total = total + pair_in[k].astype(F32)
    text_scale = lax.rsqrt(total[SIDE : SIDE + 1] + 1e-06)
    image_row = lax.rsqrt(total[SIDE + 8 : SIDE + 9] + 1e-06)
    image_scale = jnp.transpose(jnp.broadcast_to(image_row, (SIDE, SIDE)))
    place = iota((1, SIDE), 1)
    text_name = (jnp.right_shift(place, 4) * (GROUP * IMG) + b * IMG + jnp.bitwise_and(place, 15)).astype(F32)
    noted = ibuf[...].reshape(SIDE, 256)[:, 128:256].astype(F32)
    caption = noted[:, PART - 128 : PART - 127] * 32.0 + noted[:, PART - 127 : PART - 126]
    logits = LOGIT_SCALE * (total[0:SIDE] * image_scale * text_scale) + LOGIT_BIAS
    coef = 1.0 / (1.0 + jnp.exp(-logits)) - jnp.where(caption == text_name, 1.0, 0.0)
    for_images = (coef * text_scale).astype(BF16)
    for_texts = (coef * image_scale).astype(BF16)

    part = LOGIT_SCALE * nn(for_images, tbuf[...].reshape(SIDE, 256))
    grad_out[0] = part.astype(BF16).reshape(GROUP, IMG, 256)
    part = LOGIT_SCALE * tn(for_texts, ibuf[...].reshape(SIDE, 256))
    grad_out[1] = part.astype(BF16).reshape(GROUP, IMG, 256)

    def send_grad(i, k):
        there = lax.rem(b + i, GROUP)
        to_dp(a * GROUP + there, grad_out.at[0, there], grad_in.at[0, b], grad_send.at[0], grad_recv.at[0]).start()
        there = lax.rem(a + i, GROUP)
        to_dp(there * GROUP + b, grad_out.at[1, there], grad_in.at[1, a], grad_send.at[1], grad_recv.at[1]).start()
        return k

    lax.fori_loop(1, GROUP, send_grad, 0, unroll=True)
    grad_in[0, b] = grad_out[0, b]
    grad_in[1, a] = grad_out[1, a]

    some = slot_in.at[pl.ds(0, DP - 1)]
    to_dp(neighbour, some, some, slot_send.at[0], slot_recv.at[0]).wait_recv()
    arrived = jnp.transpose(slot_in[...].reshape(DP * 16, 128))
    head_lane = jnp.bitwise_and(iota((1, DP * 16), 1), 15) < CAP
    nothing = jnp.zeros((32, DP * 16), BF16)
    both = jnp.concatenate([jnp.where(head_lane, arrived, 0), jnp.where(head_lane, nothing, arrived[0:32])], axis=0)
    placed = nn(both, sel[...])
    even_slot = jnp.bitwise_and(iota((1, SLOTS), 1), 1) == 0
    packed_ref[0:128, :] = placed[0:128].astype(BF16)
    packed_ref[128:PART, :] = jnp.where(even_slot, placed[128:PART], placed[PART : PART + 16]).astype(BF16)

    for n, result in enumerate((image_grad_ref, text_grad_ref)):
        some = grad_in.at[n, pl.ds(0, GROUP - 1)]
        to_dp(neighbour, some, some, grad_send.at[n], grad_recv.at[n]).wait_recv()
        sums = grad_in[n, 0].astype(F32)
        for k in range(1, GROUP):
            sums = sums + grad_in[n, k].astype(F32)
        result[...] = sums[:, 0:PART]

    for c in range(CH):
        some = xall.at[c, pl.ds(0, MP - 1), pl.ds(0, XROWS if c == 0 else PART)]
        to_mp(1, some, some, x_send.at[c], x_recv.at[c, 0]).wait_send()
        some = part_out.at[c, pl.ds(0, MP - 1)]
        to_mp(1, some, some, p_send.at[c], p_recv.at[c, 0]).wait_send()
    some = pool_out.at[pl.ds(0, MP - 1)]
    to_mp(1, some, some, pool_send.at[0], pool_recv.at[0]).wait_send()
    some = pair_in.at[pl.ds(0, MP - 1)]
    to_mp(1, some, some, pair_send.at[0], pair_recv.at[0]).wait_send()
    for buf, send, recv in (
        (tbuf, t_send.at[0], t_recv.at[0]),
        (ibuf, i_send.at[0], i_recv.at[0]),
        (grad_out.at[0], grad_send.at[0], grad_recv.at[0]),
        (grad_out.at[1], grad_send.at[1], grad_recv.at[1]),
    ):
        some = buf.at[pl.ds(0, GROUP - 1)]
        to_dp(neighbour, some, some, send, recv).wait_send()
    some = slot_out.at[pl.ds(0, DP - 1)]
    to_dp(neighbour, some, some, slot_send.at[0], slot_recv.at[0]).wait_send()


def hand_over(packed_in, image_in, text_in, packed_out, image_out, text_out):
    packed_out[...] = packed_in[...]
    image_out[...] = image_in[...]
    text_out[...] = text_in[...]


def shards(patches, patch_shard, patch_image, caption_of, text_embed, ln_gain, fc1_weight, fc1_bias, fc2_weight, fc2_bias):
    vmem = pl.BlockSpec(memory_space=pltpu.VMEM)
    hbm = pl.BlockSpec(memory_space=pltpu.HBM)
    dma = pltpu.SemaphoreType.DMA
    shapes = (
        jax.ShapeDtypeStruct((PART, SLOTS), BF16),
        jax.ShapeDtypeStruct((IMG, PART), F32),
        jax.ShapeDtypeStruct((IMG, PART), F32),
    )
    results = pl.pallas_call(
        kernel,
        out_shape=shapes,
        in_specs=[hbm] * 10,
        out_specs=(vmem, vmem, vmem),
        scratch_shapes=[
            pltpu.VMEM((PART, ROWS), BF16),
            pltpu.VMEM((IMG, PART), BF16),
            pltpu.VMEM((1, ROWS), I32),
            pltpu.VMEM((1, ROWS), I32),
            pltpu.VMEM((1, IMG), I32),
            pltpu.VMEM((PART,), BF16),
            pltpu.VMEM((FF,), BF16),
            pltpu.VMEM((PART,), BF16),
            pltpu.VMEM((FF, FULL), BF16),
            pltpu.VMEM((FF, FULL), BF16),
            pltpu.VMEM((8, FFP), F32),
            pltpu.VMEM((FULL, FFP), BF16),
            pltpu.VMEM((CH, MP, XROWS, L), BF16),
            pltpu.VMEM((FULL, 128), F32),
            pltpu.VMEM((FFP, 128), F32),
            pltpu.VMEM((PART, 128), F32),
            pltpu.VMEM((FFP, ROWS), BF16),
            pltpu.VMEM((IMG, 256), F32),
            pltpu.VMEM((CH, 7, PART, L), BF16),
            pltpu.VMEM((CH, 7, PART, L), BF16),
            pltpu.VMEM((MP, 32, 256), BF16),
            pltpu.VMEM((MP, 32, 256), BF16),
            pltpu.VMEM((GROUP, IMG, 256), BF16),
            pltpu.VMEM((GROUP, IMG, 256), BF16),
            pltpu.VMEM((SIDE + 16, SIDE), BF16),
            pltpu.VMEM((MP, SIDE + 16, SIDE), BF16),
            pltpu.VMEM((2, GROUP, IMG, 256), BF16),
            pltpu.VMEM((2, GROUP, IMG, 256), BF16),
            pltpu.VMEM((2, DP * 16, ROWS), BF16),
            pltpu.VMEM((DP * 16, 128), BF16),
            pltpu.VMEM((DP * 16, SLOTS), BF16),
            pltpu.VMEM((ROWS, 384), BF16),
            pltpu.VMEM((DP, 16, 128), BF16),
            pltpu.VMEM((DP, 16, 128), BF16),
            dma((10,)),
            dma((CH,)), dma((CH, 7)),
            dma((1,)), dma((1,)),
            dma((CH,)), dma((CH, 7)),
            dma((1,)), dma((1,)),
            dma((1,)), dma((1,)),
            dma((1,)), dma((1,)),
            dma((2,)), dma((2,)),
            dma((1,)), dma((1,)),
            pltpu.SemaphoreType.REGULAR,
        ],
        compiler_params=pltpu.CompilerParams(
            collective_id=0, has_side_effects=True, vmem_limit_bytes=60 * 1024 * 1024
        ),
    )(
        patches.T, text_embed, patch_shard.reshape(1, ROWS), patch_image, caption_of.reshape(1, IMG),
        ln_gain, fc1_bias, fc2_bias, fc1_weight.T, fc2_weight,
    )
    packed, image_grad, text_grad = pl.pallas_call(
        hand_over,
        out_shape=shapes,
        in_specs=[vmem] * 3,
        out_specs=(vmem,) * 3,
        compiler_params=pltpu.CompilerParams(vmem_limit_bytes=60 * 1024 * 1024),
    )(*results)
    return packed.T[None], image_grad, text_grad


def solution(mesh):
    return jax.shard_map(
        shards,
        mesh=mesh,
        in_specs=(
            P("dp", "mp"),
            P("dp", None),
            P("dp", None),
            P("dp"),
            P("dp", "mp"),
            P("mp"),
            P(None, "mp"),
            P("mp"),
            P("mp", None),
            P("mp"),
        ),
        out_specs=(P("dp", None, "mp"), P("dp", "mp"), P("dp", "mp")),
        check_vma=False,
    )
```
